256 devices in a mesh: seq: 32 (over x, z_hi, y), uly: 8 (over z_lo, core).
Axes of the slice: x: 4, y: 4, z: 8 (z_hi: 2, z_lo: 4; z = z_hi * 4 + z_lo), core: 2. Of those that a mesh axis runs over, the one named last changes fastest.
Arguments:
- queries: bfloat16 [32768, 3072], P(('seq', 'uly')), may hold values from -6 to 6
- keys: bfloat16 [32768, 3072], P(('seq', 'uly')), may hold values from -6 to 6
- values: bfloat16 [32768, 3072], P(('seq', 'uly')), may hold values from -6 to 6
- cotangent: bfloat16 [32768, 3072], P(('seq', 'uly')), may hold values from -6 to 6
- doc_ids: int32 [32768], replicated, may hold values from 0 to 63, never falling along the last dimension, each value on 1 to 1024 neighbouring positions
Outputs:
- attended: bfloat16 [32768, 3072], P(('seq', 'uly'))
- grad_queries: bfloat16 [32768, 3072], P(('seq', 'uly'))
- grad_keys: bfloat16 [32768, 3072], P(('seq', 'uly'))
- grad_values: bfloat16 [32768, 3072], P(('seq', 'uly'))
The draws below stay inside these ranges and needn't reach their ends.
Inputs may be any that keep to these rules, and one draw needn't show every extreme that they name: `doc_ids`: no document has more than 1024 tokens; some document has exactly 1024.
All inputs are finite; a program needn't handle non-finite values.
Results may differ from the reference program's by a relative error of at most 0.034.
Values may be sent and summed in bfloat16 or wider, within the bound.
No kernel may reach another device: no remote copies, remote signals or barrier semaphores. Data moves between devices by JAX's collectives and lax.ppermute only.
A program may use at most 128 MiB of HBM per device.

```python
import math
import jax
import jax.numpy as jnp
import numpy as np
from jax import lax

HEADS = 32
HEAD_DIM = 96
BLOCK = 1024
TOKENS = 32768
DOCS = 64


def draw_queries(key, part):
    key = jax.random.fold_in(key, 11)
    drawn_draw = jnp.clip(jax.random.normal(key, (TOKENS, HEADS * HEAD_DIM), jnp.float32), -6.0, 6.0)
    return drawn_draw.astype(jnp.bfloat16)


def draw_keys(key, part):
    key = jax.random.fold_in(key, 23)
    drawn_key = jax.random.fold_in(key, 0)
    drawn_draw = jnp.clip(jax.random.normal(drawn_key, (TOKENS, HEADS * HEAD_DIM), jnp.float32), -6.0, 6.0)
    return drawn_draw.astype(jnp.bfloat16)


def block_scale(own_key, shape, cuts, smallest, top_value):
    loudness = 1.0
    for dim, blocks in cuts:
        heights = jax.random.uniform(jax.random.fold_in(jax.random.fold_in(own_key, 6), dim), (blocks,), jnp.float32, smallest / len(cuts), top_value / len(cuts))
        loudness = loudness * jnp.repeat(jnp.exp(heights), shape[dim] // blocks).reshape((-1,) + (1,) * (len(shape) - 1 - dim))
    return loudness


def profile(amount, total, bound, slope):
    weights = [(1 << 20) // math.isqrt(standing ** slope) + 1 for standing in range(2, amount + 1)]
    spare, counts = total - bound - (amount - 1), [1] * (amount - 1)
    while spare > 0:
        movable = [i for i in range(amount - 1) if counts[i] < bound]
        pool, budget = sum([weights[i] for i in movable]), spare
        for i in movable:
            addition = min(bound - counts[i], max(1, budget * weights[i] // pool), spare)
            counts[i] = counts[i] + addition
            spare = spare - addition
    return np.array([bound] + counts)


def uneven(own_key, amount, total, reach, lean):
    if amount == 2:
        one = jax.random.randint(own_key, (), max(1, total - reach), min(reach, total - 1) + 1)
        return jnp.stack([one, total - one])
    sizes = jnp.asarray(profile(amount, total, reach, lean), jnp.int32)
    twos = (amount - 1) // 2
    source_of, sink = sizes[1:1 + 2 * twos:2], sizes[2:2 + 2 * twos:2]
    room = jnp.minimum(source_of - 1, reach - sink)
    shifted = jax.random.randint(jax.random.fold_in(own_key, 1), (twos,), 0, 1 << 20) % (room + 1)
    sizes = sizes.at[1:1 + 2 * twos:2].set(source_of - shifted).at[2:2 + 2 * twos:2].set(sink + shifted)
    return sizes[jax.random.permutation(jax.random.fold_in(own_key, 2), amount)]


def bell_draw(key, dims, deviation, bound, cuts=(), kind=jnp.bfloat16):
    gain = block_scale(key, dims, cuts, -0.22, 0.18) if cuts else 1.0
    entries = jax.random.normal(key, dims, jnp.float32) * deviation * gain
    return jnp.minimum(jnp.maximum(entries, -bound), bound).astype(kind)


def setup_inputs(seed: int = 0) -> dict:
    splits = jax.random.split(jax.random.key(seed), 6)
    return {
        "queries": draw_queries(jax.random.fold_in(splits[5], 71), 0),
        "keys": draw_keys(jax.random.fold_in(splits[5], 71), 0),
        "values": bell_draw(splits[2], (TOKENS, HEADS * HEAD_DIM), 1.0, 6.0, ((0, 256),)),
        "cotangent": bell_draw(splits[3], (TOKENS, HEADS * HEAD_DIM), 1.0, 6.0, ((0, 256),)),
        "doc_ids": jnp.searchsorted(jnp.cumsum(uneven(splits[4], DOCS, TOKENS, BLOCK, 2)), jnp.arange(TOKENS), side="right").astype(jnp.int32),
    }


NEG = -1e+30

def reference(queries, keys, values, cotangent, doc_ids):
    num_blocks = TOKENS // BLOCK
    scaling = 1.0 / math.sqrt(HEAD_DIM)

    def blocked(array):
        return array.reshape(num_blocks, BLOCK, HEADS, HEAD_DIM)
    query_b, key_b, value_b, grad_b = (blocked(queries), blocked(keys), blocked(values), blocked(cotangent))
    doc_b = doc_ids.reshape(num_blocks, BLOCK)
    zero_block = jnp.zeros((1, BLOCK, HEADS, HEAD_DIM), keys.dtype)
    key_prev = jnp.concatenate([zero_block, key_b[:-1]], 0)
    value_prev = jnp.concatenate([zero_block, value_b[:-1]], 0)
    doc_prev = jnp.concatenate([jnp.full((1, BLOCK), -1, jnp.int32), doc_b[:-1].astype(jnp.int32)], 0)

    def per_block(pieces):
        query_t, key_p, key_o, value_p, value_o, grad_t, docs_p, docs_o = pieces
        key_cat = jnp.concatenate([key_p, key_o], 0).astype(jnp.float32)
        value_cat = jnp.concatenate([value_p, value_o], 0).astype(jnp.float32)
        docs_cat = jnp.concatenate([docs_p, docs_o], 0)
        row_pos = jnp.arange(BLOCK)
        col_pos = jnp.arange(2 * BLOCK)
        allowed = (docs_o[:, None] == docs_cat[None, :]) & (col_pos[None, :] <= row_pos[:, None] + BLOCK)
        query_f = query_t.astype(jnp.float32)
        grad_f = grad_t.astype(jnp.float32)
        scores = jnp.einsum('qhd,khd->hqk', query_f, key_cat) * scaling
        scores = jnp.where(allowed[None], scores, NEG)
        row_max = lax.optimization_barrier(jnp.max(scores, axis=2))
        log_total = row_max + jnp.log(lax.optimization_barrier(jnp.sum(jnp.exp(scores - row_max[:, :, None]), axis=2)))
        weights = jnp.where(allowed[None], jnp.exp(scores - log_total[:, :, None]), 0.0)
        weights_b = weights.astype(jnp.bfloat16)
        weights_r = weights_b.astype(jnp.float32)
        attended_b = jnp.einsum('hqk,khd->qhd', weights_r, value_cat).astype(jnp.bfloat16)
        row_delta = lax.optimization_barrier(jnp.sum(attended_b.astype(jnp.float32) * grad_f, axis=2))
        grad_prob = jnp.einsum('qhd,khd->hqk', grad_f, value_cat)
        dscore = (weights_r * (grad_prob - row_delta.T[:, :, None])).astype(jnp.bfloat16).astype(jnp.float32)
        grad_q = (jnp.einsum('hqk,khd->qhd', dscore, key_cat) * scaling).astype(jnp.bfloat16)
        grad_k = jnp.einsum('hqk,qhd->khd', dscore, query_f)
        grad_v = jnp.einsum('hqk,qhd->khd', weights_r, grad_f)
        return (attended_b, grad_q, grad_k, grad_v)
    attended, grad_q, key_parts, value_parts = lax.map(per_block, (query_b, key_prev, key_b, value_prev, value_b, grad_b, doc_prev, doc_b.astype(jnp.int32)))
    zero_part = jnp.zeros((1, BLOCK, HEADS, HEAD_DIM), jnp.float32)
    key_next = jnp.concatenate([key_parts[1:, :BLOCK], zero_part], 0)
    value_next = jnp.concatenate([value_parts[1:, :BLOCK], zero_part], 0)
    grad_k = ((key_parts[:, BLOCK:] + key_next) * scaling).astype(jnp.bfloat16)
    grad_v = (value_parts[:, BLOCK:] + value_next).astype(jnp.bfloat16)
    width = HEADS * HEAD_DIM
    return (attended.reshape(TOKENS, width), grad_q.reshape(TOKENS, width), grad_k.reshape(TOKENS, width), grad_v.reshape(TOKENS, width))
```

```python
import functools
import math

import jax
import jax.numpy as jnp
from jax import lax
from jax.experimental import pallas as pl
from jax.experimental.pallas import tpu as pltpu
from jax.sharding import Mesh
from jax.sharding import PartitionSpec as P

HEAD_DIM = 96
HEADS = 32
CHUNK = 128
CHUNKS = 32
HALO = 8
DOCS = 64
GROUP = CHUNK * CHUNKS
AHEAD = CHUNK * HALO
WINDOW = GROUP + AHEAD
TILE = 256
TILES = GROUP // TILE
AHEAD_TILES = AHEAD // TILE
REACH = AHEAD_TILES + 1
NEG = -1e30
SCALE = 1.0 / math.sqrt(HEAD_DIM)
LOG2E = 1.4426950408889634
VMEM_LIMIT = 56 * 1024 * 1024

AXES = ("x", "zh", "y", "zl", "c")
GROUP_AXES = ("y", "zl", "c")
F32 = jnp.float32
BF16 = jnp.bfloat16


def vmem():
    return pl.BlockSpec(memory_space=pltpu.VMEM)


def smem():
    return pl.BlockSpec(memory_space=pltpu.SMEM)


def pack_kernel(mirror_ref, *refs):
    sources, out_ref = refs[:-1], refs[-1]
    mirrored = mirror_ref[0]
    for n, ref in enumerate(sources):
        turned = ref[...].T
        for zl in range(4):
            slot = 2 * jnp.where(mirrored == 1, 3 - zl, zl)
            piece = turned[zl * 192 : (zl + 1) * 192]
            out_ref[pl.ds(slot, 2), n] = piece.reshape(2, HEAD_DIM, CHUNK)


def pack(mirror, *arrays):
    count = len(arrays)
    return pl.pallas_call(
        pack_kernel,
        grid=(4,),
        in_specs=[smem()] + [pl.BlockSpec((CHUNK, 768), lambda y: (0, y))] * count,
        out_specs=pl.BlockSpec((8, count, HEAD_DIM, CHUNK), lambda y: (y, 0, 0, 0)),
        out_shape=jax.ShapeDtypeStruct((HEADS, count, HEAD_DIM, CHUNK), BF16),
        compiler_params=pltpu.CompilerParams(vmem_limit_bytes=VMEM_LIMIT),
        name="pack",
    )(mirror, *arrays)


def unpack_kernel(mirror_ref, in_ref, *out_refs):
    mirrored = mirror_ref[0]
    for n, out_ref in enumerate(out_refs):
        pieces = []
        for zl in range(4):
            slot = 2 * jnp.where(mirrored == 1, 3 - zl, zl)
            pieces.append(in_ref[pl.ds(slot, 2), n].reshape(192, CHUNK))
        out_ref[...] = jnp.concatenate(pieces, 0).T


def unpack(mirror, array):
    count = array.shape[1]
    return pl.pallas_call(
        unpack_kernel,
        grid=(4,),
        in_specs=[
            smem(),
            pl.BlockSpec((8, count, HEAD_DIM, CHUNK), lambda y: (y, 0, 0, 0)),
        ],
        out_specs=[pl.BlockSpec((CHUNK, 768), lambda y: (0, y))] * count,
        out_shape=[jax.ShapeDtypeStruct((CHUNK, HEADS * HEAD_DIM), BF16)] * count,
        compiler_params=pltpu.CompilerParams(vmem_limit_bytes=VMEM_LIMIT),
        name="unpack",
    )(mirror, array)


def tile_of(ref, n, i):
    return jnp.concatenate([ref[2 * i, n], ref[2 * i + 1, n]], 1)


def nn(a, b):
    return lax.dot_general(a, b, (((1,), (0,)), ((), ())), preferred_element_type=F32)


def nt(a, b):
    return lax.dot_general(a, b, (((1,), (1,)), ((), ())), preferred_element_type=F32)


def fill(halo_ref, own_ref, n, flat, turned):
    for chunk in range(HALO + CHUNKS):
        piece = halo_ref[chunk, n] if chunk < HALO else own_ref[chunk - HALO, n]
        if turned is not None:
            turned[:, chunk * CHUNK : (chunk + 1) * CHUNK] = piece
        if flat is not None:
            flat[chunk * CHUNK : (chunk + 1) * CHUNK, :] = piece.T


def allowed_in(start, first, diagonal):
    row = lax.broadcasted_iota(jnp.int32, (TILE, TILE), 0)
    ok = row >= start - first
    if diagonal:
        ok = ok & (row <= lax.broadcasted_iota(jnp.int32, (TILE, TILE), 1))
    return ok


def per_tile(tile_start_ref, i, body):
    reach = jnp.clip(i + REACH - tile_start_ref[i], 1, REACH)
    for count in range(1, REACH + 1):
        pl.when(reach == count)(functools.partial(body, count))


def forward_kernel(
    tile_start_ref, start_ref, kvq_ref, halo_ref, out_ref, stat_ref, key_flat, value_turned
):
    fill(halo_ref, kvq_ref, 0, key_flat, None)
    fill(halo_ref, kvq_ref, 1, None, value_turned)

    def tile(i, _):
        def body(count):
            q = tile_of(kvq_ref, 2, i)
            start = start_ref[pl.ds(i, 1), :]
            scores = []
            top = None
            for j in range(count):
                first = pl.multiple_of((i + REACH - count + j) * TILE, TILE)
                s = nn(key_flat[pl.ds(first, TILE), :], q)
                s = jnp.where(allowed_in(start, first, j == count - 1), s, NEG)
                scores.append(s)
                t = jnp.max(s, axis=0, keepdims=True)
                top = t if top is None else jnp.maximum(top, t)
            shift = top * (SCALE * LOG2E)
            total = None
            out = None
            for j in range(count):
                first = pl.multiple_of((i + REACH - count + j) * TILE, TILE)
                e = jnp.exp2(scores[j] * (SCALE * LOG2E) - shift)
                t = jnp.sum(e, axis=0, keepdims=True)
                total = t if total is None else total + t
                o = nn(value_turned[:, pl.ds(first, TILE)], e.astype(BF16))
                out = o if out is None else out + o
            out = (out / total).astype(BF16)
            out_ref[2 * i, 0] = out[:, :CHUNK]
            out_ref[2 * i + 1, 0] = out[:, CHUNK:]
            stat_ref[pl.ds(i, 1), :] = shift + jnp.log2(total)

        per_tile(tile_start_ref, i, body)
        return 0

    lax.fori_loop(0, TILES, tile, 0)


def forward(tile_start, start, kvq, halo):
    return pl.pallas_call(
        forward_kernel,
        in_specs=[smem(), vmem(), vmem(), vmem()],
        out_specs=[vmem(), vmem()],
        out_shape=[
            jax.ShapeDtypeStruct((CHUNKS, 1, HEAD_DIM, CHUNK), BF16),
            jax.ShapeDtypeStruct((TILES, TILE), F32),
        ],
        scratch_shapes=[
            pltpu.VMEM((WINDOW, HEAD_DIM), BF16),
            pltpu.VMEM((HEAD_DIM, WINDOW), BF16),
        ],
        compiler_params=pltpu.CompilerParams(vmem_limit_bytes=VMEM_LIMIT),
        cost_estimate=pl.CostEstimate(
            flops=2 * 2 * 2560 * GROUP * 256, bytes_accessed=8 << 20, transcendentals=GROUP * 1280
        ),
        name="forward",
    )(tile_start, start, kvq, halo)


def backward_tiles(
    tile_start_ref, start_ref, kvq_ref, g_ref, out_ref, stat_ref, grads_ref,
    key_flat, key_turned, value_flat, key_sum, value_sum, low, high
):
    def tile(i, _):
        def body(count):
            q = tile_of(kvq_ref, 2, i)
            g = tile_of(g_ref, 0, i)
            o = tile_of(out_ref, 0, i)
            delta = jnp.sum(o.astype(F32) * g.astype(F32), axis=0, keepdims=True)
            start = start_ref[pl.ds(i, 1), :]
            stat = stat_ref[pl.ds(i, 1), :]
            grad_q = None
            for j in range(count):
                first = pl.multiple_of((i + REACH - count + j) * TILE, TILE)
                span = pl.ds(first, TILE)
                s = nn(key_flat[span, :], q)
                p = jnp.exp2(s * (SCALE * LOG2E) - stat)
                p = jnp.where(allowed_in(start, first, j == count - 1), p, 0.0)
                p_b = p.astype(BF16)
                grad_p = nn(value_flat[span, :], g)
                d = (p * (grad_p - delta)).astype(BF16)
                t = nn(key_turned[:, span], d)
                grad_q = t if grad_q is None else grad_q + t
                key_sum[:, span] += nt(q, d)
                value_sum[:, span] += nt(g, p_b)
            grad_q = (grad_q * SCALE).astype(BF16)
            grads_ref[2 * i, 2] = grad_q[:, :CHUNK]
            grads_ref[2 * i + 1, 2] = grad_q[:, CHUNK:]

        per_tile(tile_start_ref, i, body)
        return 0

    lax.fori_loop(low, high, tile, 0)


def backward_kernel(
    tile_start_ref, start_ref, kvq_ref, halo_ref, g_ref, out_ref, stat_ref,
    grads_ref, back_ref, rest_ref, key_flat, key_turned, value_flat, key_sum, value_sum
):
    fill(halo_ref, kvq_ref, 0, key_flat, key_turned)
    fill(halo_ref, kvq_ref, 1, value_flat, None)
    key_sum[...] = jnp.zeros_like(key_sum)
    value_sum[...] = jnp.zeros_like(value_sum)
    backward_tiles(
        tile_start_ref, start_ref, kvq_ref, g_ref, out_ref, stat_ref, grads_ref,
        key_flat, key_turned, value_flat, key_sum, value_sum, 0, TILES
    )
    for n, (sums, factor) in enumerate(((key_sum, SCALE), (value_sum, 1.0))):
        for chunk in range(HALO + CHUNKS):
            piece = sums[:, chunk * CHUNK : (chunk + 1) * CHUNK] * factor
            if chunk < HALO:
                back_ref[chunk, n] = piece.astype(BF16)
            else:
                grads_ref[chunk - HALO, n] = piece.astype(BF16)
            if chunk >= CHUNKS:
                rest_ref[chunk - CHUNKS, n] = piece


def backward(tile_start, start, kvq, halo, g, out, stat):
    return pl.pallas_call(
        backward_kernel,
        in_specs=[smem()] + [vmem()] * 6,
        out_specs=[vmem()] * 3,
        out_shape=[
            jax.ShapeDtypeStruct((CHUNKS, 3, HEAD_DIM, CHUNK), BF16),
            jax.ShapeDtypeStruct((HALO, 2, HEAD_DIM, CHUNK), BF16),
            jax.ShapeDtypeStruct((HALO, 2, HEAD_DIM, CHUNK), F32),
        ],
        scratch_shapes=[
            pltpu.VMEM((WINDOW, HEAD_DIM), BF16),
            pltpu.VMEM((HEAD_DIM, WINDOW), BF16),
            pltpu.VMEM((WINDOW, HEAD_DIM), BF16),
            pltpu.VMEM((HEAD_DIM, WINDOW), F32),
            pltpu.VMEM((HEAD_DIM, WINDOW), F32),
        ],
        compiler_params=pltpu.CompilerParams(vmem_limit_bytes=VMEM_LIMIT),
        cost_estimate=pl.CostEstimate(
            flops=2 * 5 * 2560 * GROUP * 256, bytes_accessed=12 << 20, transcendentals=GROUP * 1280
        ),
        name="backward",
    )(tile_start, start, kvq, halo, g, out, stat)


def join_kernel(back_ref, rest_ref, _, out_ref):
    out_ref[...] = (rest_ref[...] + back_ref[...].astype(F32)).astype(BF16)


def join(back, rest, grads):
    whole = (HALO, 2, HEAD_DIM, CHUNK)
    return pl.pallas_call(
        join_kernel,
        grid=(1,),
        in_specs=[
            pl.BlockSpec(whole, lambda i: (0, 0, 0, 0)),
            pl.BlockSpec(whole, lambda i: (0, 0, 0, 0)),
            pl.BlockSpec(memory_space=pl.ANY),
        ],
        out_specs=pl.BlockSpec(whole, lambda i: (CHUNKS // HALO - 1, 0, 0, 0)),
        out_shape=jax.ShapeDtypeStruct(grads.shape, BF16),
        input_output_aliases={2: 0},
        name="join",
    )(back, rest, grads)


def group_pairs():
    def index(x, zh, y, zl, c):
        return (((x * 2 + zh) * 4 + y) * 4 + zl) * 2 + c

    pairs = []
    for group in range(7):
        for y in range(4):
            for zl in range(4):
                for c in range(2):
                    pairs.append(
                        (
                            index(group // 2, group % 2, y, zl, c),
                            index((group + 1) // 2, (group + 1) % 2, y, 3 - zl, c),
                        )
                    )
    return pairs


def to_heads(array):
    return lax.all_to_all(array, GROUP_AXES, split_axis=0, concat_axis=0, tiled=True)


def places(doc_ids):
    group = lax.axis_index("x") * 2 + lax.axis_index("zh")
    own = lax.dynamic_slice_in_dim(doc_ids, group * GROUP, GROUP)
    ahead = lax.dynamic_slice_in_dim(doc_ids, jnp.maximum(group * GROUP - AHEAD, 0), AHEAD)
    ahead = jnp.where(group > 0, ahead, -1)
    docs = jnp.arange(DOCS, dtype=jnp.int32)[:, None]
    first = jnp.sum((own[None] < docs).astype(jnp.int32), 1) + jnp.sum(
        (ahead[None] < docs).astype(jnp.int32), 1
    )
    start = jnp.sum(jnp.where(own[None] == docs, first[:, None], 0), 0)
    start = start.reshape(TILES, TILE)
    return start[:, 0] // TILE, start


def shards(queries, keys, values, cotangent, doc_ids):
    mirror = lax.axis_index("zh").astype(jnp.int32).reshape(1)
    kvq = to_heads(pack(mirror, keys, values, queries))
    g = to_heads(pack(mirror, cotangent))
    tile_start, start = places(doc_ids)
    pairs = group_pairs()
    halo = lax.ppermute(kvq[CHUNKS - HALO :, :2], AXES, pairs)
    out, stat = forward(tile_start, start, kvq, halo)
    grads, back, rest = backward(tile_start, start, kvq, halo, g, out, stat)
    back = lax.ppermute(back, AXES, [(b, a) for a, b in pairs])
    grads = join(back, rest, grads)
    (attended,) = unpack(mirror, to_heads(out))
    grad_k, grad_v, grad_q = unpack(mirror, to_heads(grads))
    return attended, grad_q, grad_k, grad_v


def solution(mesh):
    wide = Mesh(mesh.devices.reshape(4, 2, 4, 4, 2), AXES)
    rows = P(AXES, None)
    return jax.shard_map(
        shards,
        mesh=wide,
        in_specs=(rows, rows, rows, rows, P()),
        out_specs=(rows, rows, rows, rows),
        check_vma=False,
    )
```

```python
import functools
import math

import jax
import jax.numpy as jnp
from jax import lax
from jax.experimental import pallas as pl
from jax.experimental.pallas import tpu as pltpu
from jax.sharding import Mesh
from jax.sharding import PartitionSpec as P

HEAD_DIM = 96
HEADS = 32
CHUNK = 128
CHUNKS = 32
HALO = 8
DOCS = 64
GROUP = CHUNK * CHUNKS
AHEAD = CHUNK * HALO
WINDOW = GROUP + AHEAD
TILE = 256
TILES = GROUP // TILE
AHEAD_TILES = AHEAD // TILE
REACH = AHEAD_TILES + 1
NEG = -1e30
SCALE = 1.0 / math.sqrt(HEAD_DIM)
LOG2E = 1.4426950408889634
VMEM_LIMIT = 56 * 1024 * 1024

AXES = ("x", "zh", "y", "zl", "c")
GROUP_AXES = ("y", "zl", "c")
F32 = jnp.float32
BF16 = jnp.bfloat16


def vmem():
    return pl.BlockSpec(memory_space=pltpu.VMEM)


def smem():
    return pl.BlockSpec(memory_space=pltpu.SMEM)


def pack_kernel(mirror_ref, *refs):
    sources, out_ref = refs[:-1], refs[-1]
    mirrored = mirror_ref[0]
    for n, ref in enumerate(sources):
        turned = ref[...].T
        for zl in range(4):
            slot = 2 * jnp.where(mirrored == 1, 3 - zl, zl)
            piece = turned[zl * 192 : (zl + 1) * 192]
            out_ref[pl.ds(slot, 2), n] = piece.reshape(2, HEAD_DIM, CHUNK)


def pack(mirror, *arrays):
    count = len(arrays)
    return pl.pallas_call(
        pack_kernel,
        grid=(4,),
        in_specs=[smem()] + [pl.BlockSpec((CHUNK, 768), lambda y: (0, y))] * count,
        out_specs=pl.BlockSpec((8, count, HEAD_DIM, CHUNK), lambda y: (y, 0, 0, 0)),
        out_shape=jax.ShapeDtypeStruct((HEADS, count, HEAD_DIM, CHUNK), BF16),
        compiler_params=pltpu.CompilerParams(vmem_limit_bytes=VMEM_LIMIT),
        name="pack",
    )(mirror, *arrays)


def unpack_kernel(mirror_ref, in_ref, *out_refs):
    mirrored = mirror_ref[0]
    for n, out_ref in enumerate(out_refs):
        pieces = []
        for zl in range(4):
            slot = 2 * jnp.where(mirrored == 1, 3 - zl, zl)
            pieces.append(in_ref[pl.ds(slot, 2), n].reshape(192, CHUNK))
        out_ref[...] = jnp.concatenate(pieces, 0).T


def unpack(mirror, array):
    count = array.shape[1]
    return pl.pallas_call(
        unpack_kernel,
        grid=(4,),
        in_specs=[
            smem(),
            pl.BlockSpec((8, count, HEAD_DIM, CHUNK), lambda y: (y, 0, 0, 0)),
        ],
        out_specs=[pl.BlockSpec((CHUNK, 768), lambda y: (0, y))] * count,
        out_shape=[jax.ShapeDtypeStruct((CHUNK, HEADS * HEAD_DIM), BF16)] * count,
        compiler_params=pltpu.CompilerParams(vmem_limit_bytes=VMEM_LIMIT),
        name="unpack",
    )(mirror, array)


def tile_of(ref, n, i):
    return jnp.concatenate([ref[2 * i, n], ref[2 * i + 1, n]], 1)


def nn(a, b):
    return lax.dot_general(a, b, (((1,), (0,)), ((), ())), preferred_element_type=F32)


def nt(a, b):
    return lax.dot_general(a, b, (((1,), (1,)), ((), ())), preferred_element_type=F32)


def fill(halo_ref, own_ref, n, chunks, flat, turned):
    for chunk in chunks:
        piece = halo_ref[chunk, n] if chunk < HALO else own_ref[chunk - HALO, n]
        if turned is not None:
            turned[:, chunk * CHUNK : (chunk + 1) * CHUNK] = piece
        if flat is not None:
            flat[chunk * CHUNK : (chunk + 1) * CHUNK, :] = piece.T


def allowed_in(start, first, diagonal):
    row = lax.broadcasted_iota(jnp.int32, (TILE, TILE), 0)
    ok = row >= start - first
    if diagonal:
        ok = ok & (row <= lax.broadcasted_iota(jnp.int32, (TILE, TILE), 1))
    return ok


def per_tile(tile_start_ref, i, body):
    reach = jnp.clip(i + REACH - tile_start_ref[i], 1, REACH)
    for count in range(1, REACH + 1):
        pl.when(reach == count)(functools.partial(body, count))


def forward_tiles(
    low, tile_start_ref, start_ref, kvq_ref, out_ref, stat_ref, key_flat, value_turned
):
    def tile(step, _):
        i = low + step

        def body(count):
            q = tile_of(kvq_ref, 2, i)
            start = start_ref[pl.ds(i, 1), :]
            scores = []
            top = None
            for j in range(count):
                first = pl.multiple_of((i + REACH - count + j) * TILE, TILE)
                s = nn(key_flat[pl.ds(first, TILE), :], q)
                s = jnp.where(allowed_in(start, first, j == count - 1), s, NEG)
                scores.append(s)
                t = jnp.max(s, axis=0, keepdims=True)
                top = t if top is None else jnp.maximum(top, t)
            shift = top * (SCALE * LOG2E)
            total = None
            out = None
            for j in range(count):
                first = pl.multiple_of((i + REACH - count + j) * TILE, TILE)
                e = jnp.exp2(scores[j] * (SCALE * LOG2E) - shift)
                t = jnp.sum(e, axis=0, keepdims=True)
                total = t if total is None else total + t
                o = nn(value_turned[:, pl.ds(first, TILE)], e.astype(BF16))
                out = o if out is None else out + o
            out = (out / total).astype(BF16)
            out_ref[2 * step, 0] = out[:, :CHUNK]
            out_ref[2 * step + 1, 0] = out[:, CHUNK:]
            stat_ref[0, pl.ds(step, 1), :] = shift + jnp.log2(total)

        per_tile(tile_start_ref, i, body)
        return 0

    lax.fori_loop(0, AHEAD_TILES, tile, 0)


def late_forward_kernel(
    tile_start_ref, start_ref, kvq_ref, out_ref, stat_ref, key_flat, value_turned
):
    @pl.when(pl.program_id(0) == 0)
    def _():
        fill(None, kvq_ref, 0, range(HALO, HALO + CHUNKS), key_flat, None)
        fill(None, kvq_ref, 1, range(HALO, HALO + CHUNKS), None, value_turned)

    forward_tiles(
        (pl.program_id(0) + 1) * AHEAD_TILES,
        tile_start_ref, start_ref, kvq_ref, out_ref, stat_ref, key_flat, value_turned
    )


def early_forward_kernel(
    tile_start_ref, start_ref, kvq_ref, halo_ref, _, __, out_ref, stat_ref, key_flat, value_turned
):
    fill(halo_ref, kvq_ref, 0, range(2 * HALO), key_flat, None)
    fill(halo_ref, kvq_ref, 1, range(2 * HALO), None, value_turned)
    forward_tiles(
        0, tile_start_ref, start_ref, kvq_ref, out_ref, stat_ref, key_flat, value_turned
    )


def cost(products, tiles):
    return pl.CostEstimate(
        flops=2 * products * tiles * REACH * TILE * TILE * 256,
        bytes_accessed=8 << 20,
        transcendentals=tiles * REACH * TILE * TILE,
    )


OUT_SHAPES = [
    jax.ShapeDtypeStruct((CHUNKS, 1, HEAD_DIM, CHUNK), BF16),
    jax.ShapeDtypeStruct((TILES // AHEAD_TILES, AHEAD_TILES, TILE), F32),
]


def out_specs(first):
    return [
        pl.BlockSpec((HALO, 1, HEAD_DIM, CHUNK), lambda b: (b + first, 0, 0, 0)),
        pl.BlockSpec((1, AHEAD_TILES, TILE), lambda b: (b + first, 0, 0)),
    ]


def late_forward(tile_start, start, kvq):
    return pl.pallas_call(
        late_forward_kernel,
        grid=(TILES // AHEAD_TILES - 1,),
        in_specs=[smem(), vmem(), vmem()],
        out_specs=out_specs(1),
        out_shape=OUT_SHAPES,
        scratch_shapes=[
            pltpu.VMEM((WINDOW, HEAD_DIM), BF16),
            pltpu.VMEM((HEAD_DIM, WINDOW), BF16),
        ],
        compiler_params=pltpu.CompilerParams(vmem_limit_bytes=VMEM_LIMIT),
        cost_estimate=cost(2, TILES - AHEAD_TILES),
        name="late_forward",
    )(tile_start, start, kvq)


def early_forward(tile_start, start, kvq, halo, out, stat):
    whole = pl.BlockSpec((2 * HALO, 3, HEAD_DIM, CHUNK), lambda b: (0, 0, 0, 0))
    return pl.pallas_call(
        early_forward_kernel,
        grid=(1,),
        in_specs=[smem(), vmem(), whole, vmem()] + [pl.BlockSpec(memory_space=pl.ANY)] * 2,
        out_specs=out_specs(0),
        out_shape=OUT_SHAPES,
        input_output_aliases={4: 0, 5: 1},
        scratch_shapes=[
            pltpu.VMEM((2 * AHEAD, HEAD_DIM), BF16),
            pltpu.VMEM((HEAD_DIM, 2 * AHEAD), BF16),
        ],
        compiler_params=pltpu.CompilerParams(vmem_limit_bytes=VMEM_LIMIT),
        cost_estimate=cost(2, AHEAD_TILES),
        name="early_forward",
    )(tile_start, start, kvq, halo, out, stat)


def backward_tiles(
    low, high, tile_start_ref, start_ref, kvq_ref, g_ref, out_ref, stat_ref, store,
    key_flat, key_turned, value_flat, key_sum, value_sum
):
    def tile(i, _):
        def body(count):
            q = tile_of(kvq_ref, 2, i)
            g = tile_of(g_ref, 0, i)
            o = tile_of(out_ref, 0, i)
            delta = jnp.sum(o.astype(F32) * g.astype(F32), axis=0, keepdims=True)
            start = start_ref[pl.ds(i, 1), :]
            stat = stat_ref[i // AHEAD_TILES, pl.ds(i % AHEAD_TILES, 1), :]
            grad_q = None
            for j in range(count):
                first = pl.multiple_of((i + REACH - count + j) * TILE, TILE)
                span = pl.ds(first, TILE)
                s = nn(key_flat[span, :], q)
                p = jnp.exp2(s * (SCALE * LOG2E) - stat)
                p = jnp.where(allowed_in(start, first, j == count - 1), p, 0.0)
                grad_p = nn(value_flat[span, :], g)
                d = (p * (grad_p - delta)).astype(BF16)
                t = nn(key_turned[:, span], d)
                grad_q = t if grad_q is None else grad_q + t
                key_sum[:, span] += nt(q, d)
                value_sum[:, span] += nt(g, p.astype(BF16))
            grad_q = (grad_q * SCALE).astype(BF16)
            store(2 * i, grad_q[:, :CHUNK])
            store(2 * i + 1, grad_q[:, CHUNK:])

        per_tile(tile_start_ref, i, body)
        return 0

    lax.fori_loop(low, high, tile, 0)


def early_backward_kernel(
    tile_start_ref, start_ref, kvq_ref, halo_ref, g_ref, out_ref, stat_ref,
    back_ref, carry_ref, grad_q_ref, key_flat, key_turned, value_flat, key_sum, value_sum
):
    fill(halo_ref, kvq_ref, 0, range(2 * HALO), key_flat, key_turned)
    fill(halo_ref, kvq_ref, 1, range(2 * HALO), value_flat, None)
    key_sum[...] = jnp.zeros_like(key_sum)
    value_sum[...] = jnp.zeros_like(value_sum)

    def store(chunk, value):
        grad_q_ref[chunk] = value

    backward_tiles(
        0, AHEAD_TILES, tile_start_ref, start_ref, kvq_ref, g_ref, out_ref, stat_ref, store,
        key_flat, key_turned, value_flat, key_sum, value_sum
    )
    for n, (sums, factor) in enumerate(((key_sum, SCALE), (value_sum, 1.0))):
        for chunk in range(HALO):
            piece = sums[:, chunk * CHUNK : (chunk + 1) * CHUNK] * factor
            back_ref[chunk, n] = piece.astype(BF16)
        carry_ref[n] = sums[:, AHEAD:]


def late_backward_kernel(
    tile_start_ref, start_ref, kvq_ref, g_ref, out_ref, stat_ref, carry_ref, grad_q_ref,
    grads_ref, rest_ref, key_flat, key_turned, value_flat, key_sum, value_sum
):
    chunks = range(HALO, HALO + CHUNKS)
    fill(None, kvq_ref, 0, chunks, key_flat, key_turned)
    fill(None, kvq_ref, 1, chunks, value_flat, None)
    for n, sums in enumerate((key_sum, value_sum)):
        sums[:, AHEAD : 2 * AHEAD] = carry_ref[n]
        sums[:, 2 * AHEAD :] = jnp.zeros((HEAD_DIM, WINDOW - 2 * AHEAD), F32)
    for chunk in range(HALO):
        grads_ref[chunk, 2] = grad_q_ref[chunk]

    def store(chunk, value):
        grads_ref[chunk, 2] = value

    backward_tiles(
        AHEAD_TILES, TILES, tile_start_ref, start_ref, kvq_ref, g_ref, out_ref, stat_ref, store,
        key_flat, key_turned, value_flat, key_sum, value_sum
    )
    for n, (sums, factor) in enumerate(((key_sum, SCALE), (value_sum, 1.0))):
        for chunk in chunks:
            piece = sums[:, chunk * CHUNK : (chunk + 1) * CHUNK] * factor
            grads_ref[chunk - HALO, n] = piece.astype(BF16)
            if chunk >= CHUNKS:
                rest_ref[chunk - CHUNKS, n] = piece


def sums_scratch(window):
    return [
        pltpu.VMEM((window, HEAD_DIM), BF16),
        pltpu.VMEM((HEAD_DIM, window), BF16),
        pltpu.VMEM((window, HEAD_DIM), BF16),
        pltpu.VMEM((HEAD_DIM, window), F32),
        pltpu.VMEM((HEAD_DIM, window), F32),
    ]


def early_backward(tile_start, start, kvq, halo, g, out, stat):
    def part(count, width):
        return pl.BlockSpec((count, width, HEAD_DIM, CHUNK), lambda b: (0, 0, 0, 0))

    return pl.pallas_call(
        early_backward_kernel,
        grid=(1,),
        in_specs=[smem(), vmem(), part(HALO, 3), vmem(), part(HALO, 1), part(HALO, 1), vmem()],
        out_specs=[vmem()] * 3,
        out_shape=[
            jax.ShapeDtypeStruct((HALO, 2, HEAD_DIM, CHUNK), BF16),
            jax.ShapeDtypeStruct((2, HEAD_DIM, AHEAD), F32),
            jax.ShapeDtypeStruct((HALO, HEAD_DIM, CHUNK), BF16),
        ],
        scratch_shapes=sums_scratch(2 * AHEAD),
        compiler_params=pltpu.CompilerParams(vmem_limit_bytes=VMEM_LIMIT),
        cost_estimate=cost(5, AHEAD_TILES),
        name="early_backward",
    )(tile_start, start, kvq, halo, g, out, stat)


def late_backward(tile_start, start, kvq, g, out, stat, carry, grad_q):
    return pl.pallas_call(
        late_backward_kernel,
        in_specs=[smem()] + [vmem()] * 7,
        out_specs=[vmem()] * 2,
        out_shape=[
            jax.ShapeDtypeStruct((CHUNKS, 3, HEAD_DIM, CHUNK), BF16),
            jax.ShapeDtypeStruct((HALO, 2, HEAD_DIM, CHUNK), F32),
        ],
        scratch_shapes=sums_scratch(WINDOW),
        compiler_params=pltpu.CompilerParams(vmem_limit_bytes=VMEM_LIMIT),
        cost_estimate=cost(5, TILES - AHEAD_TILES),
        name="late_backward",
    )(tile_start, start, kvq, g, out, stat, carry, grad_q)


def join_kernel(back_ref, rest_ref, _, out_ref):
    out_ref[...] = (rest_ref[...] + back_ref[...].astype(F32)).astype(BF16)


def join(back, rest, grads):
    whole = (HALO, 2, HEAD_DIM, CHUNK)
    return pl.pallas_call(
        join_kernel,
        grid=(1,),
        in_specs=[
            pl.BlockSpec(whole, lambda i: (0, 0, 0, 0)),
            pl.BlockSpec(whole, lambda i: (0, 0, 0, 0)),
            pl.BlockSpec(memory_space=pl.ANY),
        ],
        out_specs=pl.BlockSpec(whole, lambda i: (CHUNKS // HALO - 1, 0, 0, 0)),
        out_shape=jax.ShapeDtypeStruct(grads.shape, BF16),
        input_output_aliases={2: 0},
        name="join",
    )(back, rest, grads)


def group_pairs():
    def index(x, zh, y, zl, c):
        return (((x * 2 + zh) * 4 + y) * 4 + zl) * 2 + c

    pairs = []
    for group in range(7):
        for y in range(4):
            for zl in range(4):
                for c in range(2):
                    pairs.append(
                        (
                            index(group // 2, group % 2, y, zl, c),
                            index((group + 1) // 2, (group + 1) % 2, y, 3 - zl, c),
                        )
                    )
    return pairs


def to_heads(array):
    return lax.all_to_all(array, GROUP_AXES, split_axis=0, concat_axis=0, tiled=True)


def places(doc_ids):
    group = lax.axis_index("x") * 2 + lax.axis_index("zh")
    own = lax.dynamic_slice_in_dim(doc_ids, group * GROUP, GROUP)
    ahead = lax.dynamic_slice_in_dim(doc_ids, jnp.maximum(group * GROUP - AHEAD, 0), AHEAD)
    ahead = jnp.where(group > 0, ahead, -1)
    docs = jnp.arange(DOCS, dtype=jnp.int32)[:, None]
    first = jnp.sum((own[None] < docs).astype(jnp.int32), 1) + jnp.sum(
        (ahead[None] < docs).astype(jnp.int32), 1
    )
    start = jnp.sum(jnp.where(own[None] == docs, first[:, None], 0), 0)
    start = start.reshape(TILES, TILE)
    return start[:, 0] // TILE, start


def shards(queries, keys, values, cotangent, doc_ids):
    mirror = lax.axis_index("zh").astype(jnp.int32).reshape(1)
    kvq = to_heads(pack(mirror, keys, values, queries))
    g = to_heads(pack(mirror, cotangent))
    tile_start, start = places(doc_ids)
    pairs = group_pairs()
    halo = lax.ppermute(kvq[CHUNKS - HALO :, :2], AXES, pairs)
    out, stat = late_forward(tile_start, start, kvq)
    out, stat = early_forward(tile_start, start, kvq, halo, out, stat)
    back, carry, early_q = early_backward(tile_start, start, kvq, halo, g, out, stat)
    grads, rest = late_backward(tile_start, start, kvq, g, out, stat, carry, early_q)
    back = lax.ppermute(back, AXES, [(b, a) for a, b in pairs])
    grads = join(back, rest, grads)
    (attended,) = unpack(mirror, to_heads(out))
    grad_k, grad_v, grad_q = unpack(mirror, to_heads(grads))
    return attended, grad_q, grad_k, grad_v


def solution(mesh):
    wide = Mesh(mesh.devices.reshape(4, 2, 4, 4, 2), AXES)
    rows = P(AXES, None)
    return jax.shard_map(
        shards,
        mesh=wide,
        in_specs=(rows, rows, rows, rows, P()),
        out_specs=(rows, rows, rows, rows),
        check_vma=False,
    )
```

```python
import functools
import math

import jax
import jax.numpy as jnp
from jax import lax
from jax.experimental import pallas as pl
from jax.experimental.pallas import tpu as pltpu
from jax.sharding import Mesh
from jax.sharding import PartitionSpec as P

HEAD_DIM = 96
HEADS = 32
CHUNK = 128
CHUNKS = 32
HALO = 8
DOC_BITS = 6
EXTRA = 16
WIDE = HEAD_DIM + EXTRA
FAR = 2.0**20
GROUP = CHUNK * CHUNKS
AHEAD = CHUNK * HALO
WINDOW = GROUP + AHEAD
TILE = 256
TILES = GROUP // TILE
AHEAD_TILES = AHEAD // TILE
REACH = AHEAD_TILES + 1
NEG = -1e30
SCALE = 1.0 / math.sqrt(HEAD_DIM)
LOG2E = 1.4426950408889634
MIB = 1024 * 1024

AXES = ("x", "zh", "y", "zl", "c")
GROUP_AXES = ("y", "zl", "c")
F32 = jnp.float32
BF16 = jnp.bfloat16


def vmem():
    return pl.BlockSpec(memory_space=pltpu.VMEM)


def smem():
    return pl.BlockSpec(memory_space=pltpu.SMEM)


def pack_kernel(mirror_ref, *refs):
    sources, out_ref = refs[:-1], refs[-1]
    mirrored = mirror_ref[0]
    for n, ref in enumerate(sources):
        turned = ref[...].T
        for zl in range(4):
            slot = 2 * jnp.where(mirrored == 1, 3 - zl, zl)
            piece = turned[zl * 192 : (zl + 1) * 192]
            out_ref[pl.ds(slot, 2), n] = piece.reshape(2, HEAD_DIM, CHUNK)


def pack(mirror, *arrays):
    count = len(arrays)
    return pl.pallas_call(
        pack_kernel,
        grid=(4,),
        in_specs=[smem()] + [pl.BlockSpec((CHUNK, 768), lambda y: (0, y))] * count,
        out_specs=pl.BlockSpec((8, count, HEAD_DIM, CHUNK), lambda y: (y, 0, 0, 0)),
        out_shape=jax.ShapeDtypeStruct((HEADS, count, HEAD_DIM, CHUNK), BF16),
        compiler_params=pltpu.CompilerParams(vmem_limit_bytes=8 * MIB),
        name="pack",
    )(mirror, *arrays)


def unpack_kernel(mirror_ref, in_ref, *out_refs):
    mirrored = mirror_ref[0]
    for n, out_ref in enumerate(out_refs):
        pieces = []
        for zl in range(4):
            slot = 2 * jnp.where(mirrored == 1, 3 - zl, zl)
            pieces.append(in_ref[pl.ds(slot, 2), n].reshape(192, CHUNK))
        out_ref[...] = jnp.concatenate(pieces, 0).T


def unpack(mirror, array):
    count = array.shape[1]
    return pl.pallas_call(
        unpack_kernel,
        grid=(4,),
        in_specs=[
            smem(),
            pl.BlockSpec((8, count, HEAD_DIM, CHUNK), lambda y: (y, 0, 0, 0)),
        ],
        out_specs=[pl.BlockSpec((CHUNK, 768), lambda y: (0, y))] * count,
        out_shape=[jax.ShapeDtypeStruct((CHUNK, HEADS * HEAD_DIM), BF16)] * count,
        compiler_params=pltpu.CompilerParams(vmem_limit_bytes=8 * MIB),
        name="unpack",
    )(mirror, array)


def tile_of(ref, n, i):
    return jnp.concatenate([ref[2 * i, n], ref[2 * i + 1, n]], 1)


def nn(a, b):
    return lax.dot_general(a, b, (((1,), (0,)), ((), ())), preferred_element_type=F32)


def nt(a, b):
    return lax.dot_general(a, b, (((1,), (1,)), ((), ())), preferred_element_type=F32)


def each_chunk(halo_ref, own_ref, n, chunks):
    for chunk in chunks:
        piece = halo_ref[chunk, n] if chunk < HALO else own_ref[chunk - HALO, n]
        yield slice(chunk * CHUNK, (chunk + 1) * CHUNK), piece


def fill_keys(halo_ref, own_ref, code_ref, chunks, flat, turned):
    for span, piece in each_chunk(halo_ref, own_ref, 0, chunks):
        flat[span, :] = jnp.concatenate([piece, code_ref[:, span]], 0).T
        if turned is not None:
            turned[:, span] = piece


def fill_value_rows(halo_ref, own_ref, chunks, flat):
    row = lax.broadcasted_iota(jnp.int32, (EXTRA, CHUNK), 0)
    minus = jnp.where(row < 3, -1.0, 0.0).astype(BF16)
    for span, piece in each_chunk(halo_ref, own_ref, 1, chunks):
        flat[span, :] = jnp.concatenate([piece, minus], 0).T


def fill_value_columns(halo_ref, own_ref, chunks, turned):
    for span, piece in each_chunk(halo_ref, own_ref, 1, chunks):
        turned[:HEAD_DIM, span] = piece
        turned[HEAD_DIM:, span] = jnp.ones((EXTRA, CHUNK), BF16)


def with_row(extra, first, value):
    high = value.astype(BF16).astype(F32)
    middle = (value - high).astype(BF16).astype(F32)
    low = value - high - middle
    row = lax.broadcasted_iota(jnp.int32, (EXTRA, TILE), 0)
    for n, part in enumerate((high, middle, low)):
        extra = jnp.where(row == first + n, part, extra)
    return extra.astype(BF16)


def causal():
    row = lax.broadcasted_iota(jnp.int32, (TILE, TILE), 0)
    return row <= lax.broadcasted_iota(jnp.int32, (TILE, TILE), 1)


def per_tile(tile_start_ref, i, body):
    reach = jnp.clip(i + REACH - tile_start_ref[i], 1, REACH)
    for count in range(1, REACH + 1):
        pl.when(reach == count)(functools.partial(body, count))


def forward_tiles(
    low, tile_start_ref, query_code_ref, kvq_ref, out_ref, stat_ref, key_flat, value_turned
):
    def tile(step, _):
        i = low + step

        def body(count):
            q = jnp.concatenate([tile_of(kvq_ref, 2, i), query_code_ref[i]], 0)
            scores = []
            top = None
            for j in range(count):
                first = pl.multiple_of((i + REACH - count + j) * TILE, TILE)
                s = nn(key_flat[pl.ds(first, TILE), :], q)
                if j == count - 1:
                    s = jnp.where(causal(), s, NEG)
                scores.append(s)
                t = jnp.max(s, axis=0, keepdims=True)
                top = t if top is None else jnp.maximum(top, t)
            shift = top * (SCALE * LOG2E)
            out = None
            for j in range(count):
                first = pl.multiple_of((i + REACH - count + j) * TILE, TILE)
                e = jnp.exp2(scores[j] * (SCALE * LOG2E) - shift)
                o = nn(value_turned[:, pl.ds(first, TILE)], e.astype(BF16))
                out = o if out is None else out + o
            total = out[HEAD_DIM : HEAD_DIM + 1]
            out = (out[:HEAD_DIM] / total).astype(BF16)
            out_ref[2 * step, 0] = out[:, :CHUNK]
            out_ref[2 * step + 1, 0] = out[:, CHUNK:]
            stat_ref[0, pl.ds(step, 1), :] = top + jnp.log(total) * (1.0 / SCALE)

        per_tile(tile_start_ref, i, body)
        return 0

    lax.fori_loop(0, AHEAD_TILES, tile, 0)


def late_forward_kernel(
    tile_start_ref, key_code_ref, query_code_ref, kvq_ref, out_ref, stat_ref, key_flat, value_turned
):
    @pl.when(pl.program_id(0) == 0)
    def _():
        chunks = range(HALO, HALO + CHUNKS)
        fill_keys(None, kvq_ref, key_code_ref, chunks, key_flat, None)
        fill_value_columns(None, kvq_ref, chunks, value_turned)

    forward_tiles(
        (pl.program_id(0) + 1) * AHEAD_TILES,
        tile_start_ref, query_code_ref, kvq_ref, out_ref, stat_ref, key_flat, value_turned
    )


def early_forward_kernel(
    tile_start_ref, key_code_ref, query_code_ref, kvq_ref, halo_ref, _, __, out_ref, stat_ref,
    key_flat, value_turned
):
    fill_keys(halo_ref, kvq_ref, key_code_ref, range(2 * HALO), key_flat, None)
    fill_value_columns(halo_ref, kvq_ref, range(2 * HALO), value_turned)
    forward_tiles(
        0, tile_start_ref, query_code_ref, kvq_ref, out_ref, stat_ref, key_flat, value_turned
    )


def cost(products, tiles):
    return pl.CostEstimate(
        flops=2 * products * tiles * REACH * TILE * TILE * 256,
        bytes_accessed=8 << 20,
        transcendentals=tiles * REACH * TILE * TILE,
    )


OUT_SHAPES = [
    jax.ShapeDtypeStruct((CHUNKS, 1, HEAD_DIM, CHUNK), BF16),
    jax.ShapeDtypeStruct((TILES // AHEAD_TILES, AHEAD_TILES, TILE), F32),
]


def out_specs(first):
    return [
        pl.BlockSpec((HALO, 1, HEAD_DIM, CHUNK), lambda b: (b + first, 0, 0, 0)),
        pl.BlockSpec((1, AHEAD_TILES, TILE), lambda b: (b + first, 0, 0)),
    ]


def late_forward(tile_start, codes, kvq):
    return pl.pallas_call(
        late_forward_kernel,
        grid=(TILES // AHEAD_TILES - 1,),
        in_specs=[smem(), vmem(), vmem(), vmem()],
        out_specs=out_specs(1),
        out_shape=OUT_SHAPES,
        scratch_shapes=[
            pltpu.VMEM((WINDOW, WIDE), BF16),
            pltpu.VMEM((WIDE, WINDOW), BF16),
        ],
        compiler_params=pltpu.CompilerParams(vmem_limit_bytes=18 * MIB),
        cost_estimate=cost(2, TILES - AHEAD_TILES),
        name="late_forward",
    )(tile_start, *codes, kvq)


def early_forward(tile_start, codes, kvq, halo, out, stat):
    whole = pl.BlockSpec((2 * HALO, 3, HEAD_DIM, CHUNK), lambda b: (0, 0, 0, 0))
    return pl.pallas_call(
        early_forward_kernel,
        grid=(1,),
        in_specs=[smem(), vmem(), vmem(), whole, vmem()] + [pl.BlockSpec(memory_space=pl.ANY)] * 2,
        out_specs=out_specs(0),
        out_shape=OUT_SHAPES,
        input_output_aliases={5: 0, 6: 1},
        scratch_shapes=[
            pltpu.VMEM((2 * AHEAD, WIDE), BF16),
            pltpu.VMEM((WIDE, 2 * AHEAD), BF16),
        ],
        compiler_params=pltpu.CompilerParams(vmem_limit_bytes=14 * MIB),
        cost_estimate=cost(2, AHEAD_TILES),
        name="early_forward",
    )(tile_start, *codes, kvq, halo, out, stat)


def backward_tiles(
    low, high, tile_start_ref, query_code_ref, kvq_ref, g_ref, out_ref, stat_ref, store,
    key_flat, key_turned, value_flat, key_sum, value_sum
):
    def tile(i, _):
        def body(count):
            q = tile_of(kvq_ref, 2, i)
            g = tile_of(g_ref, 0, i)
            o = tile_of(out_ref, 0, i)
            delta = jnp.sum(o.astype(F32) * g.astype(F32), axis=0, keepdims=True)
            stat = stat_ref[i // AHEAD_TILES, pl.ds(i % AHEAD_TILES, 1), :]
            code = query_code_ref[i].astype(F32)
            q_wide = jnp.concatenate([q, with_row(code, 2 * DOC_BITS, stat)], 0)
            g_wide = jnp.concatenate([g, with_row(jnp.zeros_like(code), 0, delta)], 0)
            grad_q = None
            for j in range(count):
                first = pl.multiple_of((i + REACH - count + j) * TILE, TILE)
                span = pl.ds(first, TILE)
                p = jnp.exp2(nn(key_flat[span, :], q_wide) * (SCALE * LOG2E))
                if j == count - 1:
                    p = jnp.where(causal(), p, 0.0)
                d = (p * nn(value_flat[span, :], g_wide)).astype(BF16)
                t = nn(key_turned[:, span], d)
                grad_q = t if grad_q is None else grad_q + t
                key_sum[:, span] += nt(q, d)
                value_sum[:, span] += nt(g, p.astype(BF16))
            grad_q = (grad_q * SCALE).astype(BF16)
            store(2 * i, grad_q[:, :CHUNK])
            store(2 * i + 1, grad_q[:, CHUNK:])

        per_tile(tile_start_ref, i, body)
        return 0

    lax.fori_loop(low, high, tile, 0)


def early_backward_kernel(
    tile_start_ref, key_code_ref, query_code_ref, kvq_ref, halo_ref, g_ref, out_ref, stat_ref,
    back_ref, carry_ref, grad_q_ref, key_flat, key_turned, value_flat, key_sum, value_sum
):
    fill_keys(halo_ref, kvq_ref, key_code_ref, range(2 * HALO), key_flat, key_turned)
    fill_value_rows(halo_ref, kvq_ref, range(2 * HALO), value_flat)
    key_sum[...] = jnp.zeros_like(key_sum)
    value_sum[...] = jnp.zeros_like(value_sum)

    def store(chunk, value):
        grad_q_ref[chunk] = value

    backward_tiles(
        0, AHEAD_TILES, tile_start_ref, query_code_ref, kvq_ref, g_ref, out_ref, stat_ref, store,
        key_flat, key_turned, value_flat, key_sum, value_sum
    )
    for n, (sums, factor) in enumerate(((key_sum, SCALE), (value_sum, 1.0))):
        for chunk in range(HALO):
            piece = sums[:, chunk * CHUNK : (chunk + 1) * CHUNK] * factor
            back_ref[chunk, n] = piece.astype(BF16)
        carry_ref[n] = sums[:, AHEAD:]


def late_backward_kernel(
    tile_start_ref, key_code_ref, query_code_ref, kvq_ref, g_ref, out_ref, stat_ref, carry_ref,
    grad_q_ref,
    grads_ref, rest_ref, key_flat, key_turned, value_flat, key_sum, value_sum
):
    chunks = range(HALO, HALO + CHUNKS)
    fill_keys(None, kvq_ref, key_code_ref, chunks, key_flat, key_turned)
    fill_value_rows(None, kvq_ref, chunks, value_flat)
    for n, sums in enumerate((key_sum, value_sum)):
        sums[:, AHEAD : 2 * AHEAD] = carry_ref[n]
        sums[:, 2 * AHEAD :] = jnp.zeros((HEAD_DIM, WINDOW - 2 * AHEAD), F32)
    for chunk in range(HALO):
        grads_ref[chunk, 2] = grad_q_ref[chunk]

    def store(chunk, value):
        grads_ref[chunk, 2] = value

    backward_tiles(
        AHEAD_TILES, TILES, tile_start_ref, query_code_ref, kvq_ref, g_ref, out_ref, stat_ref, store,
        key_flat, key_turned, value_flat, key_sum, value_sum
    )
    for n, (sums, factor) in enumerate(((key_sum, SCALE), (value_sum, 1.0))):
        for chunk in chunks:
            piece = sums[:, chunk * CHUNK : (chunk + 1) * CHUNK] * factor
            grads_ref[chunk - HALO, n] = piece.astype(BF16)
            if chunk >= CHUNKS:
                rest_ref[chunk - CHUNKS, n] = piece


def sums_scratch(window):
    return [
        pltpu.VMEM((window, WIDE), BF16),
        pltpu.VMEM((HEAD_DIM, window), BF16),
        pltpu.VMEM((window, WIDE), BF16),
        pltpu.VMEM((HEAD_DIM, window), F32),
        pltpu.VMEM((HEAD_DIM, window), F32),
    ]


def early_backward(tile_start, codes, kvq, halo, g, out, stat):
    def part(count, width):
        return pl.BlockSpec((count, width, HEAD_DIM, CHUNK), lambda b: (0, 0, 0, 0))

    return pl.pallas_call(
        early_backward_kernel,
        grid=(1,),
        in_specs=[smem(), vmem(), vmem(), part(HALO, 3), vmem(), part(HALO, 1), part(HALO, 1), vmem()],
        out_specs=[vmem()] * 3,
        out_shape=[
            jax.ShapeDtypeStruct((HALO, 2, HEAD_DIM, CHUNK), BF16),
            jax.ShapeDtypeStruct((2, HEAD_DIM, AHEAD), F32),
            jax.ShapeDtypeStruct((HALO, HEAD_DIM, CHUNK), BF16),
        ],
        scratch_shapes=sums_scratch(2 * AHEAD),
        compiler_params=pltpu.CompilerParams(vmem_limit_bytes=16 * MIB),
        cost_estimate=cost(5, AHEAD_TILES),
        name="early_backward",
    )(tile_start, *codes, kvq, halo, g, out, stat)


def late_backward(tile_start, codes, kvq, g, out, stat, carry, grad_q):
    return pl.pallas_call(
        late_backward_kernel,
        in_specs=[smem()] + [vmem()] * 8,
        out_specs=[vmem()] * 2,
        out_shape=[
            jax.ShapeDtypeStruct((CHUNKS, 3, HEAD_DIM, CHUNK), BF16),
            jax.ShapeDtypeStruct((HALO, 2, HEAD_DIM, CHUNK), F32),
        ],
        scratch_shapes=sums_scratch(WINDOW),
        compiler_params=pltpu.CompilerParams(vmem_limit_bytes=28 * MIB),
        cost_estimate=cost(5, TILES - AHEAD_TILES),
        name="late_backward",
    )(tile_start, *codes, kvq, g, out, stat, carry, grad_q)


def join_kernel(back_ref, rest_ref, _, out_ref):
    out_ref[...] = (rest_ref[...] + back_ref[...].astype(F32)).astype(BF16)


def join(back, rest, grads):
    whole = (HALO, 2, HEAD_DIM, CHUNK)
    return pl.pallas_call(
        join_kernel,
        grid=(1,),
        in_specs=[
            pl.BlockSpec(whole, lambda i: (0, 0, 0, 0)),
            pl.BlockSpec(whole, lambda i: (0, 0, 0, 0)),
            pl.BlockSpec(memory_space=pl.ANY),
        ],
        out_specs=pl.BlockSpec(whole, lambda i: (CHUNKS // HALO - 1, 0, 0, 0)),
        out_shape=jax.ShapeDtypeStruct(grads.shape, BF16),
        input_output_aliases={2: 0},
        compiler_params=pltpu.CompilerParams(vmem_limit_bytes=6 * MIB),
        name="join",
    )(back, rest, grads)


def gate_kernel(_, __, ___):
    pass


def after(array, other):
    return pl.pallas_call(
        gate_kernel,
        in_specs=[pl.BlockSpec(memory_space=pl.ANY)] * 2,
        out_specs=pl.BlockSpec(memory_space=pl.ANY),
        out_shape=jax.ShapeDtypeStruct(array.shape, array.dtype),
        input_output_aliases={0: 0},
        name="after",
    )(array, other)


def group_pairs():
    def index(x, zh, y, zl, c):
        return (((x * 2 + zh) * 4 + y) * 4 + zl) * 2 + c

    pairs = []
    for group in range(7):
        for y in range(4):
            for zl in range(4):
                for c in range(2):
                    pairs.append(
                        (
                            index(group // 2, group % 2, y, zl, c),
                            index((group + 1) // 2, (group + 1) % 2, y, 3 - zl, c),
                        )
                    )
    return pairs


def to_heads(array):
    return lax.all_to_all(array, GROUP_AXES, split_axis=0, concat_axis=0, tiled=True)


def places(doc_ids):
    group = lax.axis_index("x") * 2 + lax.axis_index("zh")
    own = lax.dynamic_slice_in_dim(doc_ids, group * GROUP, GROUP)
    ahead = lax.dynamic_slice_in_dim(doc_ids, jnp.maximum(group * GROUP - AHEAD, 0), AHEAD)
    ahead = jnp.where(group > 0, ahead, -1)
    docs = jnp.concatenate([ahead, own])
    leads = own.reshape(TILES, TILE)[:, :1]
    tile_start = jnp.sum((docs[None] < leads).astype(jnp.int32), 1) // TILE
    row = jnp.arange(EXTRA, dtype=jnp.int32)[:, None]
    bits = (docs[None] >> (row // 2)) & 1
    coded = row < 2 * DOC_BITS
    differs = (bits != row % 2) | (docs[None] < 0)
    key_code = jnp.where(coded, jnp.where(differs, -FAR, 0.0), jnp.where(row < 15, -1.0, 0.0))
    query_code = jnp.where(coded & (bits[:, AHEAD:] == row % 2), 1.0, 0.0)
    query_code = query_code.reshape(EXTRA, TILES, TILE).transpose(1, 0, 2)
    return tile_start, (key_code.astype(BF16), query_code.astype(BF16))


def shards(queries, keys, values, cotangent, doc_ids):
    mirror = lax.axis_index("zh").astype(jnp.int32).reshape(1)
    kvq = to_heads(pack(mirror, keys, values, queries))
    tile_start, codes = places(doc_ids)
    cotangent, tile_start, codes = lax.optimization_barrier((cotangent, tile_start, codes))
    pairs = group_pairs()
    last = kvq[CHUNKS - HALO :, :2]
    halo = lax.ppermute(last, AXES, pairs)
    g = to_heads(after(pack(mirror, cotangent), last))
    out, stat = late_forward(tile_start, codes, kvq)
    out, stat = early_forward(tile_start, codes, kvq, halo, out, stat)
    back, carry, early_q = early_backward(tile_start, codes, kvq, halo, g, out, stat)
    grads, rest = late_backward(tile_start, codes, kvq, g, out, stat, carry, early_q)
    back = lax.ppermute(back, AXES, [(b, a) for a, b in pairs])
    grads = join(back, rest, grads)
    (attended,) = unpack(mirror, to_heads(out))
    grad_k, grad_v, grad_q = unpack(mirror, to_heads(grads))
    return attended, grad_q, grad_k, grad_v


def solution(mesh):
    wide = Mesh(mesh.devices.reshape(4, 2, 4, 4, 2), AXES)
    rows = P(AXES, None)
    return jax.shard_map(
        shards,
        mesh=wide,
        in_specs=(rows, rows, rows, rows, P()),
        out_specs=(rows, rows, rows, rows),
        check_vma=False,
    )
```

```python
import functools
import math

import jax
import jax.numpy as jnp
from jax import lax
from jax.experimental import pallas as pl
from jax.experimental.pallas import tpu as pltpu
from jax.sharding import Mesh
from jax.sharding import PartitionSpec as P

HEAD_DIM = 96
HEADS = 32
CHUNK = 128
CHUNKS = 32
HALO = 8
DOC_BITS = 6
EXTRA = 16
WIDE = HEAD_DIM + EXTRA
FAR = 2.0**20
GROUP = CHUNK * CHUNKS
AHEAD = CHUNK * HALO
WINDOW = GROUP + AHEAD
TILE = 256
TILES = GROUP // TILE
BLOCKS = CHUNKS // HALO
AHEAD_TILES = AHEAD // TILE
REACH = AHEAD_TILES + 1
NEG = -1e30
SCALE = 1.0 / math.sqrt(HEAD_DIM)
LOG2E = 1.4426950408889634
MIB = 1024 * 1024

AXES = ("x", "zh", "y", "zl", "c")
GROUP_AXES = ("y", "zl", "c")
F32 = jnp.float32
BF16 = jnp.bfloat16


def vmem():
    return pl.BlockSpec(memory_space=pltpu.VMEM)


def smem():
    return pl.BlockSpec(memory_space=pltpu.SMEM)


def hbm():
    return pl.BlockSpec(memory_space=pltpu.HBM)


def in_hbm(*arrays):
    return [pltpu.with_memory_space_constraint(array, pltpu.HBM) for array in arrays]


def pack_kernel(mirror_ref, *refs):
    count = len(refs) - 5
    sources, (out_ref, rows, blocks, arrived, sent) = refs[:count], refs[count:]
    mirrored = mirror_ref[0]

    def fetch(y, n):
        return pltpu.make_async_copy(
            sources[n].at[:, pl.ds(y * 768, 768)], rows.at[n, y], arrived.at[n, y]
        )

    def send(y):
        part = pl.ds(y * 8, 8)
        return pltpu.make_async_copy(blocks.at[part], out_ref.at[part], sent.at[y])

    for y in range(4):
        for n in range(count):
            fetch(y, n).start()
    for y in range(4):
        for n in range(count):
            fetch(y, n).wait()
            turned = rows[n, y].T
            for zl in range(4):
                slot = 8 * y + 2 * jnp.where(mirrored == 1, 3 - zl, zl)
                piece = turned[zl * 192 : (zl + 1) * 192]
                blocks[pl.ds(slot, 2), n] = piece.reshape(2, HEAD_DIM, CHUNK)
        send(y).start()
    for y in range(4):
        send(y).wait()


def pack(mirror, *arrays):
    count = len(arrays)
    shape = (HEADS, count, HEAD_DIM, CHUNK)
    return pl.pallas_call(
        pack_kernel,
        in_specs=[smem()] + [hbm()] * count,
        out_specs=hbm(),
        out_shape=pltpu.HBM(shape, BF16),
        scratch_shapes=[
            pltpu.VMEM((count, 4, CHUNK, 768), BF16),
            pltpu.VMEM(shape, BF16),
            pltpu.SemaphoreType.DMA((count, 4)),
            pltpu.SemaphoreType.DMA((4,)),
        ],
        compiler_params=pltpu.CompilerParams(vmem_limit_bytes=40 * MIB),
        name="pack",
    )(mirror, *in_hbm(*arrays))


def unpack_kernel(mirror_ref, in_ref, *out_refs):
    mirrored = mirror_ref[0]
    for n, out_ref in enumerate(out_refs):
        pieces = []
        for zl in range(4):
            slot = 2 * jnp.where(mirrored == 1, 3 - zl, zl)
            pieces.append(in_ref[pl.ds(slot, 2), n].reshape(192, CHUNK))
        out_ref[...] = jnp.concatenate(pieces, 0).T


def unpack(mirror, array):
    count = array.shape[1]
    return pl.pallas_call(
        unpack_kernel,
        grid=(4,),
        in_specs=[
            smem(),
            pl.BlockSpec((8, count, HEAD_DIM, CHUNK), lambda y: (y, 0, 0, 0)),
        ],
        out_specs=[pl.BlockSpec((CHUNK, 768), lambda y: (0, y))] * count,
        out_shape=[jax.ShapeDtypeStruct((CHUNK, HEADS * HEAD_DIM), BF16)] * count,
        compiler_params=pltpu.CompilerParams(vmem_limit_bytes=28 * MIB),
        name="unpack",
    )(mirror, array)


def tile_of(ref, n, i):
    return jnp.concatenate([ref[2 * i, n], ref[2 * i + 1, n]], 1)


def nn(a, b):
    return lax.dot_general(a, b, (((1,), (0,)), ((), ())), preferred_element_type=F32)


def nt(a, b):
    return lax.dot_general(a, b, (((1,), (1,)), ((), ())), preferred_element_type=F32)


def each_chunk(halo_ref, own_ref, n, chunks):
    for chunk in chunks:
        if isinstance(chunk, int) and chunk < HALO:
            piece = halo_ref[chunk, n]
        else:
            piece = own_ref[chunk - HALO, n]
        if isinstance(chunk, int):
            first = chunk * CHUNK
        else:
            first = pl.multiple_of(chunk * CHUNK, CHUNK)
        yield pl.ds(first, CHUNK), piece


def fill_keys(halo_ref, own_ref, code_ref, chunks, flat, turned):
    for span, piece in each_chunk(halo_ref, own_ref, 0, chunks):
        flat[span, :] = jnp.concatenate([piece, code_ref[:, span]], 0).T
        if turned is not None:
            turned[:, span] = piece


def fill_value_rows(halo_ref, own_ref, chunks, flat):
    row = lax.broadcasted_iota(jnp.int32, (EXTRA, CHUNK), 0)
    minus = jnp.where(row < 3, -1.0, 0.0).astype(BF16)
    for span, piece in each_chunk(halo_ref, own_ref, 1, chunks):
        flat[span, :] = jnp.concatenate([piece, minus], 0).T


def fill_value_columns(halo_ref, own_ref, chunks, turned):
    for span, piece in each_chunk(halo_ref, own_ref, 1, chunks):
        turned[:HEAD_DIM, span] = piece
        turned[HEAD_DIM:, span] = jnp.ones((EXTRA, CHUNK), BF16)


def with_row(extra, first, value):
    high = value.astype(BF16).astype(F32)
    middle = (value - high).astype(BF16).astype(F32)
    low = value - high - middle
    row = lax.broadcasted_iota(jnp.int32, (EXTRA, TILE), 0)
    for n, part in enumerate((high, middle, low)):
        extra = jnp.where(row == first + n, part, extra)
    return extra.astype(BF16)


def causal():
    row = lax.broadcasted_iota(jnp.int32, (TILE, TILE), 0)
    return row <= lax.broadcasted_iota(jnp.int32, (TILE, TILE), 1)


def per_tile(tile_start_ref, i, body):
    reach = jnp.clip(i + REACH - tile_start_ref[i], 1, REACH)
    for count in range(1, REACH + 1):
        pl.when(reach == count)(functools.partial(body, count))


def send_block(buffer, out_ref, sent, block):
    part = pl.ds(block * HALO, HALO)
    return pltpu.make_async_copy(buffer.at[part], out_ref.at[part], sent.at[block])


def forward_tiles(
    block, tile_start_ref, query_code_ref, kvq_ref, store, stat_ref, key_flat, value_turned
):
    def tile(step, _):
        i = block * AHEAD_TILES + step

        def body(count):
            q = jnp.concatenate([tile_of(kvq_ref, 2, i), query_code_ref[i]], 0)
            scores = []
            top = None
            for j in range(count):
                first = pl.multiple_of((i + REACH - count + j) * TILE, TILE)
                s = nn(key_flat[pl.ds(first, TILE), :], q)
                if j == count - 1:
                    s = jnp.where(causal(), s, NEG)
                scores.append(s)
                t = jnp.max(s, axis=0, keepdims=True)
                top = t if top is None else jnp.maximum(top, t)
            shift = top * (SCALE * LOG2E)
            out = None
            for j in range(count):
                first = pl.multiple_of((i + REACH - count + j) * TILE, TILE)
                e = jnp.exp2(scores[j] * (SCALE * LOG2E) - shift)
                o = nn(value_turned[:, pl.ds(first, TILE)], e.astype(BF16))
                out = o if out is None else out + o
            total = out[HEAD_DIM : HEAD_DIM + 1]
            out = (out[:HEAD_DIM] / total).astype(BF16)
            store(2 * i, out[:, :CHUNK])
            store(2 * i + 1, out[:, CHUNK:])
            stat_ref[i] = top + jnp.log(total) * (1.0 / SCALE)

        per_tile(tile_start_ref, i, body)
        return 0

    lax.fori_loop(0, AHEAD_TILES, tile, 0)


def late_forward_kernel(
    tile_start_ref, key_code_ref, query_code_ref, kvq_ref, out_ref, stat_ref,
    key_flat, value_turned, buffer, sent
):
    chunks = range(HALO, HALO + CHUNKS)
    fill_keys(None, kvq_ref, key_code_ref, chunks, key_flat, None)
    fill_value_columns(None, kvq_ref, chunks, value_turned)

    def store(chunk, value):
        buffer[chunk, 0] = value

    def block(b, _):
        forward_tiles(
            b, tile_start_ref, query_code_ref, kvq_ref, store, stat_ref, key_flat, value_turned
        )
        send_block(buffer, out_ref, sent, b).start()
        return 0

    lax.fori_loop(1, BLOCKS, block, 0)
    for b in range(1, BLOCKS):
        send_block(buffer, out_ref, sent, b).wait()


def cost(time):
    return pl.CostEstimate(flops=int(time * 1.1e9), bytes_accessed=0, transcendentals=0)


OUT_SHAPE = pltpu.HBM((CHUNKS, 1, HEAD_DIM, CHUNK), BF16)


def part(count, width):
    return pl.BlockSpec((count, width, HEAD_DIM, CHUNK), lambda b: (0, 0, 0, 0))


def forward_scratch(window, chunks):
    return [
        pltpu.VMEM((window, WIDE), BF16),
        pltpu.VMEM((WIDE, window), BF16),
        pltpu.VMEM((chunks, 1, HEAD_DIM, CHUNK), BF16),
        pltpu.SemaphoreType.DMA((BLOCKS,)),
    ]


def late_forward(tile_start, codes, kvq):
    return pl.pallas_call(
        late_forward_kernel,
        in_specs=[smem(), vmem(), vmem(), vmem()],
        out_specs=[hbm(), vmem()],
        out_shape=[OUT_SHAPE, jax.ShapeDtypeStruct((TILES, 1, TILE), F32)],
        scratch_shapes=forward_scratch(WINDOW, CHUNKS),
        compiler_params=pltpu.CompilerParams(vmem_limit_bytes=40 * MIB),
        cost_estimate=cost(30),
        name="late_forward",
    )(tile_start, *codes, kvq)


def backward_tiles(
    low, high, tile_start_ref, query_code_ref, kvq_ref, g_ref, out_ref, stat_ref, store,
    key_flat, key_turned, value_flat, key_sum, value_sum
):
    def tile(i, _):
        def body(count):
            q = tile_of(kvq_ref, 2, i)
            g = tile_of(g_ref, 0, i)
            o = tile_of(out_ref, 0, i)
            delta = jnp.sum(o.astype(F32) * g.astype(F32), axis=0, keepdims=True)
            stat = stat_ref[i]
            code = query_code_ref[i].astype(F32)
            q_wide = jnp.concatenate([q, with_row(code, 2 * DOC_BITS, stat)], 0)
            g_wide = jnp.concatenate([g, with_row(jnp.zeros_like(code), 0, delta)], 0)
            grad_q = None
            for j in range(count):
                first = pl.multiple_of((i + REACH - count + j) * TILE, TILE)
                span = pl.ds(first, TILE)
                p = jnp.exp2(nn(key_flat[span, :], q_wide) * (SCALE * LOG2E))
                if j == count - 1:
                    p = jnp.where(causal(), p, 0.0)
                d = (p * nn(value_flat[span, :], g_wide)).astype(BF16)
                t = nn(key_turned[:, span], d)
                grad_q = t if grad_q is None else grad_q + t
                key_sum[:, span] += nt(q, d)
                value_sum[:, span] += nt(g, p.astype(BF16))
            grad_q = (grad_q * SCALE).astype(BF16)
            store(2 * i, grad_q[:, :CHUNK])
            store(2 * i + 1, grad_q[:, CHUNK:])

        per_tile(tile_start_ref, i, body)
        return 0

    lax.fori_loop(low, high, tile, 0)


def early_forward_kernel(
    tile_start_ref, key_code_ref, query_code_ref, kvq_ref, halo_ref, _, out_ref, stat_ref,
    key_flat, value_turned, buffer, sent
):
    fill_keys(halo_ref, kvq_ref, key_code_ref, range(2 * HALO), key_flat, None)
    fill_value_columns(halo_ref, kvq_ref, range(2 * HALO), value_turned)

    def store(chunk, value):
        buffer[chunk, 0] = value

    forward_tiles(
        0, tile_start_ref, query_code_ref, kvq_ref, store, stat_ref, key_flat, value_turned
    )
    copy = send_block(buffer, out_ref, sent, 0)
    copy.start()
    copy.wait()


def early_backward_kernel(
    tile_start_ref, key_code_ref, query_code_ref, kvq_ref, halo_ref, g_ref, out_ref, stat_ref,
    back_ref, carry_ref, grad_q_ref,
    key_flat, key_turned, value_flat, key_sum, value_sum, g_part, out_part, back_part, grad_q_part,
    sent
):
    fetches = [
        pltpu.make_async_copy(source.at[pl.ds(0, HALO)], target, sent.at[n])
        for n, (source, target) in enumerate(((g_ref, g_part), (out_ref, out_part)))
    ]
    for copy in fetches:
        copy.start()
    fill_keys(halo_ref, kvq_ref, key_code_ref, range(2 * HALO), key_flat, key_turned)
    fill_value_rows(halo_ref, kvq_ref, range(2 * HALO), value_flat)
    key_sum[...] = jnp.zeros_like(key_sum)
    value_sum[...] = jnp.zeros_like(value_sum)
    for copy in fetches:
        copy.wait()

    def store(chunk, value):
        grad_q_part[chunk] = value

    backward_tiles(
        0, AHEAD_TILES, tile_start_ref, query_code_ref, kvq_ref, g_part, out_part, stat_ref, store,
        key_flat, key_turned, value_flat, key_sum, value_sum
    )
    copies = [pltpu.make_async_copy(grad_q_part, grad_q_ref, sent.at[2])]
    for n, sums in enumerate((key_sum, value_sum)):
        copies.append(
            pltpu.make_async_copy(
                sums.at[:, pl.ds(AHEAD, AHEAD)], carry_ref.at[n], sent.at[3 + n]
            )
        )
    for copy in copies:
        copy.start()
    for n, (sums, factor) in enumerate(((key_sum, SCALE), (value_sum, 1.0))):
        for chunk in range(HALO):
            piece = sums[:, chunk * CHUNK : (chunk + 1) * CHUNK] * factor
            back_part[chunk, n] = piece.astype(BF16)
    back_copy = pltpu.make_async_copy(back_part, back_ref, sent.at[5])
    back_copy.start()
    for copy in (*copies, back_copy):
        copy.wait()


def late_backward_kernel(
    tile_start_ref, key_code_ref, query_code_ref, kvq_ref, g_ref, out_ref, stat_ref, carry_ref,
    grad_q_ref, grads_ref, rest_ref,
    key_flat, key_turned, value_flat, key_sum, value_sum, buffer, g_all, out_all,
    sent, fetched
):
    later = pl.ds(HALO, CHUNKS - HALO)
    early = pl.ds(AHEAD, AHEAD)
    fetches = [
        pltpu.make_async_copy(source, target, fetched.at[n])
        for n, (source, target) in enumerate(
            (
                (g_ref.at[later], g_all.at[later]),
                (out_ref.at[later], out_all.at[later]),
                (carry_ref.at[0], key_sum.at[:, early]),
                (carry_ref.at[1], value_sum.at[:, early]),
                (grad_q_ref, buffer.at[pl.ds(0, HALO), 2]),
            )
        )
    ]
    for copy in fetches:
        copy.start()

    def fill(b):
        chunks = [(b + 1) * HALO + n for n in range(HALO)]
        fill_keys(None, kvq_ref, key_code_ref, chunks, key_flat, key_turned)
        fill_value_rows(None, kvq_ref, chunks, value_flat)

    fill(0)
    for sums in (key_sum, value_sum):
        sums[:, 2 * AHEAD :] = jnp.zeros((HEAD_DIM, WINDOW - 2 * AHEAD), F32)
    for copy in fetches:
        copy.wait()

    def store(chunk, value):
        buffer[chunk, 2] = value

    def block(b, _):
        fill(b)
        backward_tiles(
            b * AHEAD_TILES, (b + 1) * AHEAD_TILES,
            tile_start_ref, query_code_ref, kvq_ref, g_all, out_all, stat_ref, store,
            key_flat, key_turned, value_flat, key_sum, value_sum
        )
        for n, (sums, factor) in enumerate(((key_sum, SCALE), (value_sum, 1.0))):
            for chunk in range(HALO):
                first = pl.multiple_of(b * AHEAD + chunk * CHUNK, CHUNK)
                piece = sums[:, pl.ds(first, CHUNK)] * factor
                buffer[(b - 1) * HALO + chunk, n] = piece.astype(BF16)
        send_block(buffer, grads_ref, sent, b - 1).start()
        return 0

    lax.fori_loop(1, BLOCKS, block, 0)
    part = (pl.ds(CHUNKS - HALO, HALO), pl.ds(2, 1))
    last = pltpu.make_async_copy(buffer.at[part], grads_ref.at[part], sent.at[BLOCKS - 1])
    last.start()
    for n, sums in enumerate((key_sum, value_sum)):
        rest_ref[n] = sums[:, GROUP:]
    for b in range(BLOCKS - 1):
        send_block(buffer, grads_ref, sent, b).wait()
    last.wait()


def sums_scratch(window):
    return [
        pltpu.VMEM((window, WIDE), BF16),
        pltpu.VMEM((HEAD_DIM, window), BF16),
        pltpu.VMEM((window, WIDE), BF16),
        pltpu.VMEM((HEAD_DIM, window), F32),
        pltpu.VMEM((HEAD_DIM, window), F32),
    ]


def early_forward(tile_start, codes, kvq, halo, out):
    return pl.pallas_call(
        early_forward_kernel,
        grid=(1,),
        in_specs=[smem(), vmem(), vmem(), part(HALO, 3), vmem(), hbm()],
        out_specs=[hbm(), vmem()],
        out_shape=[OUT_SHAPE, jax.ShapeDtypeStruct((AHEAD_TILES, 1, TILE), F32)],
        input_output_aliases={5: 0},
        scratch_shapes=forward_scratch(2 * AHEAD, HALO),
        compiler_params=pltpu.CompilerParams(vmem_limit_bytes=40 * MIB),
        cost_estimate=cost(1),
        name="early_forward",
    )(tile_start, *codes, kvq, halo, *in_hbm(out))


def early_backward(tile_start, codes, kvq, halo, g, out, stat):
    return pl.pallas_call(
        early_backward_kernel,
        grid=(1,),
        in_specs=[smem(), vmem(), vmem(), part(HALO, 3), vmem(), hbm(), hbm(), vmem()],
        out_specs=[hbm()] * 3,
        out_shape=[
            pltpu.HBM((HALO, 2, HEAD_DIM, CHUNK), BF16),
            pltpu.HBM((2, HEAD_DIM, AHEAD), F32),
            pltpu.HBM((HALO, HEAD_DIM, CHUNK), BF16),
        ],
        scratch_shapes=sums_scratch(2 * AHEAD)
        + [
            pltpu.VMEM((HALO, 1, HEAD_DIM, CHUNK), BF16),
            pltpu.VMEM((HALO, 1, HEAD_DIM, CHUNK), BF16),
            pltpu.VMEM((HALO, 2, HEAD_DIM, CHUNK), BF16),
            pltpu.VMEM((HALO, HEAD_DIM, CHUNK), BF16),
            pltpu.SemaphoreType.DMA((6,)),
        ],
        compiler_params=pltpu.CompilerParams(vmem_limit_bytes=40 * MIB),
        cost_estimate=cost(1),
        name="early_backward",
    )(tile_start, *codes, kvq, halo, *in_hbm(g, out), stat)


def late_backward(tile_start, codes, kvq, g, out, stat, carry, grad_q):
    return pl.pallas_call(
        late_backward_kernel,
        in_specs=[smem(), vmem(), vmem(), vmem(), hbm(), hbm(), vmem(), hbm(), hbm()],
        out_specs=[hbm(), vmem()],
        out_shape=[
            pltpu.HBM((CHUNKS, 3, HEAD_DIM, CHUNK), BF16),
            jax.ShapeDtypeStruct((2, HEAD_DIM, AHEAD), F32),
        ],
        scratch_shapes=sums_scratch(WINDOW)
        + [
            pltpu.VMEM((CHUNKS, 3, HEAD_DIM, CHUNK), BF16),
            pltpu.VMEM((CHUNKS, 1, HEAD_DIM, CHUNK), BF16),
            pltpu.VMEM((CHUNKS, 1, HEAD_DIM, CHUNK), BF16),
            pltpu.SemaphoreType.DMA((BLOCKS,)),
            pltpu.SemaphoreType.DMA((5,)),
        ],
        compiler_params=pltpu.CompilerParams(vmem_limit_bytes=40 * MIB),
        cost_estimate=cost(10),
        name="late_backward",
    )(tile_start, *codes, kvq, *in_hbm(g, out), stat, *in_hbm(carry, grad_q))


def join_kernel(back_ref, rest_ref, _, out_ref, buffer, moved):
    sends = []
    for n, factor in enumerate((SCALE, 1.0)):
        for chunk in range(HALO):
            own = rest_ref[n, :, chunk * CHUNK : (chunk + 1) * CHUNK] * factor
            buffer[chunk, n] = (own + back_ref[chunk, n].astype(F32)).astype(BF16)
        target = out_ref.at[pl.ds(CHUNKS - HALO, HALO), n]
        sends.append(pltpu.make_async_copy(buffer.at[:, n], target, moved.at[n]))
        sends[n].start()
    for copy in sends:
        copy.wait()


def join(back, rest, grads):
    return pl.pallas_call(
        join_kernel,
        in_specs=[vmem(), vmem(), hbm()],
        out_specs=hbm(),
        out_shape=pltpu.HBM(grads.shape, BF16),
        input_output_aliases={2: 0},
        scratch_shapes=[
            pltpu.VMEM((HALO, 2, HEAD_DIM, CHUNK), BF16),
            pltpu.SemaphoreType.DMA((2,)),
        ],
        compiler_params=pltpu.CompilerParams(vmem_limit_bytes=40 * MIB),
        name="join",
    )(back, rest, *in_hbm(grads))


def gate_kernel(_, __, ___):
    pass


def after(array, other):
    return pl.pallas_call(
        gate_kernel,
        in_specs=[hbm(), pl.BlockSpec(memory_space=pl.ANY)],
        out_specs=hbm(),
        out_shape=pltpu.HBM(array.shape, array.dtype),
        input_output_aliases={0: 0},
        name="after",
    )(array, other)


def group_pairs():
    def index(x, zh, y, zl, c):
        return (((x * 2 + zh) * 4 + y) * 4 + zl) * 2 + c

    pairs = []
    for group in range(7):
        for y in range(4):
            for zl in range(4):
                for c in range(2):
                    pairs.append(
                        (
                            index(group // 2, group % 2, y, zl, c),
                            index((group + 1) // 2, (group + 1) % 2, y, 3 - zl, c),
                        )
                    )
    return pairs


def to_heads(array):
    return lax.all_to_all(array, GROUP_AXES, split_axis=0, concat_axis=0, tiled=True)


def places(doc_ids):
    group = lax.axis_index("x") * 2 + lax.axis_index("zh")
    own = lax.dynamic_slice_in_dim(doc_ids, group * GROUP, GROUP)
    ahead = lax.dynamic_slice_in_dim(doc_ids, jnp.maximum(group * GROUP - AHEAD, 0), AHEAD)
    ahead = jnp.where(group > 0, ahead, -1)
    docs = jnp.concatenate([ahead, own])
    leads = own.reshape(TILES, TILE)[:, :1]
    tile_start = jnp.sum((docs[None] < leads).astype(jnp.int32), 1) // TILE
    row = jnp.arange(EXTRA, dtype=jnp.int32)[:, None]
    bits = (docs[None] >> (row // 2)) & 1
    coded = row < 2 * DOC_BITS
    differs = (bits != row % 2) | (docs[None] < 0)
    key_code = jnp.where(coded, jnp.where(differs, -FAR, 0.0), jnp.where(row < 15, -1.0, 0.0))
    query_code = jnp.where(coded & (bits[:, AHEAD:] == row % 2), 1.0, 0.0)
    query_code = query_code.reshape(EXTRA, TILES, TILE).transpose(1, 0, 2)
    return tile_start, (key_code.astype(BF16), query_code.astype(BF16))


def shards(queries, keys, values, cotangent, doc_ids):
    mirror = lax.axis_index("zh").astype(jnp.int32).reshape(1)
    kvq = to_heads(pack(mirror, keys, values, queries))
    tile_start, codes = places(doc_ids)
    cotangent, tile_start, codes = lax.optimization_barrier((cotangent, tile_start, codes))
    pairs = group_pairs()
    last = kvq[CHUNKS - HALO :, :2]
    halo = lax.ppermute(last, AXES, pairs)
    g = to_heads(after(pack(mirror, cotangent), last))
    out, stat = late_forward(tile_start, codes, kvq)
    out, early_stat = early_forward(tile_start, codes, kvq, halo, out)
    back, carry, early_q = early_backward(tile_start, codes, kvq, halo, g, out, early_stat)
    grads, rest = late_backward(tile_start, codes, kvq, g, out, stat, carry, early_q)
    back = lax.ppermute(back, AXES, [(b, a) for a, b in pairs])
    grads = join(back, rest, grads)
    (attended,) = unpack(mirror, to_heads(out))
    grad_k, grad_v, grad_q = unpack(mirror, to_heads(grads))
    return attended, grad_q, grad_k, grad_v


def solution(mesh):
    wide = Mesh(mesh.devices.reshape(4, 2, 4, 4, 2), AXES)
    rows = P(AXES, None)
    return jax.shard_map(
        shards,
        mesh=wide,
        in_specs=(rows, rows, rows, rows, P()),
        out_specs=(rows, rows, rows, rows),
        check_vma=False,
    )
```

```python
import functools
import math

import jax
import jax.numpy as jnp
from jax import lax
from jax.experimental import pallas as pl
from jax.experimental.pallas import tpu as pltpu
from jax.sharding import Mesh
from jax.sharding import PartitionSpec as P

HEAD_DIM = 96
HEADS = 32
CHUNK = 128
CHUNKS = 32
HALO = 8
DOC_BITS = 6
EXTRA = 16
WIDE = HEAD_DIM + EXTRA
FAR = 2.0**20
GROUP = CHUNK * CHUNKS
AHEAD = CHUNK * HALO
WINDOW = GROUP + AHEAD
TILE = 256
TILES = GROUP // TILE
BLOCKS = CHUNKS // HALO
AHEAD_TILES = AHEAD // TILE
REACH = AHEAD_TILES + 1
NEG = -1e30
SCALE = 1.0 / math.sqrt(HEAD_DIM)
LOG2E = 1.4426950408889634
MIB = 1024 * 1024

AXES = ("x", "zh", "y", "zl", "c")
GROUP_AXES = ("y", "zl", "c")
F32 = jnp.float32
BF16 = jnp.bfloat16


def vmem():
    return pl.BlockSpec(memory_space=pltpu.VMEM)


def smem():
    return pl.BlockSpec(memory_space=pltpu.SMEM)


def hbm():
    return pl.BlockSpec(memory_space=pltpu.HBM)


def in_hbm(*arrays):
    return [pltpu.with_memory_space_constraint(array, pltpu.HBM) for array in arrays]


def pack_kernel(mirror_ref, *refs):
    count = len(refs) - 5
    sources, (out_ref, rows, blocks, arrived, sent) = refs[:count], refs[count:]
    mirrored = mirror_ref[0]

    def fetch(y, n):
        return pltpu.make_async_copy(
            sources[n].at[:, pl.ds(y * 768, 768)], rows.at[n, y], arrived.at[n, y]
        )

    def send(y):
        part = pl.ds(y * 8, 8)
        return pltpu.make_async_copy(blocks.at[part], out_ref.at[part], sent.at[y])

    for y in range(4):
        for n in range(count):
            fetch(y, n).start()
    for y in range(4):
        for n in range(count):
            fetch(y, n).wait()
            turned = rows[n, y].T
            for zl in range(4):
                slot = 8 * y + 2 * jnp.where(mirrored == 1, 3 - zl, zl)
                piece = turned[zl * 192 : (zl + 1) * 192]
                blocks[pl.ds(slot, 2), n] = piece.reshape(2, HEAD_DIM, CHUNK)
        send(y).start()
    for y in range(4):
        send(y).wait()


def pack(mirror, *arrays):
    count = len(arrays)
    shape = (HEADS, count, HEAD_DIM, CHUNK)
    return pl.pallas_call(
        pack_kernel,
        in_specs=[smem()] + [hbm()] * count,
        out_specs=hbm(),
        out_shape=pltpu.HBM(shape, BF16),
        scratch_shapes=[
            pltpu.VMEM((count, 4, CHUNK, 768), BF16),
            pltpu.VMEM(shape, BF16),
            pltpu.SemaphoreType.DMA((count, 4)),
            pltpu.SemaphoreType.DMA((4,)),
        ],
        compiler_params=pltpu.CompilerParams(vmem_limit_bytes=40 * MIB),
        name="pack",
    )(mirror, *in_hbm(*arrays))


def unpack_kernel(mirror_ref, in_ref, *out_refs):
    mirrored = mirror_ref[0]
    for n, out_ref in enumerate(out_refs):
        pieces = []
        for zl in range(4):
            slot = 2 * jnp.where(mirrored == 1, 3 - zl, zl)
            pieces.append(in_ref[pl.ds(slot, 2), n].reshape(192, CHUNK))
        out_ref[...] = jnp.concatenate(pieces, 0).T


def unpack(mirror, array):
    count = array.shape[1]
    return pl.pallas_call(
        unpack_kernel,
        grid=(4,),
        in_specs=[
            smem(),
            pl.BlockSpec((8, count, HEAD_DIM, CHUNK), lambda y: (y, 0, 0, 0)),
        ],
        out_specs=[pl.BlockSpec((CHUNK, 768), lambda y: (0, y))] * count,
        out_shape=[jax.ShapeDtypeStruct((CHUNK, HEADS * HEAD_DIM), BF16)] * count,
        compiler_params=pltpu.CompilerParams(vmem_limit_bytes=28 * MIB),
        name="unpack",
    )(mirror, array)


def tile_of(ref, n, i):
    return jnp.concatenate([ref[2 * i, n], ref[2 * i + 1, n]], 1)


def nn(a, b):
    return lax.dot_general(a, b, (((1,), (0,)), ((), ())), preferred_element_type=F32)


def nt(a, b):
    return lax.dot_general(a, b, (((1,), (1,)), ((), ())), preferred_element_type=F32)


def each_chunk(halo_ref, own_ref, n, chunks):
    for chunk in chunks:
        piece = halo_ref[chunk, n] if chunk < HALO else own_ref[chunk - HALO, n]
        yield slice(chunk * CHUNK, (chunk + 1) * CHUNK), piece


def fill_keys(halo_ref, own_ref, code_ref, chunks, flat, turned):
    for span, piece in each_chunk(halo_ref, own_ref, 0, chunks):
        flat[span, :] = jnp.concatenate([piece, code_ref[:, span]], 0).T
        if turned is not None:
            turned[:, span] = piece


def fill_value_rows(halo_ref, own_ref, chunks, flat):
    row = lax.broadcasted_iota(jnp.int32, (EXTRA, CHUNK), 0)
    minus = jnp.where(row < 3, -1.0, 0.0).astype(BF16)
    for span, piece in each_chunk(halo_ref, own_ref, 1, chunks):
        flat[span, :] = jnp.concatenate([piece, minus], 0).T


def fill_value_columns(halo_ref, own_ref, chunks, turned):
    for span, piece in each_chunk(halo_ref, own_ref, 1, chunks):
        turned[:HEAD_DIM, span] = piece
        turned[HEAD_DIM:, span] = jnp.ones((EXTRA, CHUNK), BF16)


def with_row(extra, first, value):
    high = value.astype(BF16).astype(F32)
    middle = (value - high).astype(BF16).astype(F32)
    low = value - high - middle
    row = lax.broadcasted_iota(jnp.int32, (EXTRA, TILE), 0)
    for n, part in enumerate((high, middle, low)):
        extra = jnp.where(row == first + n, part, extra)
    return extra.astype(BF16)


def causal():
    row = lax.broadcasted_iota(jnp.int32, (TILE, TILE), 0)
    return row <= lax.broadcasted_iota(jnp.int32, (TILE, TILE), 1)


def per_tile(tile_start_ref, i, body):
    reach = jnp.clip(i + REACH - tile_start_ref[i], 1, REACH)
    for count in range(1, REACH + 1):
        pl.when(reach == count)(functools.partial(body, count))


def send_block(buffer, out_ref, sent, block):
    part = pl.ds(block * HALO, HALO)
    return pltpu.make_async_copy(buffer.at[part], out_ref.at[part], sent.at[block])


def forward_tiles(
    block, tile_start_ref, query_code_ref, kvq_ref, store, stat_ref, key_flat, value_turned
):
    def tile(step, _):
        i = block * AHEAD_TILES + step

        def body(count):
            q = jnp.concatenate([tile_of(kvq_ref, 2, i), query_code_ref[i]], 0)
            scores = []
            top = None
            for j in range(count):
                first = pl.multiple_of((i + REACH - count + j) * TILE, TILE)
                s = nn(key_flat[pl.ds(first, TILE), :], q)
                if j == count - 1:
                    s = jnp.where(causal(), s, NEG)
                scores.append(s)
                t = jnp.max(s, axis=0, keepdims=True)
                top = t if top is None else jnp.maximum(top, t)
            shift = top * (SCALE * LOG2E)
            out = None
            for j in range(count):
                first = pl.multiple_of((i + REACH - count + j) * TILE, TILE)
                e = jnp.exp2(scores[j] * (SCALE * LOG2E) - shift)
                o = nn(value_turned[:, pl.ds(first, TILE)], e.astype(BF16))
                out = o if out is None else out + o
            total = out[HEAD_DIM : HEAD_DIM + 1]
            out = (out[:HEAD_DIM] / total).astype(BF16)
            store(2 * i, out[:, :CHUNK])
            store(2 * i + 1, out[:, CHUNK:])
            stat_ref[i] = top + jnp.log(total) * (1.0 / SCALE)

        per_tile(tile_start_ref, i, body)
        return 0

    lax.fori_loop(0, AHEAD_TILES, tile, 0)


def late_forward_kernel(
    tile_start_ref, key_code_ref, query_code_ref, kvq_ref, out_ref, stat_ref,
    key_flat, value_turned, buffer, sent
):
    chunks = range(HALO, HALO + CHUNKS)
    fill_keys(None, kvq_ref, key_code_ref, chunks, key_flat, None)
    fill_value_columns(None, kvq_ref, chunks, value_turned)

    def store(chunk, value):
        buffer[chunk, 0] = value

    def block(b, _):
        forward_tiles(
            b, tile_start_ref, query_code_ref, kvq_ref, store, stat_ref, key_flat, value_turned
        )
        send_block(buffer, out_ref, sent, b).start()
        return 0

    lax.fori_loop(1, BLOCKS, block, 0)
    for b in range(1, BLOCKS):
        send_block(buffer, out_ref, sent, b).wait()


def cost(time):
    return pl.CostEstimate(flops=int(time * 1.1e9), bytes_accessed=0, transcendentals=0)


OUT_SHAPE = pltpu.HBM((CHUNKS, 1, HEAD_DIM, CHUNK), BF16)


def part(count, width):
    return pl.BlockSpec((count, width, HEAD_DIM, CHUNK), lambda b: (0, 0, 0, 0))


def forward_scratch(window, chunks):
    return [
        pltpu.VMEM((window, WIDE), BF16),
        pltpu.VMEM((WIDE, window), BF16),
        pltpu.VMEM((chunks, 1, HEAD_DIM, CHUNK), BF16),
        pltpu.SemaphoreType.DMA((BLOCKS,)),
    ]


def late_forward(tile_start, codes, kvq):
    return pl.pallas_call(
        late_forward_kernel,
        in_specs=[smem(), vmem(), vmem(), vmem()],
        out_specs=[hbm(), vmem()],
        out_shape=[OUT_SHAPE, jax.ShapeDtypeStruct((TILES, 1, TILE), F32)],
        scratch_shapes=forward_scratch(WINDOW, CHUNKS),
        compiler_params=pltpu.CompilerParams(vmem_limit_bytes=40 * MIB),
        cost_estimate=cost(30),
        name="late_forward",
    )(tile_start, *codes, kvq)


def backward_tiles(
    low, high, tile_start_ref, query_code_ref, kvq_ref, g_ref, out_ref, stat_ref, store,
    key_flat, key_turned, value_flat, key_sum, value_sum
):
    def tile(i, _):
        def body(count):
            q = tile_of(kvq_ref, 2, i)
            g = tile_of(g_ref, 0, i)
            o = tile_of(out_ref, 0, i)
            delta = jnp.sum(o.astype(F32) * g.astype(F32), axis=0, keepdims=True)
            stat = stat_ref[i]
            code = query_code_ref[i].astype(F32)
            q_wide = jnp.concatenate([q, with_row(code, 2 * DOC_BITS, stat)], 0)
            g_wide = jnp.concatenate([g, with_row(jnp.zeros_like(code), 0, delta)], 0)
            first = pl.multiple_of((i + REACH - count) * TILE, TILE)
            span = pl.ds(first, count * TILE)
            p = jnp.exp2(nn(key_flat[span, :], q_wide) * (SCALE * LOG2E))
            last = (count - 1) * TILE
            tail = jnp.where(causal(), p[last:], 0.0)
            p = jnp.concatenate([p[:last], tail], 0) if last else tail
            d = (p * nn(value_flat[span, :], g_wide)).astype(BF16)
            grad_q = nn(key_turned[:, span], d)
            key_sum[:, span] += nt(q, d)
            value_sum[:, span] += nt(g, p.astype(BF16))
            grad_q = (grad_q * SCALE).astype(BF16)
            store(2 * i, grad_q[:, :CHUNK])
            store(2 * i + 1, grad_q[:, CHUNK:])

        per_tile(tile_start_ref, i, body)
        return 0

    lax.fori_loop(low, high, tile, 0)


def early_forward_kernel(
    tile_start_ref, key_code_ref, query_code_ref, kvq_ref, halo_ref, _, out_ref, stat_ref,
    key_flat, value_turned, buffer, sent
):
    fill_keys(halo_ref, kvq_ref, key_code_ref, range(2 * HALO), key_flat, None)
    fill_value_columns(halo_ref, kvq_ref, range(2 * HALO), value_turned)

    def store(chunk, value):
        buffer[chunk, 0] = value

    forward_tiles(
        0, tile_start_ref, query_code_ref, kvq_ref, store, stat_ref, key_flat, value_turned
    )
    copy = send_block(buffer, out_ref, sent, 0)
    copy.start()
    copy.wait()


def early_backward_kernel(
    tile_start_ref, key_code_ref, query_code_ref, kvq_ref, halo_ref, g_ref, out_ref, stat_ref,
    back_ref, carry_ref, grad_q_ref,
    key_flat, key_turned, value_flat, key_sum, value_sum, g_part, out_part, back_part, grad_q_part,
    sent
):
    fetches = [
        pltpu.make_async_copy(source.at[pl.ds(0, HALO)], target, sent.at[n])
        for n, (source, target) in enumerate(((g_ref, g_part), (out_ref, out_part)))
    ]
    for copy in fetches:
        copy.start()
    fill_keys(halo_ref, kvq_ref, key_code_ref, range(2 * HALO), key_flat, key_turned)
    fill_value_rows(halo_ref, kvq_ref, range(2 * HALO), value_flat)
    key_sum[...] = jnp.zeros_like(key_sum)
    value_sum[...] = jnp.zeros_like(value_sum)
    for copy in fetches:
        copy.wait()

    def store(chunk, value):
        grad_q_part[chunk] = value

    backward_tiles(
        0, AHEAD_TILES, tile_start_ref, query_code_ref, kvq_ref, g_part, out_part, stat_ref, store,
        key_flat, key_turned, value_flat, key_sum, value_sum
    )
    copies = [pltpu.make_async_copy(grad_q_part, grad_q_ref, sent.at[2])]
    for n, sums in enumerate((key_sum, value_sum)):
        copies.append(
            pltpu.make_async_copy(
                sums.at[:, pl.ds(AHEAD, AHEAD)], carry_ref.at[n], sent.at[3 + n]
            )
        )
    for copy in copies:
        copy.start()
    for n, (sums, factor) in enumerate(((key_sum, SCALE), (value_sum, 1.0))):
        for chunk in range(HALO):
            piece = sums[:, chunk * CHUNK : (chunk + 1) * CHUNK] * factor
            back_part[chunk, n] = piece.astype(BF16)
    back_copy = pltpu.make_async_copy(back_part, back_ref, sent.at[5])
    back_copy.start()
    for copy in (*copies, back_copy):
        copy.wait()


def late_backward_kernel(
    place_ref, tile_start_ref, key_code_ref, query_code_ref, kvq_ref, g_ref, out_ref, stat_ref,
    carry_ref, grad_q_ref, grads_ref, rest_ref, part_0, part_1, part_2, part_3,
    key_flat, key_turned, value_flat, key_sum, value_sum, buffer, queries, g_all,
    out_all, carry, sent, fetched, parted
):
    def fetch(b):
        part = pl.ds(b * HALO, HALO)
        return (
            pltpu.make_async_copy(g_ref.at[part], g_all.at[part], fetched.at[0, b]),
            pltpu.make_async_copy(out_ref.at[part], out_all.at[part], fetched.at[1, b]),
        )

    first = (
        pltpu.make_async_copy(carry_ref, carry, fetched.at[0, 0]),
        pltpu.make_async_copy(grad_q_ref, queries.at[pl.ds(0, HALO)], fetched.at[1, 0]),
    )
    for copy in (*fetch(1), *first, *fetch(2), *fetch(3)):
        copy.start()
    chunks = range(HALO, HALO + CHUNKS)
    fill_keys(None, kvq_ref, key_code_ref, chunks, key_flat, key_turned)
    fill_value_rows(None, kvq_ref, chunks, value_flat)
    for sums in (key_sum, value_sum):
        sums[:, AHEAD:] = jnp.zeros((HEAD_DIM, GROUP), F32)

    def store(chunk, value):
        queries[chunk] = value

    def send_queries(b):
        copies = []
        for d, ref in enumerate((part_0, part_1, part_2, part_3)):
            chunk = b * HALO + 2 * (place_ref[2] ^ d)
            copies.append(
                pltpu.make_async_copy(queries.at[pl.ds(chunk, 2)], ref.at[b], parted.at[b, d])
            )
        return copies

    def block(b, _):
        for copy in fetch(b):
            copy.wait()
        backward_tiles(
            b * AHEAD_TILES, (b + 1) * AHEAD_TILES,
            tile_start_ref, query_code_ref, kvq_ref, g_all, out_all, stat_ref, store,
            key_flat, key_turned, value_flat, key_sum, value_sum
        )

        @pl.when(b == 1)
        def _():
            for copy in first:
                copy.wait()
            for copy in send_queries(0):
                copy.start()
            key_sum[:, AHEAD : 2 * AHEAD] += carry[0]
            value_sum[:, AHEAD : 2 * AHEAD] += carry[1]

        for n, (sums, factor) in enumerate(((key_sum, SCALE), (value_sum, 1.0))):
            for chunk in range(HALO):
                place = pl.multiple_of(b * AHEAD + chunk * CHUNK, CHUNK)
                piece = sums[:, pl.ds(place, CHUNK)] * factor
                buffer[(b - 1) * HALO + chunk, n] = piece.astype(BF16)
        send_block(buffer, grads_ref, sent, b - 1).start()
        for copy in send_queries(b):
            copy.start()
        return 0

    lax.fori_loop(1, BLOCKS, block, 0)
    for n, sums in enumerate((key_sum, value_sum)):
        rest_ref[n] = sums[:, GROUP:]
    for b in range(BLOCKS - 1):
        send_block(buffer, grads_ref, sent, b).wait()
    for b in range(BLOCKS):
        for copy in send_queries(b):
            copy.wait()


def sums_scratch(window):
    return [
        pltpu.VMEM((window, WIDE), BF16),
        pltpu.VMEM((HEAD_DIM, window), BF16),
        pltpu.VMEM((window, WIDE), BF16),
        pltpu.VMEM((HEAD_DIM, window), F32),
        pltpu.VMEM((HEAD_DIM, window), F32),
    ]


def early_forward(tile_start, codes, kvq, halo, out):
    return pl.pallas_call(
        early_forward_kernel,
        grid=(1,),
        in_specs=[smem(), vmem(), vmem(), part(HALO, 3), vmem(), hbm()],
        out_specs=[hbm(), vmem()],
        out_shape=[OUT_SHAPE, jax.ShapeDtypeStruct((AHEAD_TILES, 1, TILE), F32)],
        input_output_aliases={5: 0},
        scratch_shapes=forward_scratch(2 * AHEAD, HALO),
        compiler_params=pltpu.CompilerParams(vmem_limit_bytes=40 * MIB),
        cost_estimate=cost(1),
        name="early_forward",
    )(tile_start, *codes, kvq, halo, *in_hbm(out))


def early_backward(tile_start, codes, kvq, halo, g, out, stat):
    return pl.pallas_call(
        early_backward_kernel,
        grid=(1,),
        in_specs=[smem(), vmem(), vmem(), part(HALO, 3), vmem(), hbm(), hbm(), vmem()],
        out_specs=[hbm()] * 3,
        out_shape=[
            pltpu.HBM((HALO, 2, HEAD_DIM, CHUNK), BF16),
            pltpu.HBM((2, HEAD_DIM, AHEAD), F32),
            pltpu.HBM((HALO, HEAD_DIM, CHUNK), BF16),
        ],
        scratch_shapes=sums_scratch(2 * AHEAD)
        + [
            pltpu.VMEM((HALO, 1, HEAD_DIM, CHUNK), BF16),
            pltpu.VMEM((HALO, 1, HEAD_DIM, CHUNK), BF16),
            pltpu.VMEM((HALO, 2, HEAD_DIM, CHUNK), BF16),
            pltpu.VMEM((HALO, HEAD_DIM, CHUNK), BF16),
            pltpu.SemaphoreType.DMA((6,)),
        ],
        compiler_params=pltpu.CompilerParams(vmem_limit_bytes=40 * MIB),
        cost_estimate=cost(1),
        name="early_backward",
    )(tile_start, *codes, kvq, halo, *in_hbm(g, out), stat)


def late_backward(place, tile_start, codes, kvq, g, out, stat, carry, grad_q):
    return pl.pallas_call(
        late_backward_kernel,
        in_specs=[smem(), smem(), vmem(), vmem(), vmem(), hbm(), hbm(), vmem(), hbm(), hbm()],
        out_specs=[hbm(), vmem()] + [hbm()] * 4,
        out_shape=[
            pltpu.HBM((CHUNKS, 2, HEAD_DIM, CHUNK), BF16),
            jax.ShapeDtypeStruct((2, HEAD_DIM, AHEAD), F32),
        ]
        + [pltpu.HBM((4, 2, HEAD_DIM, CHUNK), BF16)] * 4,
        scratch_shapes=sums_scratch(WINDOW)
        + [
            pltpu.VMEM((CHUNKS, 2, HEAD_DIM, CHUNK), BF16),
            pltpu.VMEM((CHUNKS, HEAD_DIM, CHUNK), BF16),
            pltpu.VMEM((CHUNKS, 1, HEAD_DIM, CHUNK), BF16),
            pltpu.VMEM((CHUNKS, 1, HEAD_DIM, CHUNK), BF16),
            pltpu.VMEM((2, HEAD_DIM, AHEAD), F32),
            pltpu.SemaphoreType.DMA((BLOCKS,)),
            pltpu.SemaphoreType.DMA((2, BLOCKS)),
            pltpu.SemaphoreType.DMA((BLOCKS, 4)),
        ],
        compiler_params=pltpu.CompilerParams(vmem_limit_bytes=40 * MIB),
        cost_estimate=cost(10),
        name="late_backward",
    )(place, tile_start, *codes, kvq, *in_hbm(g, out), stat, *in_hbm(carry, grad_q))


def join_kernel(back_ref, rest_ref, _, out_ref, buffer, moved):
    sends = []
    for n, factor in enumerate((SCALE, 1.0)):
        for chunk in range(HALO):
            own = rest_ref[n, :, chunk * CHUNK : (chunk + 1) * CHUNK] * factor
            buffer[chunk, n] = (own + back_ref[chunk, n].astype(F32)).astype(BF16)
        target = out_ref.at[pl.ds(CHUNKS - HALO, HALO), n]
        sends.append(pltpu.make_async_copy(buffer.at[:, n], target, moved.at[n]))
        sends[n].start()
    for copy in sends:
        copy.wait()


def join(back, rest, grads):
    return pl.pallas_call(
        join_kernel,
        in_specs=[vmem(), vmem(), hbm()],
        out_specs=hbm(),
        out_shape=pltpu.HBM(grads.shape, BF16),
        input_output_aliases={2: 0},
        scratch_shapes=[
            pltpu.VMEM((HALO, 2, HEAD_DIM, CHUNK), BF16),
            pltpu.SemaphoreType.DMA((2,)),
        ],
        compiler_params=pltpu.CompilerParams(vmem_limit_bytes=40 * MIB),
        name="join",
    )(back, rest, *in_hbm(grads))


def turn_kernel(axis, place_ref, *refs):
    sources, targets, sent = refs[:4], refs[4:8], refs[8]
    here = place_ref[axis]
    copies = []
    for d in range(4):
        for e in range(4):
            copies.append(
                pltpu.make_async_copy(sources[d].at[here ^ e], targets[e].at[d], sent.at[d, e])
            )
    for copy in copies:
        copy.start()
    for copy in copies:
        copy.wait()


def turn(place, axis, parts):
    return pl.pallas_call(
        functools.partial(turn_kernel, axis),
        in_specs=[smem()] + [pl.BlockSpec(memory_space=pl.ANY)] * 4,
        out_specs=[hbm()] * 4,
        out_shape=[pltpu.HBM((4, 2, HEAD_DIM, CHUNK), BF16)] * 4,
        scratch_shapes=[pltpu.SemaphoreType.DMA((4, 4))],
        compiler_params=pltpu.CompilerParams(vmem_limit_bytes=40 * MIB),
        cost_estimate=cost(1),
        name="turn",
    )(place, *parts)


def other_core_kernel(place_ref, *refs):
    sources, target, sent = refs[:4], refs[4], refs[5]
    copies = [
        pltpu.make_async_copy(sources[e].at[:, 1 - place_ref[3]], target.at[e], sent.at[e])
        for e in range(4)
    ]
    for copy in copies:
        copy.start()
    for copy in copies:
        copy.wait()


def other_core(place, parts):
    return pl.pallas_call(
        other_core_kernel,
        in_specs=[smem()] + [pl.BlockSpec(memory_space=pl.ANY)] * 4,
        out_specs=hbm(),
        out_shape=pltpu.HBM((4, 4, HEAD_DIM, CHUNK), BF16),
        scratch_shapes=[pltpu.SemaphoreType.DMA((4,))],
        compiler_params=pltpu.CompilerParams(vmem_limit_bytes=40 * MIB),
        cost_estimate=cost(1),
        name="other_core",
    )(place, *parts)


def by_distance(parts, axis):
    return [parts[0]] + [
        lax.ppermute(parts[d], axis, [(i, i ^ d) for i in range(4)]) for d in range(1, 4)
    ]


def rows_kernel(place_ref, part_0, part_1, part_2, part_3, other_ref, out_ref, rows, sent):
    mirrored, y, zl, core = place_ref[0], place_ref[1], place_ref[2], place_ref[3]
    copies = []
    for e, ref in enumerate((part_0, part_1, part_2, part_3)):
        pieces = []
        for head_zl in range(4):
            d = zl ^ jnp.where(mirrored == 1, 3 - head_zl, head_zl)
            own, other = ref[d, core], other_ref[e, d]
            pieces.append(jnp.where(core == 0, own, other))
            pieces.append(jnp.where(core == 0, other, own))
        rows[e] = jnp.concatenate(pieces, 0).T
        first = pl.multiple_of((y ^ e) * 768, 768)
        copies.append(
            pltpu.make_async_copy(rows.at[e], out_ref.at[:, pl.ds(first, 768)], sent.at[e])
        )
        copies[e].start()
    for copy in copies:
        copy.wait()


def rows_of(place, parts, other):
    return pl.pallas_call(
        rows_kernel,
        in_specs=[smem()] + [vmem()] * 5,
        out_specs=hbm(),
        out_shape=pltpu.HBM((CHUNK, HEADS * HEAD_DIM), BF16),
        scratch_shapes=[
            pltpu.VMEM((4, CHUNK, 768), BF16),
            pltpu.SemaphoreType.DMA((4,)),
        ],
        compiler_params=pltpu.CompilerParams(vmem_limit_bytes=28 * MIB),
        cost_estimate=cost(1),
        name="rows_of",
    )(place, *parts, other)


def to_rows(place, parts):
    parts = by_distance(turn(place, 1, parts), "y")
    other = lax.ppermute(other_core(place, parts), "c", [(0, 1), (1, 0)])
    return rows_of(place, parts, other)


def gate_kernel(*_):
    pass


def after(array, *others):
    return pl.pallas_call(
        gate_kernel,
        in_specs=[hbm()] + [pl.BlockSpec(memory_space=pl.ANY)] * len(others),
        out_specs=hbm(),
        out_shape=pltpu.HBM(array.shape, array.dtype),
        input_output_aliases={0: 0},
        name="after",
    )(array, *others)


def group_pairs():
    def index(x, zh, y, zl, c):
        return (((x * 2 + zh) * 4 + y) * 4 + zl) * 2 + c

    pairs = []
    for group in range(7):
        for y in range(4):
            for zl in range(4):
                for c in range(2):
                    pairs.append(
                        (
                            index(group // 2, group % 2, y, zl, c),
                            index((group + 1) // 2, (group + 1) % 2, y, 3 - zl, c),
                        )
                    )
    return pairs


def to_heads(array):
    return lax.all_to_all(array, GROUP_AXES, split_axis=0, concat_axis=0, tiled=True)


def places(doc_ids):
    group = lax.axis_index("x") * 2 + lax.axis_index("zh")
    own = lax.dynamic_slice_in_dim(doc_ids, group * GROUP, GROUP)
    ahead = lax.dynamic_slice_in_dim(doc_ids, jnp.maximum(group * GROUP - AHEAD, 0), AHEAD)
    ahead = jnp.where(group > 0, ahead, -1)
    docs = jnp.concatenate([ahead, own])
    leads = own.reshape(TILES, TILE)[:, :1]
    tile_start = jnp.sum((docs[None] < leads).astype(jnp.int32), 1) // TILE
    row = jnp.arange(EXTRA, dtype=jnp.int32)[:, None]
    bits = (docs[None] >> (row // 2)) & 1
    coded = row < 2 * DOC_BITS
    differs = (bits != row % 2) | (docs[None] < 0)
    key_code = jnp.where(coded, jnp.where(differs, -FAR, 0.0), jnp.where(row < 15, -1.0, 0.0))
    query_code = jnp.where(coded & (bits[:, AHEAD:] == row % 2), 1.0, 0.0)
    query_code = query_code.reshape(EXTRA, TILES, TILE).transpose(1, 0, 2)
    return tile_start, (key_code.astype(BF16), query_code.astype(BF16))


def shards(queries, keys, values, cotangent, doc_ids):
    place = jnp.stack([lax.axis_index(axis) for axis in ("zh", "y", "zl", "c")]).astype(jnp.int32)
    mirror = place[:1]
    kvq = to_heads(pack(mirror, keys, values, queries))
    tile_start, codes = places(doc_ids)
    cotangent, tile_start, codes = lax.optimization_barrier((cotangent, tile_start, codes))
    pairs = group_pairs()
    last = kvq[CHUNKS - HALO :, :2]
    halo = lax.ppermute(last, AXES, pairs)
    g = to_heads(after(pack(mirror, cotangent), last))
    out, stat = late_forward(tile_start, codes, kvq)
    out, early_stat = early_forward(tile_start, codes, kvq, halo, out)
    back, carry, early_q = early_backward(tile_start, codes, kvq, halo, g, out, early_stat)
    grads, rest, *grad_q_parts = late_backward(
        place, tile_start, codes, kvq, g, out, stat, carry, early_q
    )
    grad_q_parts = by_distance(grad_q_parts, "zl")
    grad_q = to_rows(place, grad_q_parts)
    back = lax.ppermute(back, AXES, [(b, a) for a, b in pairs])
    grads = after(join(back, rest, grads), *grad_q_parts[1:])
    (attended,) = unpack(mirror, to_heads(out))
    grad_k, grad_v = unpack(mirror, to_heads(grads))
    return attended, grad_q, grad_k, grad_v


def solution(mesh):
    wide = Mesh(mesh.devices.reshape(4, 2, 4, 4, 2), AXES)
    rows = P(AXES, None)
    return jax.shard_map(
        shards,
        mesh=wide,
        in_specs=(rows, rows, rows, rows, P()),
        out_specs=(rows, rows, rows, rows),
        check_vma=False,
    )
```

```python
import functools
import math

import jax
import jax.numpy as jnp
from jax import lax
from jax.experimental import pallas as pl
from jax.experimental.pallas import tpu as pltpu
from jax.sharding import Mesh
from jax.sharding import PartitionSpec as P

HEAD_DIM = 96
HEADS = 32
CHUNK = 128
CHUNKS = 32
HALO = 8
DOC_BITS = 6
EXTRA = 16
WIDE = HEAD_DIM + EXTRA
FAR = 2.0**20
GROUP = CHUNK * CHUNKS
AHEAD = CHUNK * HALO
WINDOW = GROUP + AHEAD
TILE = 256
TILES = GROUP // TILE
BLOCKS = CHUNKS // HALO
AHEAD_TILES = AHEAD // TILE
REACH = AHEAD_TILES + 1
NEG = -1e30
SCALE = 1.0 / math.sqrt(HEAD_DIM)
LOG2E = 1.4426950408889634
MIB = 1024 * 1024

AXES = ("x", "zh", "y", "zl", "c")
GROUP_AXES = ("y", "zl", "c")
F32 = jnp.float32
BF16 = jnp.bfloat16


def vmem():
    return pl.BlockSpec(memory_space=pltpu.VMEM)


def smem():
    return pl.BlockSpec(memory_space=pltpu.SMEM)


def hbm():
    return pl.BlockSpec(memory_space=pltpu.HBM)


def in_hbm(*arrays):
    return [pltpu.with_memory_space_constraint(array, pltpu.HBM) for array in arrays]


def pack_kernel(mirror_ref, *refs):
    count = len(refs) - 5
    sources, (out_ref, rows, blocks, arrived, sent) = refs[:count], refs[count:]
    mirrored = mirror_ref[0]

    def fetch(y, n):
        return pltpu.make_async_copy(
            sources[n].at[:, pl.ds(y * 768, 768)], rows.at[n, y], arrived.at[n, y]
        )

    def send(y):
        part = pl.ds(y * 8, 8)
        return pltpu.make_async_copy(blocks.at[part], out_ref.at[part], sent.at[y])

    for y in range(4):
        for n in range(count):
            fetch(y, n).start()
    for y in range(4):
        for n in range(count):
            fetch(y, n).wait()
            turned = rows[n, y].T
            for zl in range(4):
                slot = 8 * y + 2 * jnp.where(mirrored == 1, 3 - zl, zl)
                piece = turned[zl * 192 : (zl + 1) * 192]
                blocks[pl.ds(slot, 2), n] = piece.reshape(2, HEAD_DIM, CHUNK)
        send(y).start()
    for y in range(4):
        send(y).wait()


def pack(mirror, *arrays):
    count = len(arrays)
    shape = (HEADS, count, HEAD_DIM, CHUNK)
    return pl.pallas_call(
        pack_kernel,
        in_specs=[smem()] + [hbm()] * count,
        out_specs=hbm(),
        out_shape=pltpu.HBM(shape, BF16),
        scratch_shapes=[
            pltpu.VMEM((count, 4, CHUNK, 768), BF16),
            pltpu.VMEM(shape, BF16),
            pltpu.SemaphoreType.DMA((count, 4)),
            pltpu.SemaphoreType.DMA((4,)),
        ],
        compiler_params=pltpu.CompilerParams(vmem_limit_bytes=40 * MIB),
        name="pack",
    )(mirror, *in_hbm(*arrays))


def unpack_kernel(mirror_ref, in_ref, *out_refs):
    mirrored = mirror_ref[0]
    for n, out_ref in enumerate(out_refs):
        pieces = []
        for zl in range(4):
            slot = 2 * jnp.where(mirrored == 1, 3 - zl, zl)
            pieces.append(in_ref[pl.ds(slot, 2), n].reshape(192, CHUNK))
        out_ref[...] = jnp.concatenate(pieces, 0).T


def unpack(mirror, array):
    count = array.shape[1]
    return pl.pallas_call(
        unpack_kernel,
        grid=(4,),
        in_specs=[
            smem(),
            pl.BlockSpec((8, count, HEAD_DIM, CHUNK), lambda y: (y, 0, 0, 0)),
        ],
        out_specs=[pl.BlockSpec((CHUNK, 768), lambda y: (0, y))] * count,
        out_shape=[jax.ShapeDtypeStruct((CHUNK, HEADS * HEAD_DIM), BF16)] * count,
        compiler_params=pltpu.CompilerParams(vmem_limit_bytes=28 * MIB),
        name="unpack",
    )(mirror, array)


def tile_of(ref, n, i):
    return jnp.concatenate([ref[2 * i, n], ref[2 * i + 1, n]], 1)


def nn(a, b):
    return lax.dot_general(a, b, (((1,), (0,)), ((), ())), preferred_element_type=F32)


def nt(a, b):
    return lax.dot_general(a, b, (((1,), (1,)), ((), ())), preferred_element_type=F32)


def each_chunk(halo_ref, own_ref, n, chunks):
    for chunk in chunks:
        piece = halo_ref[chunk, n] if chunk < HALO else own_ref[chunk - HALO, n]
        yield slice(chunk * CHUNK, (chunk + 1) * CHUNK), piece


def fill_keys(halo_ref, own_ref, code_ref, chunks, flat, turned):
    for span, piece in each_chunk(halo_ref, own_ref, 0, chunks):
        flat[span, :] = jnp.concatenate([piece, code_ref[:, span]], 0).T
        if turned is not None:
            turned[:, span] = piece


def fill_value_rows(halo_ref, own_ref, chunks, flat):
    row = lax.broadcasted_iota(jnp.int32, (EXTRA, CHUNK), 0)
    minus = jnp.where(row < 3, -1.0, 0.0).astype(BF16)
    for span, piece in each_chunk(halo_ref, own_ref, 1, chunks):
        flat[span, :] = jnp.concatenate([piece, minus], 0).T


def fill_value_columns(halo_ref, own_ref, chunks, turned):
    for span, piece in each_chunk(halo_ref, own_ref, 1, chunks):
        turned[:HEAD_DIM, span] = piece
        turned[HEAD_DIM:, span] = jnp.ones((EXTRA, CHUNK), BF16)


def with_row(extra, first, value):
    high = value.astype(BF16).astype(F32)
    middle = (value - high).astype(BF16).astype(F32)
    low = value - high - middle
    row = lax.broadcasted_iota(jnp.int32, (EXTRA, TILE), 0)
    for n, part in enumerate((high, middle, low)):
        extra = jnp.where(row == first + n, part, extra)
    return extra.astype(BF16)


def causal():
    row = lax.broadcasted_iota(jnp.int32, (TILE, TILE), 0)
    return row <= lax.broadcasted_iota(jnp.int32, (TILE, TILE), 1)


def per_tile(tile_start_ref, i, body):
    reach = jnp.clip(i + REACH - tile_start_ref[i], 1, REACH)
    for count in range(1, REACH + 1):
        pl.when(reach == count)(functools.partial(body, count))


def send_block(buffer, out_ref, sent, block):
    part = pl.ds(block * HALO, HALO)
    return pltpu.make_async_copy(buffer.at[part], out_ref.at[part], sent.at[block])


def forward_tiles(
    block, tile_start_ref, query_code_ref, kvq_ref, store, stat_ref, key_flat, value_turned
):
    def tile(step, _):
        i = block * AHEAD_TILES + step

        def body(count):
            q = jnp.concatenate([tile_of(kvq_ref, 2, i), query_code_ref[i]], 0)
            scores = []
            top = None
            for j in range(count):
                first = pl.multiple_of((i + REACH - count + j) * TILE, TILE)
                s = nn(key_flat[pl.ds(first, TILE), :], q)
                if j == count - 1:
                    s = jnp.where(causal(), s, NEG)
                scores.append(s)
                t = jnp.max(s, axis=0, keepdims=True)
                top = t if top is None else jnp.maximum(top, t)
            shift = top * (SCALE * LOG2E)
            out = None
            for j in range(count):
                first = pl.multiple_of((i + REACH - count + j) * TILE, TILE)
                e = jnp.exp2(scores[j] * (SCALE * LOG2E) - shift)
                o = nn(value_turned[:, pl.ds(first, TILE)], e.astype(BF16))
                out = o if out is None else out + o
            total = out[HEAD_DIM : HEAD_DIM + 1]
            out = (out[:HEAD_DIM] / total).astype(BF16)
            store(2 * i, out[:, :CHUNK])
            store(2 * i + 1, out[:, CHUNK:])
            stat_ref[i] = top + jnp.log(total) * (1.0 / SCALE)

        per_tile(tile_start_ref, i, body)
        return 0

    lax.fori_loop(0, AHEAD_TILES, tile, 0)


def part_copies(place_ref, buffer, parts, b, sems, fetch=False):
    copies = []
    for d, ref in enumerate(parts):
        here = buffer.at[pl.ds(b * HALO + 2 * (place_ref[2] ^ d), 2)]
        there = ref.at[b]
        ends = (there, here) if fetch else (here, there)
        copies.append(pltpu.make_async_copy(*ends, sems.at[b, d]))
    return copies


def late_forward_kernel(
    place_ref, tile_start_ref, key_code_ref, query_code_ref, kvq_ref,
    part_0, part_1, part_2, part_3, stat_ref, key_flat, value_turned, buffer, sent
):
    parts = (part_0, part_1, part_2, part_3)
    chunks = range(HALO, HALO + CHUNKS)
    fill_keys(None, kvq_ref, key_code_ref, chunks, key_flat, None)
    fill_value_columns(None, kvq_ref, chunks, value_turned)

    def store(chunk, value):
        buffer[chunk] = value

    def block(b, _):
        forward_tiles(
            b, tile_start_ref, query_code_ref, kvq_ref, store, stat_ref, key_flat, value_turned
        )
        for copy in part_copies(place_ref, buffer, parts, b, sent):
            copy.start()
        return 0

    lax.fori_loop(1, BLOCKS, block, 0)
    for b in range(1, BLOCKS):
        for copy in part_copies(place_ref, buffer, parts, b, sent):
            copy.wait()


def cost(time):
    return pl.CostEstimate(flops=int(time * 1.1e9), bytes_accessed=0, transcendentals=0)


PARTS = [pltpu.HBM((4, 2, HEAD_DIM, CHUNK), BF16)] * 4


def part(count, width):
    return pl.BlockSpec((count, width, HEAD_DIM, CHUNK), lambda b: (0, 0, 0, 0))


def forward_scratch(window, chunks):
    return [
        pltpu.VMEM((window, WIDE), BF16),
        pltpu.VMEM((WIDE, window), BF16),
        pltpu.VMEM((chunks, HEAD_DIM, CHUNK), BF16),
        pltpu.SemaphoreType.DMA((BLOCKS, 4)),
    ]


def late_forward(place, tile_start, codes, kvq):
    return pl.pallas_call(
        late_forward_kernel,
        in_specs=[smem(), smem(), vmem(), vmem(), vmem()],
        out_specs=[hbm()] * 4 + [vmem()],
        out_shape=PARTS + [jax.ShapeDtypeStruct((TILES, 1, TILE), F32)],
        scratch_shapes=forward_scratch(WINDOW, CHUNKS),
        compiler_params=pltpu.CompilerParams(vmem_limit_bytes=40 * MIB),
        cost_estimate=cost(30),
        name="late_forward",
    )(place, tile_start, *codes, kvq)


def backward_tiles(
    low, high, tile_start_ref, query_code_ref, kvq_ref, g_ref, out_ref, stat_ref, store,
    key_flat, key_turned, value_flat, key_sum, value_sum
):
    def tile(i, _):
        def body(count):
            q = tile_of(kvq_ref, 2, i)
            g = jnp.concatenate([g_ref[2 * i], g_ref[2 * i + 1]], 1)
            o = jnp.concatenate([out_ref[2 * i], out_ref[2 * i + 1]], 1)
            delta = jnp.sum(o.astype(F32) * g.astype(F32), axis=0, keepdims=True)
            stat = stat_ref[i]
            code = query_code_ref[i].astype(F32)
            q_wide = jnp.concatenate([q, with_row(code, 2 * DOC_BITS, stat)], 0)
            g_wide = jnp.concatenate([g, with_row(jnp.zeros_like(code), 0, delta)], 0)
            first = pl.multiple_of((i + REACH - count) * TILE, TILE)
            span = pl.ds(first, count * TILE)
            p = jnp.exp2(nn(key_flat[span, :], q_wide) * (SCALE * LOG2E))
            last = (count - 1) * TILE
            tail = jnp.where(causal(), p[last:], 0.0)
            p = jnp.concatenate([p[:last], tail], 0) if last else tail
            d = (p * nn(value_flat[span, :], g_wide)).astype(BF16)
            grad_q = nn(key_turned[:, span], d)
            key_sum[:, span] += nt(q, d)
            value_sum[:, span] += nt(g, p.astype(BF16))
            grad_q = (grad_q * SCALE).astype(BF16)
            store(2 * i, grad_q[:, :CHUNK])
            store(2 * i + 1, grad_q[:, CHUNK:])

        per_tile(tile_start_ref, i, body)
        return 0

    lax.fori_loop(low, high, tile, 0)


def early_forward_kernel(
    place_ref, tile_start_ref, key_code_ref, query_code_ref, kvq_ref, halo_ref, _, __, ___, ____,
    part_0, part_1, part_2, part_3, stat_ref, key_flat, value_turned, buffer, sent
):
    fill_keys(halo_ref, kvq_ref, key_code_ref, range(2 * HALO), key_flat, None)
    fill_value_columns(halo_ref, kvq_ref, range(2 * HALO), value_turned)

    def store(chunk, value):
        buffer[chunk] = value

    forward_tiles(
        0, tile_start_ref, query_code_ref, kvq_ref, store, stat_ref, key_flat, value_turned
    )
    copies = part_copies(place_ref, buffer, (part_0, part_1, part_2, part_3), 0, sent)
    for copy in copies:
        copy.start()
    for copy in copies:
        copy.wait()


def early_backward_kernel(
    place_ref, tile_start_ref, key_code_ref, query_code_ref, kvq_ref, halo_ref, stat_ref,
    g_0, g_1, g_2, g_3, out_0, out_1, out_2, out_3,
    back_ref, carry_ref, grad_q_ref,
    key_flat, key_turned, value_flat, key_sum, value_sum, g_part, out_part, back_part, grad_q_part,
    sent, fetched_g, fetched_out
):
    fetches = part_copies(place_ref, g_part, (g_0, g_1, g_2, g_3), 0, fetched_g, True)
    fetches += part_copies(place_ref, out_part, (out_0, out_1, out_2, out_3), 0, fetched_out, True)
    for copy in fetches:
        copy.start()
    fill_keys(halo_ref, kvq_ref, key_code_ref, range(2 * HALO), key_flat, key_turned)
    fill_value_rows(halo_ref, kvq_ref, range(2 * HALO), value_flat)
    key_sum[...] = jnp.zeros_like(key_sum)
    value_sum[...] = jnp.zeros_like(value_sum)
    for copy in fetches:
        copy.wait()

    def store(chunk, value):
        grad_q_part[chunk] = value

    backward_tiles(
        0, AHEAD_TILES, tile_start_ref, query_code_ref, kvq_ref, g_part, out_part, stat_ref, store,
        key_flat, key_turned, value_flat, key_sum, value_sum
    )
    copies = [pltpu.make_async_copy(grad_q_part, grad_q_ref, sent.at[2])]
    for n, sums in enumerate((key_sum, value_sum)):
        copies.append(
            pltpu.make_async_copy(
                sums.at[:, pl.ds(AHEAD, AHEAD)], carry_ref.at[n], sent.at[3 + n]
            )
        )
    for copy in copies:
        copy.start()
    for n, (sums, factor) in enumerate(((key_sum, SCALE), (value_sum, 1.0))):
        for chunk in range(HALO):
            piece = sums[:, chunk * CHUNK : (chunk + 1) * CHUNK] * factor
            back_part[chunk, n] = piece.astype(BF16)
    back_copy = pltpu.make_async_copy(back_part, back_ref, sent.at[5])
    back_copy.start()
    for copy in (*copies, back_copy):
        copy.wait()


def late_backward_kernel(
    place_ref, tile_start_ref, key_code_ref, query_code_ref, kvq_ref, stat_ref,
    g_0, g_1, g_2, g_3, out_0, out_1, out_2, out_3, carry_ref, grad_q_ref, grads_ref, rest_ref, part_0, part_1, part_2, part_3,
    key_flat, key_turned, value_flat, key_sum, value_sum, buffer, queries, g_all,
    out_all, carry, sent, fetched, parted, fetched_g, fetched_out
):
    def fetch(b):
        return part_copies(
            place_ref, g_all, (g_0, g_1, g_2, g_3), b, fetched_g, True
        ) + part_copies(place_ref, out_all, (out_0, out_1, out_2, out_3), b, fetched_out, True)

    first = (
        pltpu.make_async_copy(carry_ref, carry, fetched.at[0]),
        pltpu.make_async_copy(grad_q_ref, queries.at[pl.ds(0, HALO)], fetched.at[1]),
    )
    for copy in (*fetch(1), *first, *fetch(2), *fetch(3)):
        copy.start()
    chunks = range(HALO, HALO + CHUNKS)
    fill_keys(None, kvq_ref, key_code_ref, chunks, key_flat, key_turned)
    fill_value_rows(None, kvq_ref, chunks, value_flat)
    for sums in (key_sum, value_sum):
        sums[:, AHEAD:] = jnp.zeros((HEAD_DIM, GROUP), F32)

    def store(chunk, value):
        queries[chunk] = value

    def send_queries(b):
        return part_copies(place_ref, queries, (part_0, part_1, part_2, part_3), b, parted)

    def block(b, _):
        for copy in fetch(b):
            copy.wait()
        backward_tiles(
            b * AHEAD_TILES, (b + 1) * AHEAD_TILES,
            tile_start_ref, query_code_ref, kvq_ref, g_all, out_all, stat_ref, store,
            key_flat, key_turned, value_flat, key_sum, value_sum
        )

        @pl.when(b == 1)
        def _():
            for copy in first:
                copy.wait()
            for copy in send_queries(0):
                copy.start()
            key_sum[:, AHEAD : 2 * AHEAD] += carry[0]
            value_sum[:, AHEAD : 2 * AHEAD] += carry[1]

        for n, (sums, factor) in enumerate(((key_sum, SCALE), (value_sum, 1.0))):
            for chunk in range(HALO):
                place = pl.multiple_of(b * AHEAD + chunk * CHUNK, CHUNK)
                piece = sums[:, pl.ds(place, CHUNK)] * factor
                buffer[(b - 1) * HALO + chunk, n] = piece.astype(BF16)
        send_block(buffer, grads_ref, sent, b - 1).start()
        for copy in send_queries(b):
            copy.start()
        return 0

    lax.fori_loop(1, BLOCKS, block, 0)
    for n, sums in enumerate((key_sum, value_sum)):
        rest_ref[n] = sums[:, GROUP:]
    for b in range(BLOCKS - 1):
        send_block(buffer, grads_ref, sent, b).wait()
    for b in range(BLOCKS):
        for copy in send_queries(b):
            copy.wait()


def sums_scratch(window):
    return [
        pltpu.VMEM((window, WIDE), BF16),
        pltpu.VMEM((HEAD_DIM, window), BF16),
        pltpu.VMEM((window, WIDE), BF16),
        pltpu.VMEM((HEAD_DIM, window), F32),
        pltpu.VMEM((HEAD_DIM, window), F32),
    ]


def early_forward(place, tile_start, codes, kvq, halo, parts):
    return pl.pallas_call(
        early_forward_kernel,
        grid=(1,),
        in_specs=[smem(), smem(), vmem(), vmem(), part(HALO, 3), vmem()] + [hbm()] * 4,
        out_specs=[hbm()] * 4 + [vmem()],
        out_shape=PARTS + [jax.ShapeDtypeStruct((AHEAD_TILES, 1, TILE), F32)],
        input_output_aliases={6 + d: d for d in range(4)},
        scratch_shapes=forward_scratch(2 * AHEAD, HALO),
        compiler_params=pltpu.CompilerParams(vmem_limit_bytes=40 * MIB),
        cost_estimate=cost(1),
        name="early_forward",
    )(place, tile_start, *codes, kvq, halo, *in_hbm(*parts))


def early_backward(place, tile_start, codes, kvq, halo, stat, g, out):
    return pl.pallas_call(
        early_backward_kernel,
        grid=(1,),
        in_specs=[smem(), smem(), vmem(), vmem(), part(HALO, 3), vmem(), vmem()] + [hbm()] * 8,
        out_specs=[hbm()] * 3,
        out_shape=[
            pltpu.HBM((HALO, 2, HEAD_DIM, CHUNK), BF16),
            pltpu.HBM((2, HEAD_DIM, AHEAD), F32),
            pltpu.HBM((HALO, HEAD_DIM, CHUNK), BF16),
        ],
        scratch_shapes=sums_scratch(2 * AHEAD)
        + [
            pltpu.VMEM((HALO, HEAD_DIM, CHUNK), BF16),
            pltpu.VMEM((HALO, HEAD_DIM, CHUNK), BF16),
            pltpu.VMEM((HALO, 2, HEAD_DIM, CHUNK), BF16),
            pltpu.VMEM((HALO, HEAD_DIM, CHUNK), BF16),
            pltpu.SemaphoreType.DMA((6,)),
            pltpu.SemaphoreType.DMA((1, 4)),
            pltpu.SemaphoreType.DMA((1, 4)),
        ],
        compiler_params=pltpu.CompilerParams(vmem_limit_bytes=40 * MIB),
        cost_estimate=cost(1),
        name="early_backward",
    )(place, tile_start, *codes, kvq, halo, stat, *in_hbm(*g, *out))


def late_backward(place, tile_start, codes, kvq, stat, g, out, carry, grad_q):
    return pl.pallas_call(
        late_backward_kernel,
        in_specs=[smem(), smem(), vmem(), vmem(), vmem(), vmem()] + [hbm()] * 10,
        out_specs=[hbm(), vmem()] + [hbm()] * 4,
        out_shape=[
            pltpu.HBM((CHUNKS, 2, HEAD_DIM, CHUNK), BF16),
            jax.ShapeDtypeStruct((2, HEAD_DIM, AHEAD), F32),
        ]
        + [pltpu.HBM((4, 2, HEAD_DIM, CHUNK), BF16)] * 4,
        scratch_shapes=sums_scratch(WINDOW)
        + [
            pltpu.VMEM((CHUNKS, 2, HEAD_DIM, CHUNK), BF16),
            pltpu.VMEM((CHUNKS, HEAD_DIM, CHUNK), BF16),
            pltpu.VMEM((CHUNKS, HEAD_DIM, CHUNK), BF16),
            pltpu.VMEM((CHUNKS, HEAD_DIM, CHUNK), BF16),
            pltpu.VMEM((2, HEAD_DIM, AHEAD), F32),
            pltpu.SemaphoreType.DMA((BLOCKS,)),
            pltpu.SemaphoreType.DMA((2,)),
            pltpu.SemaphoreType.DMA((BLOCKS, 4)),
            pltpu.SemaphoreType.DMA((BLOCKS, 4)),
            pltpu.SemaphoreType.DMA((BLOCKS, 4)),
        ],
        compiler_params=pltpu.CompilerParams(vmem_limit_bytes=40 * MIB),
        cost_estimate=cost(10),
        name="late_backward",
    )(place, tile_start, *codes, kvq, stat, *in_hbm(*g, *out, carry, grad_q))


def join_kernel(back_ref, rest_ref, _, out_ref, buffer, moved):
    sends = []
    for n, factor in enumerate((SCALE, 1.0)):
        for chunk in range(HALO):
            own = rest_ref[n, :, chunk * CHUNK : (chunk + 1) * CHUNK] * factor
            buffer[chunk, n] = (own + back_ref[chunk, n].astype(F32)).astype(BF16)
        target = out_ref.at[pl.ds(CHUNKS - HALO, HALO), n]
        sends.append(pltpu.make_async_copy(buffer.at[:, n], target, moved.at[n]))
        sends[n].start()
    for copy in sends:
        copy.wait()


def join(back, rest, grads):
    return pl.pallas_call(
        join_kernel,
        in_specs=[vmem(), vmem(), hbm()],
        out_specs=hbm(),
        out_shape=pltpu.HBM(grads.shape, BF16),
        input_output_aliases={2: 0},
        scratch_shapes=[
            pltpu.VMEM((HALO, 2, HEAD_DIM, CHUNK), BF16),
            pltpu.SemaphoreType.DMA((2,)),
        ],
        compiler_params=pltpu.CompilerParams(vmem_limit_bytes=40 * MIB),
        name="join",
    )(back, rest, *in_hbm(grads))


def move(copies):
    for copy in copies:
        copy.start()
    for copy in copies:
        copy.wait()


def turn_kernel(back, place_ref, *refs):
    sources, targets, (buffer, fetched, sent) = refs[:4], refs[4:8], refs[8:]
    y = place_ref[1]
    fetches = []
    for d in range(4):
        for e in range(4):
            if back:
                ends = (sources[e].at[d], buffer.at[d, y ^ e])
            else:
                ends = (sources[d].at[y ^ e], buffer.at[e, d])
            fetches.append(pltpu.make_async_copy(*ends, fetched.at[d, e]))
    move(fetches)
    move([pltpu.make_async_copy(buffer.at[e], targets[e], sent.at[e]) for e in range(4)])


def turn(place, parts, back=False):
    return pl.pallas_call(
        functools.partial(turn_kernel, back),
        in_specs=[smem()] + [pl.BlockSpec(memory_space=pl.ANY)] * 4,
        out_specs=[hbm()] * 4,
        out_shape=PARTS,
        scratch_shapes=[
            pltpu.VMEM((4, 4, 2, HEAD_DIM, CHUNK), BF16),
            pltpu.SemaphoreType.DMA((4, 4)),
            pltpu.SemaphoreType.DMA((4,)),
        ],
        compiler_params=pltpu.CompilerParams(vmem_limit_bytes=40 * MIB),
        cost_estimate=cost(1),
        name="turn",
    )(place, *parts)


def pack_cores_kernel(place_ref, source, own_ref, other_ref, rows, blocks, arrived, sent):
    mirrored, y, zl, core = place_ref[0], place_ref[1], place_ref[2], place_ref[3]
    fetches = [
        pltpu.make_async_copy(source.at[:, pl.ds(n * 768, 768)], rows.at[n], arrived.at[n])
        for n in range(4)
    ]
    for copy in fetches:
        copy.start()
    for n in range(4):
        fetches[n].wait()
        turned = rows[n].T
        for head_zl in range(4):
            d = zl ^ jnp.where(mirrored == 1, 3 - head_zl, head_zl)
            for head_core in range(2):
                first = (2 * head_zl + head_core) * HEAD_DIM
                blocks[core ^ head_core, y ^ n, d] = turned[first : first + HEAD_DIM]
    copies = [
        pltpu.make_async_copy(blocks.at[n], ref, sent.at[n])
        for n, ref in enumerate((own_ref, other_ref))
    ]
    for copy in copies:
        copy.start()
    for copy in copies:
        copy.wait()


CORE_SHAPE = (4, 4, HEAD_DIM, CHUNK)


def pack_cores(place, array):
    return pl.pallas_call(
        pack_cores_kernel,
        in_specs=[smem(), hbm()],
        out_specs=[hbm()] * 2,
        out_shape=[pltpu.HBM(CORE_SHAPE, BF16)] * 2,
        scratch_shapes=[
            pltpu.VMEM((4, CHUNK, 768), BF16),
            pltpu.VMEM((2, *CORE_SHAPE), BF16),
            pltpu.SemaphoreType.DMA((4,)),
            pltpu.SemaphoreType.DMA((2,)),
        ],
        compiler_params=pltpu.CompilerParams(vmem_limit_bytes=40 * MIB),
        cost_estimate=cost(1),
        name="pack_cores",
    )(place, *in_hbm(array))


def both_cores_kernel(place_ref, own_ref, other_ref, *refs):
    targets, (buffer, fetched, sent) = refs[:4], refs[4:]
    core = place_ref[3]
    fetches = []
    for e in range(4):
        for n, (ref, side) in enumerate(((own_ref, core), (other_ref, 1 - core))):
            fetches.append(
                pltpu.make_async_copy(ref.at[e], buffer.at[e, :, side], fetched.at[n, e])
            )
    move(fetches)
    move([pltpu.make_async_copy(buffer.at[e], targets[e], sent.at[e]) for e in range(4)])


def both_cores(place, own, other):
    return pl.pallas_call(
        both_cores_kernel,
        in_specs=[smem()] + [pl.BlockSpec(memory_space=pl.ANY)] * 2,
        out_specs=[hbm()] * 4,
        out_shape=PARTS,
        scratch_shapes=[
            pltpu.VMEM((4, 4, 2, HEAD_DIM, CHUNK), BF16),
            pltpu.SemaphoreType.DMA((2, 4)),
            pltpu.SemaphoreType.DMA((4,)),
        ],
        compiler_params=pltpu.CompilerParams(vmem_limit_bytes=40 * MIB),
        cost_estimate=cost(1),
        name="both_cores",
    )(place, own, other)


def to_parts(place, array):
    own, other = pack_cores(place, array)
    other = lax.ppermute(other, "c", [(0, 1), (1, 0)])
    return turn(place, by_distance(both_cores(place, own, other), "y"), back=True)


def other_core_kernel(place_ref, *refs):
    sources, (target, buffer, fetched, sent) = refs[:4], refs[4:]
    move(
        [
            pltpu.make_async_copy(sources[e].at[:, 1 - place_ref[3]], buffer.at[e], fetched.at[e])
            for e in range(4)
        ]
    )
    move([pltpu.make_async_copy(buffer, target, sent)])


def other_core(place, parts):
    return pl.pallas_call(
        other_core_kernel,
        in_specs=[smem()] + [pl.BlockSpec(memory_space=pl.ANY)] * 4,
        out_specs=hbm(),
        out_shape=pltpu.HBM((4, 4, HEAD_DIM, CHUNK), BF16),
        scratch_shapes=[
            pltpu.VMEM((4, 4, HEAD_DIM, CHUNK), BF16),
            pltpu.SemaphoreType.DMA((4,)),
            pltpu.SemaphoreType.DMA(()),
        ],
        compiler_params=pltpu.CompilerParams(vmem_limit_bytes=40 * MIB),
        cost_estimate=cost(1),
        name="other_core",
    )(place, *parts)


def by_distance(parts, axis):
    return [parts[0]] + [
        lax.ppermute(parts[d], axis, [(i, i ^ d) for i in range(4)]) for d in range(1, 4)
    ]


def rows_kernel(place_ref, part_0, part_1, part_2, part_3, other_ref, out_ref, rows, sent):
    mirrored, y, zl, core = place_ref[0], place_ref[1], place_ref[2], place_ref[3]
    copies = []
    for e, ref in enumerate((part_0, part_1, part_2, part_3)):
        pieces = []
        for head_zl in range(4):
            d = zl ^ jnp.where(mirrored == 1, 3 - head_zl, head_zl)
            own, other = ref[d, core], other_ref[e, d]
            pieces.append(jnp.where(core == 0, own, other))
            pieces.append(jnp.where(core == 0, other, own))
        rows[e] = jnp.concatenate(pieces, 0).T
        first = pl.multiple_of((y ^ e) * 768, 768)
        copies.append(
            pltpu.make_async_copy(rows.at[e], out_ref.at[:, pl.ds(first, 768)], sent.at[e])
        )
        copies[e].start()
    for copy in copies:
        copy.wait()


def rows_of(place, parts, other):
    return pl.pallas_call(
        rows_kernel,
        in_specs=[smem()] + [vmem()] * 5,
        out_specs=hbm(),
        out_shape=pltpu.HBM((CHUNK, HEADS * HEAD_DIM), BF16),
        scratch_shapes=[
            pltpu.VMEM((4, CHUNK, 768), BF16),
            pltpu.SemaphoreType.DMA((4,)),
        ],
        compiler_params=pltpu.CompilerParams(vmem_limit_bytes=28 * MIB),
        cost_estimate=cost(1),
        name="rows_of",
    )(place, *parts, other)


def to_rows(place, parts):
    other = lax.ppermute(other_core(place, parts), "c", [(0, 1), (1, 0)])
    return rows_of(place, parts, other)


def gate_kernel(*_):
    pass


def after(arrays, others):
    count = len(arrays)
    return pl.pallas_call(
        gate_kernel,
        in_specs=[hbm()] * count + [pl.BlockSpec(memory_space=pl.ANY)] * len(others),
        out_specs=[hbm()] * count,
        out_shape=[pltpu.HBM(array.shape, array.dtype) for array in arrays],
        input_output_aliases={n: n for n in range(count)},
        name="after",
    )(*arrays, *others)


def group_pairs():
    def index(x, zh, y, zl, c):
        return (((x * 2 + zh) * 4 + y) * 4 + zl) * 2 + c

    pairs = []
    for group in range(7):
        for y in range(4):
            for zl in range(4):
                for c in range(2):
                    pairs.append(
                        (
                            index(group // 2, group % 2, y, zl, c),
                            index((group + 1) // 2, (group + 1) % 2, y, 3 - zl, c),
                        )
                    )
    return pairs


def to_heads(array):
    return lax.all_to_all(array, GROUP_AXES, split_axis=0, concat_axis=0, tiled=True)


def places(doc_ids):
    group = lax.axis_index("x") * 2 + lax.axis_index("zh")
    own = lax.dynamic_slice_in_dim(doc_ids, group * GROUP, GROUP)
    ahead = lax.dynamic_slice_in_dim(doc_ids, jnp.maximum(group * GROUP - AHEAD, 0), AHEAD)
    ahead = jnp.where(group > 0, ahead, -1)
    docs = jnp.concatenate([ahead, own])
    leads = own.reshape(TILES, TILE)[:, :1]
    tile_start = jnp.sum((docs[None] < leads).astype(jnp.int32), 1) // TILE
    row = jnp.arange(EXTRA, dtype=jnp.int32)[:, None]
    bits = (docs[None] >> (row // 2)) & 1
    coded = row < 2 * DOC_BITS
    differs = (bits != row % 2) | (docs[None] < 0)
    key_code = jnp.where(coded, jnp.where(differs, -FAR, 0.0), jnp.where(row < 15, -1.0, 0.0))
    query_code = jnp.where(coded & (bits[:, AHEAD:] == row % 2), 1.0, 0.0)
    query_code = query_code.reshape(EXTRA, TILES, TILE).transpose(1, 0, 2)
    return tile_start, (key_code.astype(BF16), query_code.astype(BF16))


def shards(queries, keys, values, cotangent, doc_ids):
    place = jnp.stack([lax.axis_index(axis) for axis in ("zh", "y", "zl", "c")]).astype(jnp.int32)
    mirror = place[:1]
    kvq = to_heads(pack(mirror, keys, values, queries))
    tile_start, codes = places(doc_ids)
    cotangent, tile_start, codes = lax.optimization_barrier((cotangent, tile_start, codes))
    pairs = group_pairs()
    last = kvq[CHUNKS - HALO :, :2]
    halo = lax.ppermute(last, AXES, pairs)
    g = by_distance(after(to_parts(place, cotangent), [last]), "zl")
    *out, stat = late_forward(place, tile_start, codes, kvq)
    *out, early_stat = early_forward(place, tile_start, codes, kvq, halo, out)
    back, carry, early_q = early_backward(
        place, tile_start, codes, kvq, halo, early_stat, g, out
    )
    grads, rest, *grad_q = late_backward(
        place, tile_start, codes, kvq, stat, g, out, carry, early_q
    )
    out = by_distance(out, "zl")
    grad_q = by_distance(after(grad_q, out[1:]), "zl")
    out = by_distance(turn(place, out), "y")
    back = lax.ppermute(back, AXES, [(b, a) for a, b in pairs])
    (grads,) = after([join(back, rest, grads)], grad_q[1:] + out[1:])
    attended = to_rows(place, out)
    grad_q = to_rows(place, by_distance(turn(place, grad_q), "y"))
    grad_k, grad_v = unpack(mirror, to_heads(grads))
    return attended, grad_q, grad_k, grad_v


def solution(mesh):
    wide = Mesh(mesh.devices.reshape(4, 2, 4, 4, 2), AXES)
    rows = P(AXES, None)
    return jax.shard_map(
        shards,
        mesh=wide,
        in_specs=(rows, rows, rows, rows, P()),
        out_specs=(rows, rows, rows, rows),
        check_vma=False,
    )
```

```python
import functools
import math

import jax
import jax.numpy as jnp
from jax import lax
from jax.experimental import pallas as pl
from jax.experimental.pallas import tpu as pltpu
from jax.sharding import Mesh
from jax.sharding import PartitionSpec as P

HEAD_DIM = 96
HEADS = 32
CHUNK = 128
CHUNKS = 32
HALO = 8
DOC_BITS = 6
EXTRA = 16
WIDE = HEAD_DIM + EXTRA
FAR = 2.0**20
GROUP = CHUNK * CHUNKS
AHEAD = CHUNK * HALO
WINDOW = GROUP + AHEAD
TILE = 256
TILES = GROUP // TILE
BLOCKS = CHUNKS // HALO
AHEAD_TILES = AHEAD // TILE
REACH = AHEAD_TILES + 1
NEG = -1e30
SCALE = 1.0 / math.sqrt(HEAD_DIM)
LOG2E = 1.4426950408889634
MIB = 1024 * 1024

AXES = ("x", "zh", "y", "zl", "c")
GROUP_AXES = ("y", "zl", "c")
F32 = jnp.float32
BF16 = jnp.bfloat16


def vmem():
    return pl.BlockSpec(memory_space=pltpu.VMEM)


def smem():
    return pl.BlockSpec(memory_space=pltpu.SMEM)


def hbm():
    return pl.BlockSpec(memory_space=pltpu.HBM)


def in_hbm(*arrays):
    return [pltpu.with_memory_space_constraint(array, pltpu.HBM) for array in arrays]


def pack_kernel(mirror_ref, *refs):
    count = len(refs) - 5
    sources, (out_ref, rows, blocks, arrived, sent) = refs[:count], refs[count:]
    mirrored = mirror_ref[0]

    def fetch(y, n):
        return pltpu.make_async_copy(
            sources[n].at[:, pl.ds(y * 768, 768)], rows.at[n, y], arrived.at[n, y]
        )

    def send(y):
        part = pl.ds(y * 8, 8)
        return pltpu.make_async_copy(blocks.at[part], out_ref.at[part], sent.at[y])

    for y in range(4):
        for n in range(count):
            fetch(y, n).start()
    for y in range(4):
        for n in range(count):
            fetch(y, n).wait()
            turned = rows[n, y].T
            for zl in range(4):
                slot = 8 * y + 2 * jnp.where(mirrored == 1, 3 - zl, zl)
                piece = turned[zl * 192 : (zl + 1) * 192]
                blocks[pl.ds(slot, 2), n] = piece.reshape(2, HEAD_DIM, CHUNK)
        send(y).start()
    for y in range(4):
        send(y).wait()


def pack(mirror, *arrays):
    count = len(arrays)
    shape = (HEADS, count, HEAD_DIM, CHUNK)
    return pl.pallas_call(
        pack_kernel,
        in_specs=[smem()] + [hbm()] * count,
        out_specs=hbm(),
        out_shape=pltpu.HBM(shape, BF16),
        scratch_shapes=[
            pltpu.VMEM((count, 4, CHUNK, 768), BF16),
            pltpu.VMEM(shape, BF16),
            pltpu.SemaphoreType.DMA((count, 4)),
            pltpu.SemaphoreType.DMA((4,)),
        ],
        compiler_params=pltpu.CompilerParams(vmem_limit_bytes=40 * MIB),
        name="pack",
    )(mirror, *in_hbm(*arrays))


def unpack_kernel(mirror_ref, in_ref, *out_refs):
    mirrored = mirror_ref[0]
    for n, out_ref in enumerate(out_refs):
        pieces = []
        for zl in range(4):
            slot = 2 * jnp.where(mirrored == 1, 3 - zl, zl)
            pieces.append(in_ref[pl.ds(slot, 2), n].reshape(192, CHUNK))
        out_ref[...] = jnp.concatenate(pieces, 0).T


def unpack(mirror, array):
    count = array.shape[1]
    return pl.pallas_call(
        unpack_kernel,
        grid=(4,),
        in_specs=[
            smem(),
            pl.BlockSpec((8, count, HEAD_DIM, CHUNK), lambda y: (y, 0, 0, 0)),
        ],
        out_specs=[pl.BlockSpec((CHUNK, 768), lambda y: (0, y))] * count,
        out_shape=[jax.ShapeDtypeStruct((CHUNK, HEADS * HEAD_DIM), BF16)] * count,
        compiler_params=pltpu.CompilerParams(vmem_limit_bytes=28 * MIB),
        name="unpack",
    )(mirror, array)


def tile_of(ref, i):
    return jnp.concatenate([ref[2 * i], ref[2 * i + 1]], 1)


def nn(a, b):
    return lax.dot_general(a, b, (((1,), (0,)), ((), ())), preferred_element_type=F32)


def nt(a, b):
    return lax.dot_general(a, b, (((1,), (1,)), ((), ())), preferred_element_type=F32)


def each_chunk(halo_ref, own_ref, n, chunks):
    for chunk in chunks:
        piece = halo_ref[chunk, n] if chunk < HALO else own_ref[chunk - HALO, n]
        yield slice(chunk * CHUNK, (chunk + 1) * CHUNK), piece


def fill_keys(halo_ref, own_ref, code_ref, chunks, flat, turned):
    for span, piece in each_chunk(halo_ref, own_ref, 0, chunks):
        flat[span, :] = jnp.concatenate([piece, code_ref[:, span]], 0).T
        if turned is not None:
            turned[:, span] = piece


def fill_value_rows(halo_ref, own_ref, chunks, flat):
    row = lax.broadcasted_iota(jnp.int32, (EXTRA, CHUNK), 0)
    minus = jnp.where(row < 3, -1.0, 0.0).astype(BF16)
    for span, piece in each_chunk(halo_ref, own_ref, 1, chunks):
        flat[span, :] = jnp.concatenate([piece, minus], 0).T


def fill_value_columns(halo_ref, own_ref, chunks, turned):
    for span, piece in each_chunk(halo_ref, own_ref, 1, chunks):
        turned[:HEAD_DIM, span] = piece
        turned[HEAD_DIM:, span] = jnp.ones((EXTRA, CHUNK), BF16)


def with_row(extra, first, value):
    high = value.astype(BF16).astype(F32)
    middle = (value - high).astype(BF16).astype(F32)
    low = value - high - middle
    row = lax.broadcasted_iota(jnp.int32, (EXTRA, TILE), 0)
    for n, part in enumerate((high, middle, low)):
        extra = jnp.where(row == first + n, part, extra)
    return extra.astype(BF16)


def causal():
    row = lax.broadcasted_iota(jnp.int32, (TILE, TILE), 0)
    return row <= lax.broadcasted_iota(jnp.int32, (TILE, TILE), 1)


def per_tile(tile_start_ref, i, body):
    reach = jnp.clip(i + REACH - tile_start_ref[i], 1, REACH)
    for count in range(1, REACH + 1):
        pl.when(reach == count)(functools.partial(body, count))


def send_block(buffer, out_ref, sent, block):
    part = pl.ds(block * HALO, HALO)
    return pltpu.make_async_copy(buffer.at[part], out_ref.at[part], sent.at[block])


def forward_tiles(
    block, tile_start_ref, query_code_ref, q_ref, store, stat_ref, key_flat, value_turned
):
    def tile(step, _):
        i = block * AHEAD_TILES + step

        def body(count):
            q = jnp.concatenate([tile_of(q_ref, i), query_code_ref[i]], 0)
            scores = []
            top = None
            for j in range(count):
                first = pl.multiple_of((i + REACH - count + j) * TILE, TILE)
                s = nn(key_flat[pl.ds(first, TILE), :], q)
                if j == count - 1:
                    s = jnp.where(causal(), s, NEG)
                scores.append(s)
                t = jnp.max(s, axis=0, keepdims=True)
                top = t if top is None else jnp.maximum(top, t)
            shift = top * (SCALE * LOG2E)
            out = None
            for j in range(count):
                first = pl.multiple_of((i + REACH - count + j) * TILE, TILE)
                e = jnp.exp2(scores[j] * (SCALE * LOG2E) - shift)
                o = nn(value_turned[:, pl.ds(first, TILE)], e.astype(BF16))
                out = o if out is None else out + o
            total = out[HEAD_DIM : HEAD_DIM + 1]
            out = (out[:HEAD_DIM] / total).astype(BF16)
            store(2 * i, out[:, :CHUNK])
            store(2 * i + 1, out[:, CHUNK:])
            stat_ref[i] = top + jnp.log(total) * (1.0 / SCALE)

        per_tile(tile_start_ref, i, body)
        return 0

    lax.fori_loop(0, AHEAD_TILES, tile, 0)


def part_copies(place_ref, buffer, parts, b, sems, fetch=False):
    copies = []
    for d, ref in enumerate(parts):
        here = buffer.at[pl.ds(b * HALO + 2 * (place_ref[2] ^ d), 2)]
        there = ref.at[b]
        ends = (there, here) if fetch else (here, there)
        copies.append(pltpu.make_async_copy(*ends, sems.at[b, d]))
    return copies


def late_forward_kernel(
    place_ref, tile_start_ref, key_code_ref, query_code_ref, kv_ref, q_0, q_1, q_2, q_3,
    part_0, part_1, part_2, part_3, stat_ref, key_flat, value_turned, buffer, queries,
    sent, fetched_q
):
    parts = (part_0, part_1, part_2, part_3)

    def fetch(b):
        return part_copies(place_ref, queries, (q_0, q_1, q_2, q_3), b, fetched_q, True)

    for b in range(1, BLOCKS):
        for copy in fetch(b):
            copy.start()
    chunks = range(HALO, HALO + CHUNKS)
    fill_keys(None, kv_ref, key_code_ref, chunks, key_flat, None)
    fill_value_columns(None, kv_ref, chunks, value_turned)

    def store(chunk, value):
        buffer[chunk] = value

    def block(b, _):
        for copy in fetch(b):
            copy.wait()
        forward_tiles(
            b, tile_start_ref, query_code_ref, queries, store, stat_ref, key_flat, value_turned
        )
        for copy in part_copies(place_ref, buffer, parts, b, sent):
            copy.start()
        return 0

    lax.fori_loop(1, BLOCKS, block, 0)
    for b in range(1, BLOCKS):
        for copy in part_copies(place_ref, buffer, parts, b, sent):
            copy.wait()


def cost(time):
    return pl.CostEstimate(flops=int(time * 1.1e9), bytes_accessed=0, transcendentals=0)


PARTS = [pltpu.HBM((4, 2, HEAD_DIM, CHUNK), BF16)] * 4


def part(count, width):
    return pl.BlockSpec((count, width, HEAD_DIM, CHUNK), lambda b: (0, 0, 0, 0))


def forward_scratch(window, chunks):
    return [
        pltpu.VMEM((window, WIDE), BF16),
        pltpu.VMEM((WIDE, window), BF16),
        pltpu.VMEM((chunks, HEAD_DIM, CHUNK), BF16),
        pltpu.VMEM((chunks, HEAD_DIM, CHUNK), BF16),
        pltpu.SemaphoreType.DMA((BLOCKS, 4)),
        pltpu.SemaphoreType.DMA((BLOCKS, 4)),
    ]


def late_forward(place, tile_start, codes, kv, q):
    return pl.pallas_call(
        late_forward_kernel,
        in_specs=[smem(), smem(), vmem(), vmem(), vmem()] + [hbm()] * 4,
        out_specs=[hbm()] * 4 + [vmem()],
        out_shape=PARTS + [jax.ShapeDtypeStruct((TILES, 1, TILE), F32)],
        scratch_shapes=forward_scratch(WINDOW, CHUNKS),
        compiler_params=pltpu.CompilerParams(vmem_limit_bytes=40 * MIB),
        cost_estimate=cost(30),
        name="late_forward",
    )(place, tile_start, *codes, kv, *in_hbm(*q))


def backward_tiles(
    low, high, tile_start_ref, query_code_ref, q_ref, g_ref, out_ref, stat_ref, store,
    key_flat, key_turned, value_flat, key_sum, value_sum
):
    def tile(i, _):
        def body(count):
            q = tile_of(q_ref, i)
            g = tile_of(g_ref, i)
            o = tile_of(out_ref, i)
            delta = jnp.sum(o.astype(F32) * g.astype(F32), axis=0, keepdims=True)
            stat = stat_ref[i]
            code = query_code_ref[i].astype(F32)
            q_wide = jnp.concatenate([q, with_row(code, 2 * DOC_BITS, stat)], 0)
            g_wide = jnp.concatenate([g, with_row(jnp.zeros_like(code), 0, delta)], 0)
            first = pl.multiple_of((i + REACH - count) * TILE, TILE)
            span = pl.ds(first, count * TILE)
            p = jnp.exp2(nn(key_flat[span, :], q_wide) * (SCALE * LOG2E))
            last = (count - 1) * TILE
            tail = jnp.where(causal(), p[last:], 0.0)
            p = jnp.concatenate([p[:last], tail], 0) if last else tail
            d = (p * nn(value_flat[span, :], g_wide)).astype(BF16)
            grad_q = nn(key_turned[:, span], d)
            key_sum[:, span] += nt(q, d)
            value_sum[:, span] += nt(g, p.astype(BF16))
            grad_q = (grad_q * SCALE).astype(BF16)
            store(2 * i, grad_q[:, :CHUNK])
            store(2 * i + 1, grad_q[:, CHUNK:])

        per_tile(tile_start_ref, i, body)
        return 0

    lax.fori_loop(low, high, tile, 0)


def early_forward_kernel(
    place_ref, tile_start_ref, key_code_ref, query_code_ref, kv_ref, halo_ref,
    q_0, q_1, q_2, q_3, _, __, ___, ____,
    part_0, part_1, part_2, part_3, stat_ref, key_flat, value_turned, buffer, queries,
    sent, fetched_q
):
    fetches = part_copies(place_ref, queries, (q_0, q_1, q_2, q_3), 0, fetched_q, True)
    for copy in fetches:
        copy.start()
    fill_keys(halo_ref, kv_ref, key_code_ref, range(2 * HALO), key_flat, None)
    fill_value_columns(halo_ref, kv_ref, range(2 * HALO), value_turned)
    for copy in fetches:
        copy.wait()

    def store(chunk, value):
        buffer[chunk] = value

    forward_tiles(
        0, tile_start_ref, query_code_ref, queries, store, stat_ref, key_flat, value_turned
    )
    copies = part_copies(place_ref, buffer, (part_0, part_1, part_2, part_3), 0, sent)
    for copy in copies:
        copy.start()
    for copy in copies:
        copy.wait()


def early_backward_kernel(
    place_ref, tile_start_ref, key_code_ref, query_code_ref, kv_ref, halo_ref, stat_ref,
    q_0, q_1, q_2, q_3, g_0, g_1, g_2, g_3, out_0, out_1, out_2, out_3,
    back_ref, carry_ref, grad_q_ref,
    key_flat, key_turned, value_flat, key_sum, value_sum, q_part, g_part, out_part, back_part,
    grad_q_part, sent, fetched_q, fetched_g, fetched_out
):
    fetches = part_copies(place_ref, q_part, (q_0, q_1, q_2, q_3), 0, fetched_q, True)
    fetches += part_copies(place_ref, g_part, (g_0, g_1, g_2, g_3), 0, fetched_g, True)
    fetches += part_copies(place_ref, out_part, (out_0, out_1, out_2, out_3), 0, fetched_out, True)
    for copy in fetches:
        copy.start()
    fill_keys(halo_ref, kv_ref, key_code_ref, range(2 * HALO), key_flat, key_turned)
    fill_value_rows(halo_ref, kv_ref, range(2 * HALO), value_flat)
    key_sum[...] = jnp.zeros_like(key_sum)
    value_sum[...] = jnp.zeros_like(value_sum)
    for copy in fetches:
        copy.wait()

    def store(chunk, value):
        grad_q_part[chunk] = value

    backward_tiles(
        0, AHEAD_TILES, tile_start_ref, query_code_ref, q_part, g_part, out_part, stat_ref, store,
        key_flat, key_turned, value_flat, key_sum, value_sum
    )
    copies = [pltpu.make_async_copy(grad_q_part, grad_q_ref, sent.at[2])]
    for n, sums in enumerate((key_sum, value_sum)):
        copies.append(
            pltpu.make_async_copy(
                sums.at[:, pl.ds(AHEAD, AHEAD)], carry_ref.at[n], sent.at[3 + n]
            )
        )
    for copy in copies:
        copy.start()
    for n, (sums, factor) in enumerate(((key_sum, SCALE), (value_sum, 1.0))):
        for chunk in range(HALO):
            piece = sums[:, chunk * CHUNK : (chunk + 1) * CHUNK] * factor
            back_part[chunk, n] = piece.astype(BF16)
    back_copy = pltpu.make_async_copy(back_part, back_ref, sent.at[5])
    back_copy.start()
    for copy in (*copies, back_copy):
        copy.wait()


def late_backward_kernel(
    place_ref, tile_start_ref, key_code_ref, query_code_ref, kv_ref, stat_ref,
    q_0, q_1, q_2, q_3, g_0, g_1, g_2, g_3, out_0, out_1, out_2, out_3, carry_ref, grad_q_ref, grads_ref, rest_ref, part_0, part_1, part_2, part_3,
    key_flat, key_turned, value_flat, key_sum, value_sum, buffer, queries, q_all, g_all,
    out_all, carry, sent, fetched, parted, fetched_q, fetched_g, fetched_out
):
    def fetch(b):
        return part_copies(
            place_ref, q_all, (q_0, q_1, q_2, q_3), b, fetched_q, True
        ) + part_copies(place_ref, g_all, (g_0, g_1, g_2, g_3), b, fetched_g, True) + part_copies(place_ref, out_all, (out_0, out_1, out_2, out_3), b, fetched_out, True)

    first = (
        pltpu.make_async_copy(carry_ref, carry, fetched.at[0]),
        pltpu.make_async_copy(grad_q_ref, queries.at[pl.ds(0, HALO)], fetched.at[1]),
    )
    for copy in (*fetch(1), *first, *fetch(2), *fetch(3)):
        copy.start()
    chunks = range(HALO, HALO + CHUNKS)
    fill_keys(None, kv_ref, key_code_ref, chunks, key_flat, key_turned)
    fill_value_rows(None, kv_ref, chunks, value_flat)
    for sums in (key_sum, value_sum):
        sums[:, AHEAD:] = jnp.zeros((HEAD_DIM, GROUP), F32)

    def store(chunk, value):
        queries[chunk] = value

    def send_queries(b):
        return part_copies(place_ref, queries, (part_0, part_1, part_2, part_3), b, parted)

    def block(b, _):
        for copy in fetch(b):
            copy.wait()
        backward_tiles(
            b * AHEAD_TILES, (b + 1) * AHEAD_TILES,
            tile_start_ref, query_code_ref, q_all, g_all, out_all, stat_ref, store,
            key_flat, key_turned, value_flat, key_sum, value_sum
        )

        @pl.when(b == 1)
        def _():
            for copy in first:
                copy.wait()
            for copy in send_queries(0):
                copy.start()
            key_sum[:, AHEAD : 2 * AHEAD] += carry[0]
            value_sum[:, AHEAD : 2 * AHEAD] += carry[1]

        for n, (sums, factor) in enumerate(((key_sum, SCALE), (value_sum, 1.0))):
            for chunk in range(HALO):
                place = pl.multiple_of(b * AHEAD + chunk * CHUNK, CHUNK)
                piece = sums[:, pl.ds(place, CHUNK)] * factor
                buffer[(b - 1) * HALO + chunk, n] = piece.astype(BF16)
        send_block(buffer, grads_ref, sent, b - 1).start()
        for copy in send_queries(b):
            copy.start()
        return 0

    lax.fori_loop(1, BLOCKS, block, 0)
    for n, sums in enumerate((key_sum, value_sum)):
        rest_ref[n] = sums[:, GROUP:]
    for b in range(BLOCKS - 1):
        send_block(buffer, grads_ref, sent, b).wait()
    for b in range(BLOCKS):
        for copy in send_queries(b):
            copy.wait()


def sums_scratch(window):
    return [
        pltpu.VMEM((window, WIDE), BF16),
        pltpu.VMEM((HEAD_DIM, window), BF16),
        pltpu.VMEM((window, WIDE), BF16),
        pltpu.VMEM((HEAD_DIM, window), F32),
        pltpu.VMEM((HEAD_DIM, window), F32),
    ]


def early_forward(place, tile_start, codes, kv, halo, q, parts):
    return pl.pallas_call(
        early_forward_kernel,
        grid=(1,),
        in_specs=[smem(), smem(), vmem(), vmem(), part(HALO, 2), vmem()] + [hbm()] * 8,
        out_specs=[hbm()] * 4 + [vmem()],
        out_shape=PARTS + [jax.ShapeDtypeStruct((AHEAD_TILES, 1, TILE), F32)],
        input_output_aliases={10 + d: d for d in range(4)},
        scratch_shapes=forward_scratch(2 * AHEAD, HALO),
        compiler_params=pltpu.CompilerParams(vmem_limit_bytes=40 * MIB),
        cost_estimate=cost(1),
        name="early_forward",
    )(place, tile_start, *codes, kv, halo, *in_hbm(*q, *parts))


def early_backward(place, tile_start, codes, kv, halo, stat, q, g, out):
    return pl.pallas_call(
        early_backward_kernel,
        grid=(1,),
        in_specs=[smem(), smem(), vmem(), vmem(), part(HALO, 2), vmem(), vmem()] + [hbm()] * 12,
        out_specs=[hbm()] * 3,
        out_shape=[
            pltpu.HBM((HALO, 2, HEAD_DIM, CHUNK), BF16),
            pltpu.HBM((2, HEAD_DIM, AHEAD), F32),
            pltpu.HBM((HALO, HEAD_DIM, CHUNK), BF16),
        ],
        scratch_shapes=sums_scratch(2 * AHEAD)
        + [
            pltpu.VMEM((HALO, HEAD_DIM, CHUNK), BF16),
            pltpu.VMEM((HALO, HEAD_DIM, CHUNK), BF16),
            pltpu.VMEM((HALO, HEAD_DIM, CHUNK), BF16),
            pltpu.VMEM((HALO, 2, HEAD_DIM, CHUNK), BF16),
            pltpu.VMEM((HALO, HEAD_DIM, CHUNK), BF16),
            pltpu.SemaphoreType.DMA((6,)),
            pltpu.SemaphoreType.DMA((1, 4)),
            pltpu.SemaphoreType.DMA((1, 4)),
            pltpu.SemaphoreType.DMA((1, 4)),
        ],
        compiler_params=pltpu.CompilerParams(vmem_limit_bytes=40 * MIB),
        cost_estimate=cost(1),
        name="early_backward",
    )(place, tile_start, *codes, kv, halo, stat, *in_hbm(*q, *g, *out))


def late_backward(place, tile_start, codes, kv, stat, q, g, out, carry, grad_q):
    return pl.pallas_call(
        late_backward_kernel,
        in_specs=[smem(), smem(), vmem(), vmem(), vmem(), vmem()] + [hbm()] * 14,
        out_specs=[hbm(), vmem()] + [hbm()] * 4,
        out_shape=[
            pltpu.HBM((CHUNKS, 2, HEAD_DIM, CHUNK), BF16),
            jax.ShapeDtypeStruct((2, HEAD_DIM, AHEAD), F32),
        ]
        + [pltpu.HBM((4, 2, HEAD_DIM, CHUNK), BF16)] * 4,
        scratch_shapes=sums_scratch(WINDOW)
        + [
            pltpu.VMEM((CHUNKS, 2, HEAD_DIM, CHUNK), BF16),
            pltpu.VMEM((CHUNKS, HEAD_DIM, CHUNK), BF16),
            pltpu.VMEM((CHUNKS, HEAD_DIM, CHUNK), BF16),
            pltpu.VMEM((CHUNKS, HEAD_DIM, CHUNK), BF16),
            pltpu.VMEM((CHUNKS, HEAD_DIM, CHUNK), BF16),
            pltpu.VMEM((2, HEAD_DIM, AHEAD), F32),
            pltpu.SemaphoreType.DMA((BLOCKS,)),
            pltpu.SemaphoreType.DMA((2,)),
            pltpu.SemaphoreType.DMA((BLOCKS, 4)),
            pltpu.SemaphoreType.DMA((BLOCKS, 4)),
            pltpu.SemaphoreType.DMA((BLOCKS, 4)),
            pltpu.SemaphoreType.DMA((BLOCKS, 4)),
        ],
        compiler_params=pltpu.CompilerParams(vmem_limit_bytes=40 * MIB),
        cost_estimate=cost(10),
        name="late_backward",
    )(place, tile_start, *codes, kv, stat, *in_hbm(*q, *g, *out, carry, grad_q))


def join_kernel(back_ref, rest_ref, _, out_ref, buffer, moved):
    sends = []
    for n, factor in enumerate((SCALE, 1.0)):
        for chunk in range(HALO):
            own = rest_ref[n, :, chunk * CHUNK : (chunk + 1) * CHUNK] * factor
            buffer[chunk, n] = (own + back_ref[chunk, n].astype(F32)).astype(BF16)
        target = out_ref.at[pl.ds(CHUNKS - HALO, HALO), n]
        sends.append(pltpu.make_async_copy(buffer.at[:, n], target, moved.at[n]))
        sends[n].start()
    for copy in sends:
        copy.wait()


def join(back, rest, grads):
    return pl.pallas_call(
        join_kernel,
        in_specs=[vmem(), vmem(), hbm()],
        out_specs=hbm(),
        out_shape=pltpu.HBM(grads.shape, BF16),
        input_output_aliases={2: 0},
        scratch_shapes=[
            pltpu.VMEM((HALO, 2, HEAD_DIM, CHUNK), BF16),
            pltpu.SemaphoreType.DMA((2,)),
        ],
        compiler_params=pltpu.CompilerParams(vmem_limit_bytes=40 * MIB),
        name="join",
    )(back, rest, *in_hbm(grads))


def move(copies):
    for copy in copies:
        copy.start()
    for copy in copies:
        copy.wait()


def turn_kernel(back, place_ref, *refs):
    sources, targets, (buffer, fetched, sent) = refs[:4], refs[4:8], refs[8:]
    y = place_ref[1]
    fetches = []
    for d in range(4):
        for e in range(4):
            if back:
                ends = (sources[e].at[d], buffer.at[d, y ^ e])
            else:
                ends = (sources[d].at[y ^ e], buffer.at[e, d])
            fetches.append(pltpu.make_async_copy(*ends, fetched.at[d, e]))
    move(fetches)
    move([pltpu.make_async_copy(buffer.at[e], targets[e], sent.at[e]) for e in range(4)])


def turn(place, parts, back=False):
    return pl.pallas_call(
        functools.partial(turn_kernel, back),
        in_specs=[smem()] + [pl.BlockSpec(memory_space=pl.ANY)] * 4,
        out_specs=[hbm()] * 4,
        out_shape=PARTS,
        scratch_shapes=[
            pltpu.VMEM((4, 4, 2, HEAD_DIM, CHUNK), BF16),
            pltpu.SemaphoreType.DMA((4, 4)),
            pltpu.SemaphoreType.DMA((4,)),
        ],
        compiler_params=pltpu.CompilerParams(vmem_limit_bytes=40 * MIB),
        cost_estimate=cost(1),
        name="turn",
    )(place, *parts)


def pack_cores_kernel(place_ref, source, own_ref, other_ref, rows, blocks, arrived, sent):
    mirrored, y, zl, core = place_ref[0], place_ref[1], place_ref[2], place_ref[3]
    fetches = [
        pltpu.make_async_copy(source.at[:, pl.ds(n * 768, 768)], rows.at[n], arrived.at[n])
        for n in range(4)
    ]
    for copy in fetches:
        copy.start()
    for n in range(4):
        fetches[n].wait()
        turned = rows[n].T
        for head_zl in range(4):
            d = zl ^ jnp.where(mirrored == 1, 3 - head_zl, head_zl)
            for head_core in range(2):
                first = (2 * head_zl + head_core) * HEAD_DIM
                blocks[core ^ head_core, y ^ n, d] = turned[first : first + HEAD_DIM]
    copies = [
        pltpu.make_async_copy(blocks.at[n], ref, sent.at[n])
        for n, ref in enumerate((own_ref, other_ref))
    ]
    for copy in copies:
        copy.start()
    for copy in copies:
        copy.wait()


CORE_SHAPE = (4, 4, HEAD_DIM, CHUNK)


def pack_cores(place, array):
    return pl.pallas_call(
        pack_cores_kernel,
        in_specs=[smem(), hbm()],
        out_specs=[hbm()] * 2,
        out_shape=[pltpu.HBM(CORE_SHAPE, BF16)] * 2,
        scratch_shapes=[
            pltpu.VMEM((4, CHUNK, 768), BF16),
            pltpu.VMEM((2, *CORE_SHAPE), BF16),
            pltpu.SemaphoreType.DMA((4,)),
            pltpu.SemaphoreType.DMA((2,)),
        ],
        compiler_params=pltpu.CompilerParams(vmem_limit_bytes=40 * MIB),
        cost_estimate=cost(1),
        name="pack_cores",
    )(place, *in_hbm(array))


def both_cores_kernel(place_ref, own_ref, other_ref, *refs):
    targets, (buffer, fetched, sent) = refs[:4], refs[4:]
    core = place_ref[3]
    fetches = []
    for e in range(4):
        for n, (ref, side) in enumerate(((own_ref, core), (other_ref, 1 - core))):
            fetches.append(
                pltpu.make_async_copy(ref.at[e], buffer.at[e, :, side], fetched.at[n, e])
            )
    move(fetches)
    move([pltpu.make_async_copy(buffer.at[e], targets[e], sent.at[e]) for e in range(4)])


def both_cores(place, own, other):
    return pl.pallas_call(
        both_cores_kernel,
        in_specs=[smem()] + [pl.BlockSpec(memory_space=pl.ANY)] * 2,
        out_specs=[hbm()] * 4,
        out_shape=PARTS,
        scratch_shapes=[
            pltpu.VMEM((4, 4, 2, HEAD_DIM, CHUNK), BF16),
            pltpu.SemaphoreType.DMA((2, 4)),
            pltpu.SemaphoreType.DMA((4,)),
        ],
        compiler_params=pltpu.CompilerParams(vmem_limit_bytes=40 * MIB),
        cost_estimate=cost(1),
        name="both_cores",
    )(place, own, other)


def to_parts(place, array):
    own, other = pack_cores(place, array)
    other = lax.ppermute(other, "c", [(0, 1), (1, 0)])
    return turn(place, by_distance(both_cores(place, own, other), "y"), back=True)


def other_core_kernel(place_ref, *refs):
    sources, (target, buffer, fetched, sent) = refs[:4], refs[4:]
    move(
        [
            pltpu.make_async_copy(sources[e].at[:, 1 - place_ref[3]], buffer.at[e], fetched.at[e])
            for e in range(4)
        ]
    )
    move([pltpu.make_async_copy(buffer, target, sent)])


def other_core(place, parts):
    return pl.pallas_call(
        other_core_kernel,
        in_specs=[smem()] + [pl.BlockSpec(memory_space=pl.ANY)] * 4,
        out_specs=hbm(),
        out_shape=pltpu.HBM((4, 4, HEAD_DIM, CHUNK), BF16),
        scratch_shapes=[
            pltpu.VMEM((4, 4, HEAD_DIM, CHUNK), BF16),
            pltpu.SemaphoreType.DMA((4,)),
            pltpu.SemaphoreType.DMA(()),
        ],
        compiler_params=pltpu.CompilerParams(vmem_limit_bytes=40 * MIB),
        cost_estimate=cost(1),
        name="other_core",
    )(place, *parts)


def by_distance(parts, axis):
    return [parts[0]] + [
        lax.ppermute(parts[d], axis, [(i, i ^ d) for i in range(4)]) for d in range(1, 4)
    ]


def rows_kernel(place_ref, part_0, part_1, part_2, part_3, other_ref, out_ref, rows, sent):
    mirrored, y, zl, core = place_ref[0], place_ref[1], place_ref[2], place_ref[3]
    copies = []
    for e, ref in enumerate((part_0, part_1, part_2, part_3)):
        pieces = []
        for head_zl in range(4):
            d = zl ^ jnp.where(mirrored == 1, 3 - head_zl, head_zl)
            own, other = ref[d, core], other_ref[e, d]
            pieces.append(jnp.where(core == 0, own, other))
            pieces.append(jnp.where(core == 0, other, own))
        rows[e] = jnp.concatenate(pieces, 0).T
        first = pl.multiple_of((y ^ e) * 768, 768)
        copies.append(
            pltpu.make_async_copy(rows.at[e], out_ref.at[:, pl.ds(first, 768)], sent.at[e])
        )
        copies[e].start()
    for copy in copies:
        copy.wait()


def rows_of(place, parts, other):
    return pl.pallas_call(
        rows_kernel,
        in_specs=[smem()] + [vmem()] * 5,
        out_specs=hbm(),
        out_shape=pltpu.HBM((CHUNK, HEADS * HEAD_DIM), BF16),
        scratch_shapes=[
            pltpu.VMEM((4, CHUNK, 768), BF16),
            pltpu.SemaphoreType.DMA((4,)),
        ],
        compiler_params=pltpu.CompilerParams(vmem_limit_bytes=28 * MIB),
        cost_estimate=cost(1),
        name="rows_of",
    )(place, *parts, other)


def to_rows(place, parts):
    other = lax.ppermute(other_core(place, parts), "c", [(0, 1), (1, 0)])
    return rows_of(place, parts, other)


def gate_kernel(*_):
    pass


def after(arrays, others):
    count = len(arrays)
    return pl.pallas_call(
        gate_kernel,
        in_specs=[hbm()] * count + [pl.BlockSpec(memory_space=pl.ANY)] * len(others),
        out_specs=[hbm()] * count,
        out_shape=[pltpu.HBM(array.shape, array.dtype) for array in arrays],
        input_output_aliases={n: n for n in range(count)},
        name="after",
    )(*arrays, *others)


def group_pairs():
    def index(x, zh, y, zl, c):
        return (((x * 2 + zh) * 4 + y) * 4 + zl) * 2 + c

    pairs = []
    for group in range(7):
        for y in range(4):
            for zl in range(4):
                for c in range(2):
                    pairs.append(
                        (
                            index(group // 2, group % 2, y, zl, c),
                            index((group + 1) // 2, (group + 1) % 2, y, 3 - zl, c),
                        )
                    )
    return pairs


def to_heads(array):
    return lax.all_to_all(array, GROUP_AXES, split_axis=0, concat_axis=0, tiled=True)


def places(doc_ids):
    group = lax.axis_index("x") * 2 + lax.axis_index("zh")
    own = lax.dynamic_slice_in_dim(doc_ids, group * GROUP, GROUP)
    ahead = lax.dynamic_slice_in_dim(doc_ids, jnp.maximum(group * GROUP - AHEAD, 0), AHEAD)
    ahead = jnp.where(group > 0, ahead, -1)
    docs = jnp.concatenate([ahead, own])
    leads = own.reshape(TILES, TILE)[:, :1]
    tile_start = jnp.sum((docs[None] < leads).astype(jnp.int32), 1) // TILE
    row = jnp.arange(EXTRA, dtype=jnp.int32)[:, None]
    bits = (docs[None] >> (row // 2)) & 1
    coded = row < 2 * DOC_BITS
    differs = (bits != row % 2) | (docs[None] < 0)
    key_code = jnp.where(coded, jnp.where(differs, -FAR, 0.0), jnp.where(row < 15, -1.0, 0.0))
    query_code = jnp.where(coded & (bits[:, AHEAD:] == row % 2), 1.0, 0.0)
    query_code = query_code.reshape(EXTRA, TILES, TILE).transpose(1, 0, 2)
    return tile_start, (key_code.astype(BF16), query_code.astype(BF16))


def shards(queries, keys, values, cotangent, doc_ids):
    place = jnp.stack([lax.axis_index(axis) for axis in ("zh", "y", "zl", "c")]).astype(jnp.int32)
    mirror = place[:1]
    kv = to_heads(pack(mirror, keys, values))
    tile_start, codes = places(doc_ids)
    queries, cotangent, tile_start, codes = lax.optimization_barrier(
        (queries, cotangent, tile_start, codes)
    )
    pairs = group_pairs()
    last = kv[CHUNKS - HALO :]
    halo = lax.ppermute(last, AXES, pairs)
    q = by_distance(after(to_parts(place, queries), [last]), "zl")
    g = by_distance(after(to_parts(place, cotangent), q[2:3]), "zl")
    *out, stat = late_forward(place, tile_start, codes, kv, q)
    *out, early_stat = early_forward(place, tile_start, codes, kv, halo, q, out)
    back, carry, early_q = early_backward(
        place, tile_start, codes, kv, halo, early_stat, q, g, out
    )
    grads, rest, *grad_q = late_backward(
        place, tile_start, codes, kv, stat, q, g, out, carry, early_q
    )
    out = by_distance(out, "zl")
    grad_q = by_distance(after(grad_q, out[1:]), "zl")
    out = by_distance(turn(place, out), "y")
    back = lax.ppermute(back, AXES, [(b, a) for a, b in pairs])
    (grads,) = after([join(back, rest, grads)], grad_q[1:] + out[1:])
    attended = to_rows(place, out)
    grad_q = to_rows(place, by_distance(turn(place, grad_q), "y"))
    grad_k, grad_v = unpack(mirror, to_heads(grads))
    return attended, grad_q, grad_k, grad_v


def solution(mesh):
    wide = Mesh(mesh.devices.reshape(4, 2, 4, 4, 2), AXES)
    rows = P(AXES, None)
    return jax.shard_map(
        shards,
        mesh=wide,
        in_specs=(rows, rows, rows, rows, P()),
        out_specs=(rows, rows, rows, rows),
        check_vma=False,
    )
```

```python
import functools
import math

import jax
import jax.numpy as jnp
from jax import lax
from jax.experimental import pallas as pl
from jax.experimental.pallas import tpu as pltpu
from jax.sharding import Mesh
from jax.sharding import PartitionSpec as P

HEAD_DIM = 96
HEADS = 32
CHUNK = 128
CHUNKS = 32
HALO = 8
DOC_BITS = 6
EXTRA = 16
WIDE = HEAD_DIM + EXTRA
FAR = 2.0**20
GROUP = CHUNK * CHUNKS
AHEAD = CHUNK * HALO
WINDOW = GROUP + AHEAD
TILE = 256
TILES = GROUP // TILE
BLOCKS = CHUNKS // HALO
AHEAD_TILES = AHEAD // TILE
REACH = AHEAD_TILES + 1
NEG = -1e30
SCALE = 1.0 / math.sqrt(HEAD_DIM)
LOG2E = 1.4426950408889634
MIB = 1024 * 1024

AXES = ("x", "zh", "y", "zl", "c")
GROUP_AXES = ("y", "zl", "c")
F32 = jnp.float32
BF16 = jnp.bfloat16


def vmem():
    return pl.BlockSpec(memory_space=pltpu.VMEM)


def smem():
    return pl.BlockSpec(memory_space=pltpu.SMEM)


def hbm():
    return pl.BlockSpec(memory_space=pltpu.HBM)


def in_hbm(*arrays):
    return [pltpu.with_memory_space_constraint(array, pltpu.HBM) for array in arrays]


def pack_kernel(mirror_ref, *refs):
    count = len(refs) - 5
    sources, (out_ref, rows, blocks, arrived, sent) = refs[:count], refs[count:]
    mirrored = mirror_ref[0]

    def fetch(y, n):
        return pltpu.make_async_copy(
            sources[n].at[:, pl.ds(y * 768, 768)], rows.at[n, y], arrived.at[n, y]
        )

    def send(y):
        part = pl.ds(y * 8, 8)
        return pltpu.make_async_copy(blocks.at[part], out_ref.at[part], sent.at[y])

    for y in range(4):
        for n in range(count):
            fetch(y, n).start()
    for y in range(4):
        for n in range(count):
            fetch(y, n).wait()
            turned = rows[n, y].T
            for zl in range(4):
                slot = 8 * y + 2 * jnp.where(mirrored == 1, 3 - zl, zl)
                piece = turned[zl * 192 : (zl + 1) * 192]
                blocks[pl.ds(slot, 2), n] = piece.reshape(2, HEAD_DIM, CHUNK)
        send(y).start()
    for y in range(4):
        send(y).wait()


def pack(mirror, *arrays):
    count = len(arrays)
    shape = (HEADS, count, HEAD_DIM, CHUNK)
    return pl.pallas_call(
        pack_kernel,
        in_specs=[smem()] + [hbm()] * count,
        out_specs=hbm(),
        out_shape=pltpu.HBM(shape, BF16),
        scratch_shapes=[
            pltpu.VMEM((count, 4, CHUNK, 768), BF16),
            pltpu.VMEM(shape, BF16),
            pltpu.SemaphoreType.DMA((count, 4)),
            pltpu.SemaphoreType.DMA((4,)),
        ],
        compiler_params=pltpu.CompilerParams(vmem_limit_bytes=40 * MIB),
        name="pack",
    )(mirror, *in_hbm(*arrays))


def unpack_kernel(mirror_ref, in_ref, *out_refs):
    mirrored = mirror_ref[0]
    for n, out_ref in enumerate(out_refs):
        pieces = []
        for zl in range(4):
            slot = 2 * jnp.where(mirrored == 1, 3 - zl, zl)
            pieces.append(in_ref[pl.ds(slot, 2), n].reshape(192, CHUNK))
        out_ref[...] = jnp.concatenate(pieces, 0).T


def unpack(mirror, array):
    count = array.shape[1]
    return pl.pallas_call(
        unpack_kernel,
        grid=(4,),
        in_specs=[
            smem(),
            pl.BlockSpec((8, count, HEAD_DIM, CHUNK), lambda y: (y, 0, 0, 0)),
        ],
        out_specs=[pl.BlockSpec((CHUNK, 768), lambda y: (0, y))] * count,
        out_shape=[jax.ShapeDtypeStruct((CHUNK, HEADS * HEAD_DIM), BF16)] * count,
        compiler_params=pltpu.CompilerParams(vmem_limit_bytes=28 * MIB),
        name="unpack",
    )(mirror, array)


def tile_of(ref, i):
    return jnp.concatenate([ref[2 * i], ref[2 * i + 1]], 1)


def nn(a, b):
    return lax.dot_general(a, b, (((1,), (0,)), ((), ())), preferred_element_type=F32)


def nt(a, b):
    return lax.dot_general(a, b, (((1,), (1,)), ((), ())), preferred_element_type=F32)


def each_chunk(halo_ref, own_ref, n, chunks):
    for chunk in chunks:
        piece = halo_ref[chunk, n] if chunk < HALO else own_ref[chunk - HALO, n]
        yield slice(chunk * CHUNK, (chunk + 1) * CHUNK), piece


def fill_keys(halo_ref, own_ref, code_ref, chunks, flat, turned):
    for span, piece in each_chunk(halo_ref, own_ref, 0, chunks):
        flat[span, :] = jnp.concatenate([piece, code_ref[:, span]], 0).T
        if turned is not None:
            turned[:, span] = piece


def fill_value_rows(halo_ref, own_ref, chunks, flat):
    row = lax.broadcasted_iota(jnp.int32, (EXTRA, CHUNK), 0)
    minus = jnp.where(row < 3, -1.0, 0.0).astype(BF16)
    for span, piece in each_chunk(halo_ref, own_ref, 1, chunks):
        flat[span, :] = jnp.concatenate([piece, minus], 0).T


def fill_value_columns(halo_ref, own_ref, chunks, turned):
    for span, piece in each_chunk(halo_ref, own_ref, 1, chunks):
        turned[:HEAD_DIM, span] = piece
        turned[HEAD_DIM:, span] = jnp.ones((EXTRA, CHUNK), BF16)


def with_row(extra, first, value):
    high = value.astype(BF16).astype(F32)
    middle = (value - high).astype(BF16).astype(F32)
    low = value - high - middle
    row = lax.broadcasted_iota(jnp.int32, (EXTRA, TILE), 0)
    for n, part in enumerate((high, middle, low)):
        extra = jnp.where(row == first + n, part, extra)
    return extra.astype(BF16)


def causal():
    row = lax.broadcasted_iota(jnp.int32, (TILE, TILE), 0)
    return row <= lax.broadcasted_iota(jnp.int32, (TILE, TILE), 1)


def per_tile(tile_start_ref, i, body):
    reach = jnp.clip(i + REACH - tile_start_ref[i], 1, REACH)
    for count in range(1, REACH + 1):
        pl.when(reach == count)(functools.partial(body, count))


def send_block(buffer, out_ref, sent, block):
    part = pl.ds(block * HALO, HALO)
    return pltpu.make_async_copy(buffer.at[part], out_ref.at[part], sent.at[block])


def forward_tiles(
    block, tile_start_ref, query_code_ref, q_ref, store, stat_ref, key_flat, value_turned
):
    def tile(step, _):
        i = block * AHEAD_TILES + step

        def body(count):
            q = jnp.concatenate([tile_of(q_ref, i), query_code_ref[i]], 0)
            scores = []
            top = None
            for j in range(count):
                first = pl.multiple_of((i + REACH - count + j) * TILE, TILE)
                s = nn(key_flat[pl.ds(first, TILE), :], q)
                if j == count - 1:
                    s = jnp.where(causal(), s, NEG)
                scores.append(s)
                t = jnp.max(s, axis=0, keepdims=True)
                top = t if top is None else jnp.maximum(top, t)
            shift = top * (SCALE * LOG2E)
            out = None
            for j in range(count):
                first = pl.multiple_of((i + REACH - count + j) * TILE, TILE)
                e = jnp.exp2(scores[j] * (SCALE * LOG2E) - shift)
                o = nn(value_turned[:, pl.ds(first, TILE)], e.astype(BF16))
                out = o if out is None else out + o
            total = out[HEAD_DIM : HEAD_DIM + 1]
            out = (out[:HEAD_DIM] / total).astype(BF16)
            store(2 * i, out[:, :CHUNK])
            store(2 * i + 1, out[:, CHUNK:])
            stat_ref[i] = top + jnp.log(total) * (1.0 / SCALE)

        per_tile(tile_start_ref, i, body)
        return 0

    lax.fori_loop(0, AHEAD_TILES, tile, 0)


def part_copies(place_ref, buffer, parts, b, sems, fetch=False):
    copies = []
    for d, ref in enumerate(parts):
        here = buffer.at[pl.ds(b * HALO + 2 * (place_ref[2] ^ d), 2)]
        there = ref.at[b]
        ends = (there, here) if fetch else (here, there)
        copies.append(pltpu.make_async_copy(*ends, sems.at[b, d]))
    return copies


def late_forward_kernel(
    place_ref, tile_start_ref, key_code_ref, query_code_ref, kv_ref, q_0, q_1, q_2, q_3,
    part_0, part_1, part_2, part_3, stat_ref, key_flat, value_turned, buffer, queries,
    sent, fetched_q
):
    parts = (part_0, part_1, part_2, part_3)

    def fetch(b):
        return part_copies(place_ref, queries, (q_0, q_1, q_2, q_3), b, fetched_q, True)

    for b in range(1, BLOCKS):
        for copy in fetch(b):
            copy.start()
    chunks = range(HALO, HALO + CHUNKS)
    fill_keys(None, kv_ref, key_code_ref, chunks, key_flat, None)
    fill_value_columns(None, kv_ref, chunks, value_turned)

    def store(chunk, value):
        buffer[chunk] = value

    def block(b, _):
        for copy in fetch(b):
            copy.wait()
        forward_tiles(
            b, tile_start_ref, query_code_ref, queries, store, stat_ref, key_flat, value_turned
        )
        for copy in part_copies(place_ref, buffer, parts, b, sent):
            copy.start()
        return 0

    lax.fori_loop(1, BLOCKS, block, 0)
    for b in range(1, BLOCKS):
        for copy in part_copies(place_ref, buffer, parts, b, sent):
            copy.wait()


def cost(time):
    return pl.CostEstimate(flops=int(time * 1.1e9), bytes_accessed=0, transcendentals=0)


PARTS = [pltpu.HBM((4, 2, HEAD_DIM, CHUNK), BF16)] * 4


def part(count, width):
    return pl.BlockSpec((count, width, HEAD_DIM, CHUNK), lambda b: (0, 0, 0, 0))


def forward_scratch(window, chunks):
    return [
        pltpu.VMEM((window, WIDE), BF16),
        pltpu.VMEM((WIDE, window), BF16),
        pltpu.VMEM((chunks, HEAD_DIM, CHUNK), BF16),
        pltpu.VMEM((chunks, HEAD_DIM, CHUNK), BF16),
        pltpu.SemaphoreType.DMA((BLOCKS, 4)),
        pltpu.SemaphoreType.DMA((BLOCKS, 4)),
    ]


def late_forward(place, tile_start, codes, kv, q):
    return pl.pallas_call(
        late_forward_kernel,
        in_specs=[smem(), smem(), vmem(), vmem(), vmem()] + [hbm()] * 4,
        out_specs=[hbm()] * 4 + [vmem()],
        out_shape=PARTS + [jax.ShapeDtypeStruct((TILES, 1, TILE), F32)],
        scratch_shapes=forward_scratch(WINDOW, CHUNKS),
        compiler_params=pltpu.CompilerParams(vmem_limit_bytes=40 * MIB),
        cost_estimate=cost(30),
        name="late_forward",
    )(place, tile_start, *codes, kv, *in_hbm(*q))


def backward_tiles(
    low, high, tile_start_ref, query_code_ref, q_ref, g_ref, out_ref, stat_ref, store,
    key_flat, key_turned, value_flat, key_sum, value_sum
):
    def tile(i, _):
        def body(count):
            q = tile_of(q_ref, i)
            g = tile_of(g_ref, i)
            o = tile_of(out_ref, i)
            delta = jnp.sum(o.astype(F32) * g.astype(F32), axis=0, keepdims=True)
            stat = stat_ref[i]
            code = query_code_ref[i].astype(F32)
            q_wide = jnp.concatenate([q, with_row(code, 2 * DOC_BITS, stat)], 0)
            g_wide = jnp.concatenate([g, with_row(jnp.zeros_like(code), 0, delta)], 0)
            first = pl.multiple_of((i + REACH - count) * TILE, TILE)
            span = pl.ds(first, count * TILE)
            p = jnp.exp2(nn(key_flat[span, :], q_wide) * (SCALE * LOG2E))
            last = (count - 1) * TILE
            tail = jnp.where(causal(), p[last:], 0.0)
            p = jnp.concatenate([p[:last], tail], 0) if last else tail
            d = (p * nn(value_flat[span, :], g_wide)).astype(BF16)
            grad_q = nn(key_turned[:, span], d)
            key_sum[:, span] += nt(q, d)
            value_sum[:, span] += nt(g, p.astype(BF16))
            grad_q = (grad_q * SCALE).astype(BF16)
            store(2 * i, grad_q[:, :CHUNK])
            store(2 * i + 1, grad_q[:, CHUNK:])

        per_tile(tile_start_ref, i, body)
        return 0

    lax.fori_loop(low, high, tile, 0)


def early_forward_kernel(
    place_ref, tile_start_ref, key_code_ref, query_code_ref, kv_ref, halo_ref,
    q_0, q_1, q_2, q_3, _, __, ___, ____,
    part_0, part_1, part_2, part_3, stat_ref, key_flat, value_turned, buffer, queries,
    sent, fetched_q
):
    fetches = part_copies(place_ref, queries, (q_0, q_1, q_2, q_3), 0, fetched_q, True)
    for copy in fetches:
        copy.start()
    fill_keys(halo_ref, kv_ref, key_code_ref, range(2 * HALO), key_flat, None)
    fill_value_columns(halo_ref, kv_ref, range(2 * HALO), value_turned)
    for copy in fetches:
        copy.wait()

    def store(chunk, value):
        buffer[chunk] = value

    forward_tiles(
        0, tile_start_ref, query_code_ref, queries, store, stat_ref, key_flat, value_turned
    )
    copies = part_copies(place_ref, buffer, (part_0, part_1, part_2, part_3), 0, sent)
    for copy in copies:
        copy.start()
    for copy in copies:
        copy.wait()


def early_backward_kernel(
    place_ref, tile_start_ref, key_code_ref, query_code_ref, kv_ref, halo_ref, stat_ref,
    q_0, q_1, q_2, q_3, g_0, g_1, g_2, g_3, out_0, out_1, out_2, out_3,
    back_ref, carry_ref, grad_q_ref,
    key_flat, key_turned, value_flat, key_sum, value_sum, q_part, g_part, out_part, back_part,
    grad_q_part, sent, fetched_q, fetched_g, fetched_out
):
    fetches = part_copies(place_ref, q_part, (q_0, q_1, q_2, q_3), 0, fetched_q, True)
    fetches += part_copies(place_ref, g_part, (g_0, g_1, g_2, g_3), 0, fetched_g, True)
    fetches += part_copies(place_ref, out_part, (out_0, out_1, out_2, out_3), 0, fetched_out, True)
    for copy in fetches:
        copy.start()
    fill_keys(halo_ref, kv_ref, key_code_ref, range(2 * HALO), key_flat, key_turned)
    fill_value_rows(halo_ref, kv_ref, range(2 * HALO), value_flat)
    key_sum[...] = jnp.zeros_like(key_sum)
    value_sum[...] = jnp.zeros_like(value_sum)
    for copy in fetches:
        copy.wait()

    def store(chunk, value):
        grad_q_part[chunk] = value

    backward_tiles(
        0, AHEAD_TILES, tile_start_ref, query_code_ref, q_part, g_part, out_part, stat_ref, store,
        key_flat, key_turned, value_flat, key_sum, value_sum
    )
    copies = [pltpu.make_async_copy(grad_q_part, grad_q_ref, sent.at[2])]
    for n, sums in enumerate((key_sum, value_sum)):
        copies.append(
            pltpu.make_async_copy(
                sums.at[:, pl.ds(AHEAD, AHEAD)], carry_ref.at[n], sent.at[3 + n]
            )
        )
    for copy in copies:
        copy.start()
    for n, (sums, factor) in enumerate(((key_sum, SCALE), (value_sum, 1.0))):
        for chunk in range(HALO):
            piece = sums[:, chunk * CHUNK : (chunk + 1) * CHUNK] * factor
            back_part[chunk, n] = piece.astype(BF16)
    back_copy = pltpu.make_async_copy(back_part, back_ref, sent.at[5])
    back_copy.start()
    for copy in (*copies, back_copy):
        copy.wait()


def late_backward_kernel(
    place_ref, tile_start_ref, key_code_ref, query_code_ref, kv_ref, stat_ref,
    q_0, q_1, q_2, q_3, g_0, g_1, g_2, g_3, out_0, out_1, out_2, out_3, carry_ref, grad_q_ref, grads_ref, rest_ref, part_0, part_1, part_2, part_3,
    key_flat, key_turned, value_flat, key_sum, value_sum, buffer, queries, q_all, g_all,
    out_all, carry, sent, fetched, parted, fetched_q, fetched_g, fetched_out
):
    def fetch(b):
        return part_copies(
            place_ref, q_all, (q_0, q_1, q_2, q_3), b, fetched_q, True
        ) + part_copies(place_ref, g_all, (g_0, g_1, g_2, g_3), b, fetched_g, True) + part_copies(place_ref, out_all, (out_0, out_1, out_2, out_3), b, fetched_out, True)

    first = (
        pltpu.make_async_copy(carry_ref, carry, fetched.at[0]),
        pltpu.make_async_copy(grad_q_ref, queries.at[pl.ds(0, HALO)], fetched.at[1]),
    )
    for copy in (*fetch(1), *first, *fetch(2), *fetch(3)):
        copy.start()
    chunks = range(HALO, HALO + CHUNKS)
    fill_keys(None, kv_ref, key_code_ref, chunks, key_flat, key_turned)
    fill_value_rows(None, kv_ref, chunks, value_flat)
    for sums in (key_sum, value_sum):
        sums[:, AHEAD:] = jnp.zeros((HEAD_DIM, GROUP), F32)

    def store(chunk, value):
        queries[chunk] = value

    def send_queries(b):
        return part_copies(place_ref, queries, (part_0, part_1, part_2, part_3), b, parted)

    def block(b, _):
        for copy in fetch(b):
            copy.wait()
        backward_tiles(
            b * AHEAD_TILES, (b + 1) * AHEAD_TILES,
            tile_start_ref, query_code_ref, q_all, g_all, out_all, stat_ref, store,
            key_flat, key_turned, value_flat, key_sum, value_sum
        )

        @pl.when(b == 1)
        def _():
            for copy in first:
                copy.wait()
            for copy in send_queries(0):
                copy.start()
            key_sum[:, AHEAD : 2 * AHEAD] += carry[0]
            value_sum[:, AHEAD : 2 * AHEAD] += carry[1]

        for n, (sums, factor) in enumerate(((key_sum, SCALE), (value_sum, 1.0))):
            for chunk in range(HALO):
                place = pl.multiple_of(b * AHEAD + chunk * CHUNK, CHUNK)
                piece = sums[:, pl.ds(place, CHUNK)] * factor
                buffer[(b - 1) * HALO + chunk, n] = piece.astype(BF16)
        send_block(buffer, grads_ref, sent, b - 1).start()
        for copy in send_queries(b):
            copy.start()
        return 0

    lax.fori_loop(1, BLOCKS, block, 0)
    for n, sums in enumerate((key_sum, value_sum)):
        rest_ref[n] = sums[:, GROUP:]
    for b in range(BLOCKS - 1):
        send_block(buffer, grads_ref, sent, b).wait()
    for b in range(BLOCKS):
        for copy in send_queries(b):
            copy.wait()


def sums_scratch(window):
    return [
        pltpu.VMEM((window, WIDE), BF16),
        pltpu.VMEM((HEAD_DIM, window), BF16),
        pltpu.VMEM((window, WIDE), BF16),
        pltpu.VMEM((HEAD_DIM, window), F32),
        pltpu.VMEM((HEAD_DIM, window), F32),
    ]


def early_forward(place, tile_start, codes, kv, halo, q, parts):
    return pl.pallas_call(
        early_forward_kernel,
        grid=(1,),
        in_specs=[smem(), smem(), vmem(), vmem(), part(HALO, 2), vmem()] + [hbm()] * 8,
        out_specs=[hbm()] * 4 + [vmem()],
        out_shape=PARTS + [jax.ShapeDtypeStruct((AHEAD_TILES, 1, TILE), F32)],
        input_output_aliases={10 + d: d for d in range(4)},
        scratch_shapes=forward_scratch(2 * AHEAD, HALO),
        compiler_params=pltpu.CompilerParams(vmem_limit_bytes=40 * MIB),
        cost_estimate=cost(1),
        name="early_forward",
    )(place, tile_start, *codes, kv, halo, *in_hbm(*q, *parts))


def early_backward(place, tile_start, codes, kv, halo, stat, q, g, out):
    return pl.pallas_call(
        early_backward_kernel,
        grid=(1,),
        in_specs=[smem(), smem(), vmem(), vmem(), part(HALO, 2), vmem(), vmem()] + [hbm()] * 12,
        out_specs=[hbm()] * 3,
        out_shape=[
            pltpu.HBM((HALO, 2, HEAD_DIM, CHUNK), BF16),
            pltpu.HBM((2, HEAD_DIM, AHEAD), F32),
            pltpu.HBM((HALO, HEAD_DIM, CHUNK), BF16),
        ],
        scratch_shapes=sums_scratch(2 * AHEAD)
        + [
            pltpu.VMEM((HALO, HEAD_DIM, CHUNK), BF16),
            pltpu.VMEM((HALO, HEAD_DIM, CHUNK), BF16),
            pltpu.VMEM((HALO, HEAD_DIM, CHUNK), BF16),
            pltpu.VMEM((HALO, 2, HEAD_DIM, CHUNK), BF16),
            pltpu.VMEM((HALO, HEAD_DIM, CHUNK), BF16),
            pltpu.SemaphoreType.DMA((6,)),
            pltpu.SemaphoreType.DMA((1, 4)),
            pltpu.SemaphoreType.DMA((1, 4)),
            pltpu.SemaphoreType.DMA((1, 4)),
        ],
        compiler_params=pltpu.CompilerParams(vmem_limit_bytes=40 * MIB),
        cost_estimate=cost(1),
        name="early_backward",
    )(place, tile_start, *codes, kv, halo, stat, *in_hbm(*q, *g, *out))


def late_backward(place, tile_start, codes, kv, stat, q, g, out, carry, grad_q):
    return pl.pallas_call(
        late_backward_kernel,
        in_specs=[smem(), smem(), vmem(), vmem(), vmem(), vmem()] + [hbm()] * 14,
        out_specs=[hbm(), vmem()] + [hbm()] * 4,
        out_shape=[
            pltpu.HBM((CHUNKS, 2, HEAD_DIM, CHUNK), BF16),
            jax.ShapeDtypeStruct((2, HEAD_DIM, AHEAD), F32),
        ]
        + [pltpu.HBM((4, 2, HEAD_DIM, CHUNK), BF16)] * 4,
        scratch_shapes=sums_scratch(WINDOW)
        + [
            pltpu.VMEM((CHUNKS, 2, HEAD_DIM, CHUNK), BF16),
            pltpu.VMEM((CHUNKS, HEAD_DIM, CHUNK), BF16),
            pltpu.VMEM((CHUNKS, HEAD_DIM, CHUNK), BF16),
            pltpu.VMEM((CHUNKS, HEAD_DIM, CHUNK), BF16),
            pltpu.VMEM((CHUNKS, HEAD_DIM, CHUNK), BF16),
            pltpu.VMEM((2, HEAD_DIM, AHEAD), F32),
            pltpu.SemaphoreType.DMA((BLOCKS,)),
            pltpu.SemaphoreType.DMA((2,)),
            pltpu.SemaphoreType.DMA((BLOCKS, 4)),
            pltpu.SemaphoreType.DMA((BLOCKS, 4)),
            pltpu.SemaphoreType.DMA((BLOCKS, 4)),
            pltpu.SemaphoreType.DMA((BLOCKS, 4)),
        ],
        compiler_params=pltpu.CompilerParams(vmem_limit_bytes=40 * MIB),
        cost_estimate=cost(10),
        name="late_backward",
    )(place, tile_start, *codes, kv, stat, *in_hbm(*q, *g, *out, carry, grad_q))


def join_kernel(back_ref, rest_ref, _, out_ref, buffer, moved):
    sends = []
    for n, factor in enumerate((SCALE, 1.0)):
        for chunk in range(HALO):
            own = rest_ref[n, :, chunk * CHUNK : (chunk + 1) * CHUNK] * factor
            buffer[chunk, n] = (own + back_ref[chunk, n].astype(F32)).astype(BF16)
        target = out_ref.at[pl.ds(CHUNKS - HALO, HALO), n]
        sends.append(pltpu.make_async_copy(buffer.at[:, n], target, moved.at[n]))
        sends[n].start()
    for copy in sends:
        copy.wait()


def join(back, rest, grads):
    return pl.pallas_call(
        join_kernel,
        in_specs=[vmem(), vmem(), hbm()],
        out_specs=hbm(),
        out_shape=pltpu.HBM(grads.shape, BF16),
        input_output_aliases={2: 0},
        scratch_shapes=[
            pltpu.VMEM((HALO, 2, HEAD_DIM, CHUNK), BF16),
            pltpu.SemaphoreType.DMA((2,)),
        ],
        compiler_params=pltpu.CompilerParams(vmem_limit_bytes=40 * MIB),
        name="join",
    )(back, rest, *in_hbm(grads))


def move(copies):
    for copy in copies:
        copy.start()
    for copy in copies:
        copy.wait()


def turn_kernel(back, place_ref, *refs):
    sources, targets, (buffer, fetched, sent) = refs[:4], refs[4:8], refs[8:]
    y = place_ref[1]
    fetches = []
    for d in range(4):
        for e in range(4):
            if back:
                ends = (sources[e].at[d], buffer.at[d, y ^ e])
            else:
                ends = (sources[d].at[y ^ e], buffer.at[e, d])
            fetches.append(pltpu.make_async_copy(*ends, fetched.at[d, e]))
    move(fetches)
    move([pltpu.make_async_copy(buffer.at[e], targets[e], sent.at[e]) for e in range(4)])


def turn(place, parts, back=False):
    return pl.pallas_call(
        functools.partial(turn_kernel, back),
        in_specs=[smem()] + [pl.BlockSpec(memory_space=pl.ANY)] * 4,
        out_specs=[hbm()] * 4,
        out_shape=PARTS,
        scratch_shapes=[
            pltpu.VMEM((4, 4, 2, HEAD_DIM, CHUNK), BF16),
            pltpu.SemaphoreType.DMA((4, 4)),
            pltpu.SemaphoreType.DMA((4,)),
        ],
        compiler_params=pltpu.CompilerParams(vmem_limit_bytes=40 * MIB),
        cost_estimate=cost(1),
        name="turn",
    )(place, *parts)


def pack_cores_kernel(place_ref, source, own_ref, other_ref, rows, blocks, arrived, sent):
    mirrored, y, zl, core = place_ref[0], place_ref[1], place_ref[2], place_ref[3]
    fetches = [
        pltpu.make_async_copy(source.at[:, pl.ds(n * 768, 768)], rows.at[n], arrived.at[n])
        for n in range(4)
    ]
    for copy in fetches:
        copy.start()
    for n in range(4):
        fetches[n].wait()
        turned = rows[n].T
        for head_zl in range(4):
            d = zl ^ jnp.where(mirrored == 1, 3 - head_zl, head_zl)
            for head_core in range(2):
                first = (2 * head_zl + head_core) * HEAD_DIM
                blocks[core ^ head_core, y ^ n, d] = turned[first : first + HEAD_DIM]
    copies = [
        pltpu.make_async_copy(blocks.at[n], ref, sent.at[n])
        for n, ref in enumerate((own_ref, other_ref))
    ]
    for copy in copies:
        copy.start()
    for copy in copies:
        copy.wait()


CORE_SHAPE = (4, 4, HEAD_DIM, CHUNK)


def pack_cores(place, array):
    return pl.pallas_call(
        pack_cores_kernel,
        in_specs=[smem(), hbm()],
        out_specs=[hbm()] * 2,
        out_shape=[pltpu.HBM(CORE_SHAPE, BF16)] * 2,
        scratch_shapes=[
            pltpu.VMEM((4, CHUNK, 768), BF16),
            pltpu.VMEM((2, *CORE_SHAPE), BF16),
            pltpu.SemaphoreType.DMA((4,)),
            pltpu.SemaphoreType.DMA((2,)),
        ],
        compiler_params=pltpu.CompilerParams(vmem_limit_bytes=40 * MIB),
        cost_estimate=cost(1),
        name="pack_cores",
    )(place, *in_hbm(array))


def both_cores_kernel(place_ref, own_ref, other_ref, *refs):
    targets, (buffer, fetched, sent) = refs[:4], refs[4:]
    core = place_ref[3]
    fetches = []
    for e in range(4):
        for n, (ref, side) in enumerate(((own_ref, core), (other_ref, 1 - core))):
            fetches.append(
                pltpu.make_async_copy(ref.at[e], buffer.at[e, :, side], fetched.at[n, e])
            )
    move(fetches)
    move([pltpu.make_async_copy(buffer.at[e], targets[e], sent.at[e]) for e in range(4)])


def both_cores(place, own, other):
    return pl.pallas_call(
        both_cores_kernel,
        in_specs=[smem()] + [pl.BlockSpec(memory_space=pl.ANY)] * 2,
        out_specs=[hbm()] * 4,
        out_shape=PARTS,
        scratch_shapes=[
            pltpu.VMEM((4, 4, 2, HEAD_DIM, CHUNK), BF16),
            pltpu.SemaphoreType.DMA((2, 4)),
            pltpu.SemaphoreType.DMA((4,)),
        ],
        compiler_params=pltpu.CompilerParams(vmem_limit_bytes=40 * MIB),
        cost_estimate=cost(1),
        name="both_cores",
    )(place, own, other)


def to_parts(place, array):
    own, other = pack_cores(place, array)
    other = lax.ppermute(other, "c", [(0, 1), (1, 0)])
    return turn(place, by_distance(both_cores(place, own, other), "y"), back=True)


def other_core_kernel(place_ref, *refs):
    sources, (target, buffer, fetched, sent) = refs[:4], refs[4:]
    move(
        [
            pltpu.make_async_copy(sources[e].at[:, 1 - place_ref[3]], buffer.at[e], fetched.at[e])
            for e in range(4)
        ]
    )
    move([pltpu.make_async_copy(buffer, target, sent)])


def other_core(place, parts):
    return pl.pallas_call(
        other_core_kernel,
        in_specs=[smem()] + [pl.BlockSpec(memory_space=pl.ANY)] * 4,
        out_specs=hbm(),
        out_shape=pltpu.HBM((4, 4, HEAD_DIM, CHUNK), BF16),
        scratch_shapes=[
            pltpu.VMEM((4, 4, HEAD_DIM, CHUNK), BF16),
            pltpu.SemaphoreType.DMA((4,)),
            pltpu.SemaphoreType.DMA(()),
        ],
        compiler_params=pltpu.CompilerParams(vmem_limit_bytes=40 * MIB),
        cost_estimate=cost(1),
        name="other_core",
    )(place, *parts)


def by_distance(parts, axis):
    return [parts[0]] + [
        lax.ppermute(parts[d], axis, [(i, i ^ d) for i in range(4)]) for d in range(1, 4)
    ]


def rows_kernel(place_ref, part_0, part_1, part_2, part_3, other_ref, out_ref, rows, sent):
    mirrored, y, zl, core = place_ref[0], place_ref[1], place_ref[2], place_ref[3]
    copies = []
    for e, ref in enumerate((part_0, part_1, part_2, part_3)):
        pieces = []
        for head_zl in range(4):
            d = zl ^ jnp.where(mirrored == 1, 3 - head_zl, head_zl)
            own, other = ref[d, core], other_ref[e, d]
            pieces.append(jnp.where(core == 0, own, other))
            pieces.append(jnp.where(core == 0, other, own))
        rows[e] = jnp.concatenate(pieces, 0).T
        first = pl.multiple_of((y ^ e) * 768, 768)
        copies.append(
            pltpu.make_async_copy(rows.at[e], out_ref.at[:, pl.ds(first, 768)], sent.at[e])
        )
        copies[e].start()
    for copy in copies:
        copy.wait()


def rows_of(place, parts, other):
    return pl.pallas_call(
        rows_kernel,
        in_specs=[smem()] + [vmem()] * 5,
        out_specs=hbm(),
        out_shape=pltpu.HBM((CHUNK, HEADS * HEAD_DIM), BF16),
        scratch_shapes=[
            pltpu.VMEM((4, CHUNK, 768), BF16),
            pltpu.SemaphoreType.DMA((4,)),
        ],
        compiler_params=pltpu.CompilerParams(vmem_limit_bytes=28 * MIB),
        cost_estimate=cost(1),
        name="rows_of",
    )(place, *parts, other)


def to_rows(place, parts):
    other = lax.ppermute(other_core(place, parts), "c", [(0, 1), (1, 0)])
    return rows_of(place, parts, other)


def gate_kernel(*_):
    pass


def after(arrays, others):
    count = len(arrays)
    return pl.pallas_call(
        gate_kernel,
        in_specs=[hbm()] * count + [pl.BlockSpec(memory_space=pl.ANY)] * len(others),
        out_specs=[hbm()] * count,
        out_shape=[pltpu.HBM(array.shape, array.dtype) for array in arrays],
        input_output_aliases={n: n for n in range(count)},
        name="after",
    )(*arrays, *others)


def group_pairs():
    def index(x, zh, y, zl, c):
        return (((x * 2 + zh) * 4 + y) * 4 + zl) * 2 + c

    pairs = []
    for group in range(7):
        for y in range(4):
            for zl in range(4):
                for c in range(2):
                    pairs.append(
                        (
                            index(group // 2, group % 2, y, zl, c),
                            index((group + 1) // 2, (group + 1) % 2, y, 3 - zl, c),
                        )
                    )
    return pairs


def to_heads(array):
    return lax.all_to_all(array, GROUP_AXES, split_axis=0, concat_axis=0, tiled=True)


def places(doc_ids):
    group = lax.axis_index("x") * 2 + lax.axis_index("zh")
    own = lax.dynamic_slice_in_dim(doc_ids, group * GROUP, GROUP)
    ahead = lax.dynamic_slice_in_dim(doc_ids, jnp.maximum(group * GROUP - AHEAD, 0), AHEAD)
    ahead = jnp.where(group > 0, ahead, -1)
    docs = jnp.concatenate([ahead, own])
    leads = own.reshape(TILES, TILE)[:, :1]
    tile_start = jnp.sum((docs[None] < leads).astype(jnp.int32), 1) // TILE
    row = jnp.arange(EXTRA, dtype=jnp.int32)[:, None]
    bits = (docs[None] >> (row // 2)) & 1
    coded = row < 2 * DOC_BITS
    differs = (bits != row % 2) | (docs[None] < 0)
    key_code = jnp.where(coded, jnp.where(differs, -FAR, 0.0), jnp.where(row < 15, -1.0, 0.0))
    query_code = jnp.where(coded & (bits[:, AHEAD:] == row % 2), 1.0, 0.0)
    query_code = query_code.reshape(EXTRA, TILES, TILE).transpose(1, 0, 2)
    return tile_start, (key_code.astype(BF16), query_code.astype(BF16))


def shards(queries, keys, values, cotangent, doc_ids):
    place = jnp.stack([lax.axis_index(axis) for axis in ("zh", "y", "zl", "c")]).astype(jnp.int32)
    mirror = place[:1]
    kv = to_heads(pack(mirror, keys, values))
    tile_start, codes = places(doc_ids)
    queries, cotangent, tile_start, codes = lax.optimization_barrier(
        (queries, cotangent, tile_start, codes)
    )
    pairs = group_pairs()
    last = kv[CHUNKS - HALO :]
    halo = lax.ppermute(last, AXES, pairs)
    q = by_distance(after(to_parts(place, queries), [kv]), "zl")
    g = by_distance(after(to_parts(place, cotangent), q[2:3]), "zl")
    *out, stat = late_forward(place, tile_start, codes, kv, q)
    *out, early_stat = early_forward(place, tile_start, codes, kv, halo, q, out)
    back, carry, early_q = early_backward(
        place, tile_start, codes, kv, halo, early_stat, q, g, out
    )
    grads, rest, *grad_q = late_backward(
        place, tile_start, codes, kv, stat, q, g, out, carry, early_q
    )
    out = by_distance(out, "zl")
    grad_q = by_distance(after(grad_q, out[1:]), "zl")
    out = by_distance(turn(place, out), "y")
    back = lax.ppermute(back, AXES, [(b, a) for a, b in pairs])
    (grads,) = after([join(back, rest, grads)], grad_q[1:] + out[1:])
    attended = to_rows(place, out)
    grad_q = to_rows(place, by_distance(turn(place, grad_q), "y"))
    grad_k, grad_v = unpack(mirror, to_heads(grads))
    return attended, grad_q, grad_k, grad_v


def solution(mesh):
    wide = Mesh(mesh.devices.reshape(4, 2, 4, 4, 2), AXES)
    rows = P(AXES, None)
    return jax.shard_map(
        shards,
        mesh=wide,
        in_specs=(rows, rows, rows, rows, P()),
        out_specs=(rows, rows, rows, rows),
        check_vma=False,
    )
```
